32 devices in a mesh: grp: 2 (over x), sub: 16 (over z, y, core).
Axes of the slice: x: 2, y: 2, z: 4, core: 2. Of those that a mesh axis runs over, the one named last changes fastest.
Arguments:
- schur_t: bfloat16 [2, 16, 1024, 1024], P('grp', 'sub')
- neumann_t: bfloat16 [2, 16, 1024, 1024], P('grp', 'sub')
- face_weights: float32 [2, 16, 1024], P('grp', 'sub'), as said below
- coarse_basis: bfloat16 [2, 16, 1024, 24], P('grp', 'sub'), may hold values from -0.375 to 0.375
- coarse_inverse: float32 [2, 192, 192], P('grp', 'sub')
- coarse_number: int32 [2, 384], P('grp'), may hold values from 0 to 191, as said below
- loads: bfloat16 [2, 16, 1024, 128], P('grp', 'sub'), may hold values from -6 to 6
- iterate: bfloat16 [2, 16, 1024, 128], P('grp', 'sub'), as said below
Outputs:
- iterate_out: bfloat16 [2, 16, 1024, 128], P('grp', 'sub')
The draws below stay inside these ranges and needn't reach their ends.
Inputs may be any that keep to these rules, and one draw needn't show every extreme that they name: `face_weights`: the weights of an unknown and of its partner unknown on the face it shares sum to one. `coarse_number`: each value appears exactly twice in each group's row. `iterate`: equal on the two copies of each shared unknown.
All inputs are finite; a program needn't handle non-finite values.
Results may differ from the reference program's by a relative error of at most 0.0051.
Values sent between devices are 32-bit elements; how exact they have to be, the bound alone decides.
No kernel may reach another device: no remote copies, remote signals or barrier semaphores. Data moves between devices by JAX's collectives and lax.ppermute only.
A program may use at most 64 MiB of HBM per device.

```python
import math
import jax
import jax.numpy as jnp
from jax import lax

IFACE = 1024
RHS = 128
NCL = 24
NC = 192
ITERS = 3
N_GRP = 2
N_SUB = 16


def diagonal_helper(key):
    inner = jax.random.fold_in(key, 11)
    shape = (N_GRP, N_SUB, IFACE)
    values = jnp.exp(jax.random.uniform(inner, shape, jnp.float32, 0.0, math.log(4.0)))
    return values


def spread_helper(key, shape):
    return jax.random.normal(key, shape, jnp.float32)


def draw_schur_t(key, part):
    diagonal = diagonal_helper(key)
    shape = (N_GRP, N_SUB, IFACE, IFACE)
    off = spread_helper(jax.random.fold_in(key, 12), shape) * (0.7 / math.sqrt(IFACE))
    identity = jnp.eye(IFACE, dtype=jnp.float32)
    return (off + diagonal[..., None] * identity).astype(jnp.bfloat16)


def draw_neumann_t(key, part):
    diagonal = diagonal_helper(key)
    shape = (N_GRP, N_SUB, IFACE, IFACE)
    off = spread_helper(jax.random.fold_in(key, 13), shape) * (0.3 / math.sqrt(IFACE))
    identity = jnp.eye(IFACE, dtype=jnp.float32)
    return (off + (1.0 / diagonal)[..., None] * identity).astype(jnp.bfloat16)


def draw_face_weights(key, part):
    diagonal = diagonal_helper(key).reshape(N_GRP, N_SUB, 4, IFACE // 4)
    first = jnp.roll(diagonal[:, :, 1], 1, axis=1)
    second = jnp.roll(diagonal[:, :, 0], -1, axis=1)
    third = jnp.roll(diagonal[:, :, 3], 1, axis=0)
    fourth = jnp.roll(diagonal[:, :, 2], -1, axis=0)
    mates = jnp.stack([first, second, third, fourth], axis=2)
    return (diagonal / (diagonal + mates)).reshape(N_GRP, N_SUB, IFACE).astype(jnp.float32)


def draw_coarse_inverse(key, part):
    shape = (N_GRP, NC)
    inner = jax.random.fold_in(key, 21)
    diagonal = jnp.exp(jax.random.uniform(inner, shape, jnp.float32, math.log(0.5), math.log(2.0)))
    off = spread_helper(jax.random.fold_in(key, 22), (N_GRP, NC, NC)) * (0.4 / math.sqrt(NC))
    identity = jnp.eye(NC, dtype=jnp.float32)
    return (off + diagonal[..., None] * identity).astype(jnp.float32)


def draw_coarse_number(key, part):
    keys = jax.random.split(jax.random.fold_in(key, 31), N_GRP)
    orders = jax.vmap(lambda k: jax.random.permutation(k, N_SUB * NCL))(keys)
    return (orders % NC).astype(jnp.int32)


def draw_iterate(key, part):
    shape = (N_GRP, N_SUB, 4, IFACE // 4, RHS)
    values = spread_helper(jax.random.fold_in(key, 41), shape)
    second = jnp.roll(values[:, :, 0], -1, axis=1)
    fourth = jnp.roll(values[:, :, 2], -1, axis=0)
    joined = jnp.stack([values[:, :, 0], second, values[:, :, 2], fourth], axis=2)
    return joined.reshape(N_GRP, N_SUB, IFACE, RHS).astype(jnp.bfloat16)


def level_of(own_key, dims, shards, smallest, high):
    level, own = 1.0, jax.random.fold_in(own_key, 6)
    for axis_at, shards_of in shards:
        heights = jnp.exp(jax.random.uniform(jax.random.fold_in(own, axis_at), (shards_of,), jnp.float32, smallest / len(shards), high / len(shards)))
        level = level * jnp.repeat(heights, dims[axis_at] // shards_of).reshape([-1 if axis == axis_at else 1 for axis in range(len(dims))])
    return level


def scatter_about(own_key, extent, width, most, pieces=(), kind=jnp.bfloat16):
    values = width * jax.random.normal(own_key, extent, jnp.float32)
    if pieces:
        values = values * level_of(own_key, extent, pieces, -0.22, 0.18)
    return jnp.clip(values, -most, most).astype(kind)


def setup_inputs(seed: int = 0) -> dict:
    streams_of = jax.random.split(jax.random.key(seed), 9)
    return {
        "schur_t": draw_schur_t(jax.random.fold_in(streams_of[8], 71), 0),
        "neumann_t": draw_neumann_t(jax.random.fold_in(streams_of[8], 71), 0),
        "face_weights": draw_face_weights(jax.random.fold_in(streams_of[8], 71), 0),
        "coarse_basis": scatter_about(streams_of[3], (N_GRP, N_SUB, IFACE, NCL), (IFACE // 4) ** -0.5, 0.375, ((0, 2), (1, 16))),
        "coarse_inverse": draw_coarse_inverse(jax.random.fold_in(streams_of[8], 71), 0),
        "coarse_number": draw_coarse_number(jax.random.fold_in(streams_of[8], 71), 0),
        "loads": scatter_about(streams_of[6], (N_GRP, N_SUB, IFACE, RHS), 1.0, 6.0, ((0, 2), (1, 16))),
        "iterate": draw_iterate(jax.random.fold_in(streams_of[8], 71), 0),
    }


def partner(values):
    columns = values.shape[-1]
    faces = values.reshape(N_GRP, N_SUB, 4, IFACE // 4, columns)
    first = jnp.roll(faces[:, :, 1], 1, axis=1)
    second = jnp.roll(faces[:, :, 0], -1, axis=1)
    third = jnp.roll(faces[:, :, 3], 1, axis=0)
    fourth = jnp.roll(faces[:, :, 2], -1, axis=0)
    return jnp.stack([first, second, third, fourth], axis=2).reshape(N_GRP, N_SUB, IFACE, columns)


def products(mats, vectors):
    return lax.map(lambda pair: jnp.dot(pair[0], pair[1], preferred_element_type=jnp.float32), (mats, vectors))


def reference(schur_t, neumann_t, face_weights, coarse_basis, coarse_inverse, coarse_number, loads, iterate):
    whole = (N_GRP, N_SUB, IFACE, RHS)
    flat = (N_GRP * N_SUB, IFACE, RHS)
    schur_flat = schur_t.reshape(N_GRP * N_SUB, IFACE, IFACE)
    neumann_flat = neumann_t.reshape(N_GRP * N_SUB, IFACE, IFACE)
    weights = face_weights[..., None]
    basis_wide = coarse_basis.astype(jnp.float32)
    load_wide = loads.astype(jnp.float32)
    highest = lax.Precision.HIGHEST
    current = iterate
    for step in range(ITERS):
        image = products(schur_flat, current.reshape(flat)).reshape(whole)
        part = load_wide - image
        resid = part + partner(part)
        weighted = (weights * resid).astype(jnp.bfloat16)
        local_coarse = jnp.einsum("gsin,gsik->gsnk", basis_wide, weighted.astype(jnp.float32), precision=highest)
        coarse_rhs = jax.vmap(lambda c, n: jax.ops.segment_sum(c, n, num_segments=NC))(
            local_coarse.reshape(N_GRP, N_SUB * NCL, RHS), coarse_number)
        solved = jnp.einsum("gnm,gmk->gnk", coarse_inverse, coarse_rhs, precision=highest)
        own_values = jax.vmap(lambda x, n: jnp.take(x, n, axis=0))(solved, coarse_number).reshape(N_GRP, N_SUB, NCL, RHS)
        fine = products(neumann_flat, weighted.reshape(flat)).reshape(whole)
        correction = fine + jnp.einsum("gsin,gsnk->gsik", basis_wide, own_values, precision=highest)
        scaled = weights * correction
        update = scaled + partner(scaled)
        current = (current.astype(jnp.float32) + update).astype(jnp.bfloat16)
    return current
```

```python
import functools

import jax
import jax.numpy as jnp
from jax import lax
from jax.experimental import pallas as pl
from jax.experimental.pallas import tpu as pltpu
from jax.sharding import PartitionSpec as P

ITERS = 3
HIGHEST = lax.Precision.HIGHEST
BOTH, EVEN, ODD = 2, 0, 1
WHOLE = pl.BlockSpec(memory_space=pltpu.VMEM)


def channels(grp, sub, face):
    found = []
    for axis, devices, base in (("grp", grp, 2 * face), ("sub", sub, 0)):
        if devices == 2:
            found.append((axis, BOTH, base, 2 * face))
        else:
            found.append((axis, ODD, base, face))
            found.append((axis, EVEN, base, face))
    return tuple(found)


def mate(kind, index, devices):
    if kind == BOTH:
        return 1 - index
    step = 1 - 2 * (index % 2)
    if kind == ODD:
        step = -step
    return (index + step + devices) % devices


def swap(array, axis, kind):
    devices = lax.axis_size(axis)
    return lax.ppermute(array, axis, [(i, mate(kind, i, devices)) for i in range(devices)])


def first_row(channel):
    axis, kind, base, rows = channel
    if kind == BOTH:
        return base
    odd = lax.rem(lax.axis_index(axis), 2)
    return pl.multiple_of(base + (odd if kind == ODD else 1 - odd) * rows, rows)


def across(kind, got, rows):
    if kind == BOTH:
        half = rows // 2
        return jnp.concatenate([got[half:rows], got[0:half]], axis=0)
    return got[0:rows]


def product(a, b):
    return jnp.dot(a, b, preferred_element_type=jnp.float32)


def call(body, outs, args, scratch=(), flops=0):
    moved = sum(a.size * a.dtype.itemsize for a in args)
    return pl.pallas_call(
        body,
        out_shape=outs,
        in_specs=[WHOLE] * len(args),
        out_specs=jax.tree.map(lambda _: WHOLE, outs),
        scratch_shapes=scratch,
        cost_estimate=pl.CostEstimate(flops=flops, bytes_accessed=moved, transcendentals=0),
        compiler_params=pltpu.CompilerParams(vmem_limit_bytes=32 * 2**20),
    )(*args)


def opening(chans, matrix, load, state, basis, basis_across, *sends):
    turned = basis[...].astype(jnp.float32).T
    basis_across[...] = turned
    ncl = turned.shape[0]
    for channel, send in zip(chans, sends):
        rows = channel[3]
        first = first_row(channel)
        own = pl.ds(first, rows)
        send[0:rows] = load[own].astype(jnp.float32) - product(matrix[own], state[...])
        for block in range(rows // 128):
            columns = pl.ds(pl.multiple_of(first + block * 128, 128), 128)
            send[rows + block * ncl : rows + (block + 1) * ncl] = basis_across[:, columns]


def smoothing(chans, ncl, matrix, weights, basis_across, *refs):
    count = len(chans)
    parts, gots = refs[:count], refs[count : 2 * count]
    coarse, sends, weighted = refs[2 * count], refs[2 * count + 1 : -1], refs[-1]
    for channel, part, got in zip(chans, parts, gots):
        rows = channel[3]
        own = pl.ds(first_row(channel), rows)
        resid = part[0:rows] + across(channel[1], got, rows)
        weighted[own] = (weights[own] * resid).astype(jnp.bfloat16)
    for channel, send in zip(chans, sends):
        own = pl.ds(first_row(channel), channel[3])
        send[...] = weights[own] * product(matrix[own], weighted[...])
    coarse[...] = product(basis_across[...].astype(jnp.bfloat16), weighted[...])


def spreading(chans, ncl, weights, basis, *refs):
    gots, out = refs[:-1], refs[-1]
    for channel, got in zip(chans, gots):
        rows = channel[3]
        first = first_row(channel)
        blocks = rows // 128
        for block in range(blocks):
            from_block = (block + blocks // 2) % blocks if channel[1] == BOTH else block
            at = rows + from_block * ncl
            own = pl.ds(pl.multiple_of(first + block * 128, 128), 128)
            weight = weights[own][:, 0:ncl]
            here = weight * basis[own].astype(jnp.float32)
            there = (1.0 - weight) * got[at : at + ncl].T
            both = jnp.concatenate([here, there], axis=1)
            high = both.astype(jnp.bfloat16)
            low = both - high.astype(jnp.float32)
            wide = high.astype(jnp.float32)
            out[own] = jnp.concatenate([wide, wide, low], axis=1).astype(jnp.bfloat16)


def coarse_map(order, kinds, sub, ncl, numbers, kept, got, out, arranged, relative):
    index = lax.axis_index("sub")
    rows_of = order // sub
    padded = kept.shape[0] * 2 // sub
    for block, origin in enumerate(origins(sub)):
        origin = jnp.bitwise_xor(index, origin)
        half = sub // 2
        source = kept if block < half else got
        at = (block % half) * padded
        arranged[pl.ds(pl.multiple_of(origin * padded, 8), padded)] = source[at : at + padded]
        relative[block * ncl : (block + 1) * ncl] = numbers[pl.ds(pl.multiple_of(origin * ncl, 8), ncl)]
    wanted = [index] + [mate(kind, index, sub) for kind in kinds]
    wanted = jnp.concatenate([numbers[pl.ds(pl.multiple_of(w * ncl, 8), ncl)] for w in wanted], axis=0)
    lane = lax.broadcasted_iota(jnp.int32, (wanted.shape[0], sub * padded), 1)
    inside = lane % padded
    held = jnp.where(inside < rows_of, (lane // padded) * rows_of + inside, -1)
    pick = jnp.where(wanted == held, 1.0, 0.0).astype(jnp.float32)
    chosen = jnp.dot(pick, arranged[...], precision=HIGHEST, preferred_element_type=jnp.float32)
    column = lax.broadcasted_iota(jnp.int32, (relative.shape[0], arranged.shape[1]), 1)
    place = jnp.where(relative[...] == column, 1.0, 0.0).astype(jnp.float32)
    out[...] = lax.dot_general(
        chosen, place, (((1,), (1,)), ((), ())), precision=HIGHEST, preferred_element_type=jnp.float32
    )


def coarse_values(ncl, mapping, kept, got, own, sides):
    half = kept.shape[0]
    total = jnp.dot(mapping[:, 0:half], kept[...], precision=HIGHEST, preferred_element_type=jnp.float32)
    total += jnp.dot(mapping[:, half:], got[...], precision=HIGHEST, preferred_element_type=jnp.float32)
    own[...] = total[0:ncl]
    sides[...] = total[ncl:]


def advance(chans, ncl, state, spread, own_values, side_values, refs, out):
    count = len(chans)
    parts, gots, far = refs[:count], refs[count : 2 * count], refs[2 * count :]
    far_at, side_at = 0, 0
    for channel, part, got in zip(chans, parts, gots):
        axis, kind, _, rows = channel
        if axis == "grp":
            theirs = far[far_at][...]
            far_at += 1
        else:
            theirs = side_values[side_at * ncl : (side_at + 1) * ncl]
            side_at += 1
        values = jnp.concatenate([own_values[...], theirs], axis=0)
        high = values.astype(jnp.bfloat16)
        low = (values - high.astype(jnp.float32)).astype(jnp.bfloat16)
        own = pl.ds(first_row(channel), rows)
        update = product(spread[own], jnp.concatenate([high, low, high], axis=0))
        update += part[...] + across(kind, got, rows)
        out[own] = (state[own].astype(jnp.float32) + update).astype(jnp.bfloat16)


def between(chans, ncl, matrix, load, state, spread, own_values, side_values, *refs):
    count = len(chans)
    ins, out, sends = refs[: -count - 1], refs[-count - 1], refs[-count:]
    advance(chans, ncl, state, spread, own_values, side_values, ins, out)
    for channel, send in zip(chans, sends):
        own = pl.ds(first_row(channel), channel[3])
        send[...] = load[own].astype(jnp.float32) - product(matrix[own], out[...])


def closing(chans, ncl, state, spread, own_values, side_values, *refs):
    advance(chans, ncl, state, spread, own_values, side_values, refs[:-1], refs[-1])


def steps(sub):
    step = sub // 2
    while step:
        yield step
        step //= 2


def origins(sub):
    found = [0]
    for step in steps(sub):
        found += [origin ^ step for origin in found]
    return found


def gathered(piece, sub):
    got = None
    for step in steps(sub):
        if got is not None:
            piece = jnp.concatenate([piece, got], axis=0)
        got = lax.ppermute(piece, "sub", [(i, i ^ step) for i in range(sub)])
    return piece, got


def shards(
    schur_t, neumann_t, face_weights, coarse_basis, coarse_inverse, coarse_number, loads, iterate
):
    schur, neumann = schur_t[0, 0], neumann_t[0, 0]
    basis = coarse_basis[0, 0]
    load, state = loads[0, 0], iterate[0, 0]
    iface, columns = state.shape
    ncl = basis.shape[1]
    face = iface // 4
    grp, sub = lax.axis_size("grp"), lax.axis_size("sub")
    chans = channels(grp, sub, face)
    kinds = tuple(c[1] for c in chans if c[0] == "sub")
    far_kinds = tuple(c[1] for c in chans if c[0] == "grp")
    weights = jnp.broadcast_to(face_weights[0, 0][:, None], (iface, columns))
    numbers = coarse_number[0][:, None]
    order = coarse_inverse.shape[2]

    def wide(rows):
        return jax.ShapeDtypeStruct((rows, columns), jnp.float32)

    plain = tuple(wide(c[3]) for c in chans)
    flops = 2 * iface * iface * columns

    def exchange(sends):
        return tuple(swap(send, c[0], c[1]) for c, send in zip(chans, sends))

    basis_across, *parts = call(
        functools.partial(opening, chans),
        (jax.ShapeDtypeStruct((ncl, iface), jnp.float32),)
        + tuple(wide(c[3] + c[3] // 128 * ncl) for c in chans),
        (schur, load, state, basis),
        flops=flops,
    )
    gots = exchange(parts)

    rows_of = coarse_inverse.shape[1]
    inverse = jnp.pad(coarse_inverse[0], ((0, -rows_of % 8), (0, -order % 128)))
    inverse_kept, inverse_got = gathered(inverse, sub)
    mapping = call(
        functools.partial(coarse_map, order, kinds, sub, ncl),
        jax.ShapeDtypeStruct(((1 + len(kinds)) * ncl, sub * ncl), jnp.float32),
        (numbers, inverse_kept, inverse_got),
        scratch=(
            pltpu.VMEM((sub * inverse.shape[0], inverse.shape[1]), jnp.float32),
            pltpu.VMEM((sub * ncl, 1), jnp.int32),
        ),
    )
    spread = call(
        functools.partial(spreading, chans, ncl),
        jax.ShapeDtypeStruct((iface, 6 * ncl), jnp.bfloat16),
        (weights, basis, *gots),
    )

    for step in range(ITERS):
        coarse, *scaled = call(
            functools.partial(smoothing, chans, ncl),
            (wide(ncl),) + plain,
            (neumann, weights, basis_across, *parts, *gots),
            scratch=(pltpu.VMEM((iface, columns), jnp.bfloat16),),
            flops=flops,
        )
        scaled_gots = exchange(scaled)
        kept, got = gathered(coarse, sub)
        own_values, side_values = call(
            functools.partial(coarse_values, ncl),
            (wide(ncl), wide(len(kinds) * ncl)),
            (mapping, kept, got),
        )
        far = [swap(own_values, "grp", kind) for kind in far_kinds]
        ins = (spread, own_values, side_values, *scaled, *scaled_gots, *far)
        if step + 1 < ITERS:
            state, *parts = call(
                functools.partial(between, chans, ncl),
                (jax.ShapeDtypeStruct(state.shape, state.dtype),) + plain,
                (schur, load, state, *ins),
                flops=flops,
            )
            gots = exchange(parts)
        else:
            state = call(
                functools.partial(closing, chans, ncl),
                jax.ShapeDtypeStruct(state.shape, state.dtype),
                (state, *ins),
            )
    return state[None, None]


def solution(mesh):
    return jax.shard_map(
        shards,
        mesh=mesh,
        in_specs=(
            P("grp", "sub", None, None),
            P("grp", "sub", None, None),
            P("grp", "sub", None),
            P("grp", "sub", None, None),
            P("grp", "sub", None),
            P("grp", None),
            P("grp", "sub", None, None),
            P("grp", "sub", None, None),
        ),
        out_specs=P("grp", "sub", None, None),
        check_vma=False,
    )
```

```python
import functools

import jax
import jax.numpy as jnp
from jax import lax
from jax.experimental import pallas as pl
from jax.experimental.pallas import tpu as pltpu
from jax.sharding import PartitionSpec as P

ITERS = 3
HIGHEST = lax.Precision.HIGHEST
EVEN, ODD, LOW, HIGH = range(4)
WHOLE = pl.BlockSpec(memory_space=pltpu.VMEM)
AWAY = pl.BlockSpec(memory_space=pltpu.HBM)
ANYWHERE = pl.BlockSpec(memory_space=pl.ANY)


def channels(grp, sub, face):
    found = []
    for axis, devices, base in (("grp", grp, 2 * face), ("sub", sub, 0)):
        for kind in (LOW, HIGH) if devices == 2 else (ODD, EVEN):
            found.append((axis, kind, base, face))
    return tuple(found)


def mate(kind, index, devices):
    if kind in (LOW, HIGH):
        return 1 - index
    step = 1 - 2 * (index % 2)
    if kind == ODD:
        step = -step
    return (index + step + devices) % devices


def swap(array, axis, kind):
    devices = lax.axis_size(axis)
    return lax.ppermute(array, axis, [(i, mate(kind, i, devices)) for i in range(devices)])


def exchange(chans, sends):
    gots = [swap(send, c[0], c[1]) for c, send in zip(chans, sends)]
    for at, c in enumerate(chans):
        if c[1] == LOW:
            gots[at], gots[at + 1] = gots[at + 1], gots[at]
    return tuple(gots)


def first_row(channel):
    axis, kind, base, rows = channel
    if kind in (LOW, HIGH):
        return base + (kind - LOW) * rows
    odd = lax.rem(lax.axis_index(axis), 2)
    return pl.multiple_of(base + (odd if kind == ODD else 1 - odd) * rows, rows)


def product(a, b):
    return jnp.dot(a, b, preferred_element_type=jnp.float32)


def call(body, outs, args, scratch=(), flops=0, away=0, after=()):
    moved = sum(a.size * a.dtype.itemsize for a in args)
    ahead = len(after)
    return pl.pallas_call(
        lambda *refs: body(*refs[ahead:]),
        out_shape=outs,
        in_specs=[ANYWHERE] * ahead + [AWAY] * away + [WHOLE] * (len(args) - away),
        out_specs=jax.tree.map(lambda _: WHOLE, outs),
        scratch_shapes=scratch,
        cost_estimate=pl.CostEstimate(flops=flops, bytes_accessed=moved, transcendentals=0),
        compiler_params=pltpu.CompilerParams(vmem_limit_bytes=32 * 2**20),
    )(*after, *args)


def send_basis(channel, basis_across, send):
    rows = channel[3]
    ncl = basis_across.shape[0]
    for block in range(rows // 128):
        columns = pl.ds(pl.multiple_of(first_row(channel) + block * 128, 128), 128)
        piece = basis_across[:, columns].astype(jnp.float32)
        send[rows + block * ncl : rows + (block + 1) * ncl] = piece


def opening(chans, matrix, load, state, basis_across, *refs):
    sends, (rows, mine, now, basis, sems) = refs[:-5], refs[-5:]
    face = chans[0][3]
    pairs = [(state, now), (load, mine)]
    order = (2, 3, 0, 1)
    pairs += [(matrix.at[pl.ds(at * face, face)], rows.at[pl.ds(at * face, face)]) for at in order]
    pairs.append((basis_across, basis))
    copies = [pltpu.make_async_copy(a, b, sems.at[i]) for i, (a, b) in enumerate(pairs)]
    for copy in copies:
        copy.start()
    for copy in copies[:4]:
        copy.wait()
    for at, (channel, send) in enumerate(zip(chans, sends)):
        if at == 2:
            for copy in copies[4:]:
                copy.wait()
        own = pl.ds(first_row(channel), channel[3])
        send[0 : channel[3]] = mine[own].astype(jnp.float32) - product(rows[own], now[...])
    for channel, send in zip(chans, sends):
        send_basis(channel, basis, send)


def smoothing_far(chans, far, matrix, weights, *refs):
    count = len(chans)
    parts, gots = refs[:count], refs[count : 2 * count]
    weighted, sends = refs[2 * count], refs[2 * count + 1 :]
    for channel, part, got in zip(chans, parts, gots):
        rows = channel[3]
        own = pl.ds(first_row(channel), rows)
        weighted[own] = (weights[own] * (part[0:rows] + got[0:rows])).astype(jnp.bfloat16)
    for channel, send in zip(far, sends):
        own = pl.ds(first_row(channel), channel[3])
        send[...] = weights[own] * product(matrix[own], weighted[...])


def smoothing_near(near, matrix, weights, weighted, basis_across, coarse, *sends):
    coarse[...] = product(basis_across[...], weighted[...])
    for channel, send in zip(near, sends):
        own = pl.ds(first_row(channel), channel[3])
        send[...] = weights[own] * product(matrix[own], weighted[...])


def spreading(chans, weights, basis_across, *refs):
    gots, out = refs[:-1], refs[-1]
    ncl = basis_across.shape[0]
    for channel, got in zip(chans, gots):
        rows = channel[3]
        for block in range(rows // 128):
            at = rows + block * ncl
            start = pl.multiple_of(first_row(channel) + block * 128, 128)
            own = pl.ds(start, 128)
            weight = weights[own][:, 0:ncl]
            here = weight * basis_across[:, own].astype(jnp.float32).T
            there = (1.0 - weight) * got[at : at + ncl].T
            both = jnp.concatenate([here, there], axis=1)
            high = both.astype(jnp.bfloat16).astype(jnp.float32)
            out[own] = jnp.concatenate([high, high, both - high], axis=1).astype(jnp.bfloat16)


def padding(rows, out):
    out[...] = jnp.zeros_like(out)
    out[0 : rows.shape[0], 0 : rows.shape[1]] = rows[...]


def coarse_map(order, kinds, sub, ncl, numbers, inverse, out, upright):
    index = lax.axis_index("sub")
    rows_of = order // sub
    padded = inverse.shape[0] // sub
    upright[...] = jnp.broadcast_to(numbers[...].astype(jnp.float32), (8, numbers.shape[1])).T
    wanted = [index] + [mate(kind, index, sub) for kind in kinds]
    wanted = [upright[pl.ds(pl.multiple_of(w * ncl, 8), ncl)] for w in wanted]
    wanted = jnp.concatenate(wanted, axis=0)[:, 0:1].astype(jnp.int32)
    lane = lax.broadcasted_iota(jnp.int32, (wanted.shape[0], sub * padded), 1)
    inside = lane % padded
    held = jnp.where(inside < rows_of, (lane // padded) * rows_of + inside, -1)
    pick = jnp.where(wanted == held, 1.0, 0.0).astype(jnp.float32)
    chosen = jnp.dot(pick, inverse[...], precision=HIGHEST, preferred_element_type=jnp.float32)
    column = lax.broadcasted_iota(jnp.int32, (upright.shape[0], inverse.shape[1]), 1)
    place = jnp.where(upright[...][:, 0:1].astype(jnp.int32) == column, 1.0, 0.0).astype(jnp.float32)
    out[...] = lax.dot_general(
        chosen, place, (((1,), (1,)), ((), ())), precision=HIGHEST, preferred_element_type=jnp.float32
    )


def coarse_values(ncl, grp, kinds, mapping, *refs):
    maps, pieces, near, far = refs[: len(kinds)], refs[-3], refs[-2], refs[-1]
    rows = pieces.shape[0] // grp
    mine = lax.axis_index("grp")

    def values(maps, index):
        group = pieces[pl.ds(pl.multiple_of(index * rows, 8), rows)]
        return jnp.dot(maps, group, precision=HIGHEST, preferred_element_type=jnp.float32)

    near[...] = values(mapping[...], mine)
    for at, (kind, theirs) in enumerate(zip(kinds, maps)):
        far[at * ncl : (at + 1) * ncl] = values(theirs[...], mate(kind, mine, grp))


def advance(chans, ncl, state, spread, near_values, far_values, refs, out):
    count = len(chans)
    parts, gots = refs[:count], refs[count:]
    far_at, side_at = 0, 1
    for channel, part, got in zip(chans, parts, gots):
        axis, kind, _, rows = channel
        if axis == "grp":
            theirs = far_values[far_at * ncl : (far_at + 1) * ncl]
            far_at += kind != LOW
        else:
            theirs = near_values[side_at * ncl : (side_at + 1) * ncl]
            side_at += kind != LOW
        values = jnp.concatenate([near_values[0:ncl], theirs], axis=0)
        high = values.astype(jnp.bfloat16)
        low = (values - high.astype(jnp.float32)).astype(jnp.bfloat16)
        own = pl.ds(first_row(channel), rows)
        update = product(spread[own], jnp.concatenate([high, low, high], axis=0))
        update += part[...] + got[...]
        out[own] = (state[own].astype(jnp.float32) + update).astype(jnp.bfloat16)


def between_far(chans, far, ncl, matrix, load, state, spread, near_values, far_values, *refs):
    count = len(far)
    ins, out, sends = refs[: -count - 1], refs[-count - 1], refs[-count:]
    advance(chans, ncl, state, spread, near_values, far_values, ins, out)
    between_near(far, matrix, load, out, *sends)


def between_near(chans, matrix, load, state, *sends):
    for channel, send in zip(chans, sends):
        own = pl.ds(first_row(channel), channel[3])
        send[...] = load[own].astype(jnp.float32) - product(matrix[own], state[...])


def closing(chans, ncl, state, spread, near_values, far_values, *refs):
    advance(chans, ncl, state, spread, near_values, far_values, refs[:-1], refs[-1])


def gathered(piece, axes):
    devices = lax.axis_size(axes)
    copies = jnp.broadcast_to(piece[None], (devices, *piece.shape))
    whole = lax.all_to_all(copies, axes, 0, 0, tiled=True)
    return whole.reshape(devices * piece.shape[0], piece.shape[1])


def shards(
    schur_t, neumann_t, face_weights, coarse_basis, coarse_inverse, coarse_number, loads, iterate
):
    schur, neumann = schur_t[0, 0], neumann_t[0, 0]
    basis_across = coarse_basis[0, 0].T
    load, state = loads[0, 0], iterate[0, 0]
    iface, columns = state.shape
    ncl = basis_across.shape[0]
    face = iface // 4
    grp, sub = lax.axis_size("grp"), lax.axis_size("sub")
    chans = channels(grp, sub, face)
    far, near = chans[:2], chans[2:]
    kinds = tuple(c[1] for c in near if c[1] != HIGH)
    far_kinds = tuple(c[1] for c in far if c[1] != HIGH)
    order = coarse_inverse.shape[2]

    def wide(rows):
        return jax.ShapeDtypeStruct((rows, columns), jnp.float32)

    half = jax.ShapeDtypeStruct(state.shape, jnp.bfloat16)
    plain = (wide(face),) * 2
    long = (wide(face + face // 128 * ncl),) * 2
    flops = iface * iface * columns

    parts = call(
        functools.partial(opening, chans),
        long * 2,
        (schur, load, state, basis_across),
        scratch=(
            pltpu.VMEM(schur.shape, schur.dtype),
            pltpu.VMEM(load.shape, load.dtype),
            pltpu.VMEM(state.shape, state.dtype),
            pltpu.VMEM(basis_across.shape, basis_across.dtype),
            pltpu.SemaphoreType.DMA((7,)),
        ),
        flops=2 * flops,
        away=4,
    )
    gots = exchange(chans, parts)

    weights = jnp.broadcast_to(face_weights[0, 0][:, None], (iface, columns))
    rows_of = coarse_inverse.shape[1]
    inverse = call(
        padding,
        jax.ShapeDtypeStruct((rows_of + -rows_of % 8, order + -order % 128), jnp.float32),
        (coarse_inverse[0],),
        after=parts[-1:],
    )
    mapping = call(
        functools.partial(coarse_map, order, kinds, sub, ncl),
        jax.ShapeDtypeStruct(((1 + len(kinds)) * ncl, sub * ncl), jnp.float32),
        (coarse_number, gathered(inverse, "sub")),
        scratch=(pltpu.VMEM((sub * ncl, 8), jnp.float32),),
    )
    far_maps = [swap(mapping[0:ncl], "grp", kind) for kind in far_kinds]
    spread = call(
        functools.partial(spreading, chans),
        jax.ShapeDtypeStruct((iface, 6 * ncl), jnp.bfloat16),
        (weights, basis_across, *gots),
    )

    for step in range(ITERS):
        weighted, *far_scaled = call(
            functools.partial(smoothing_far, chans, far),
            (half,) + plain,
            (neumann, weights, *parts, *gots),
            flops=flops,
        )
        coarse, *near_scaled = call(
            functools.partial(smoothing_near, near),
            (wide(ncl),) + plain,
            (neumann, weights, weighted, basis_across),
            flops=flops,
        )
        scaled = (*far_scaled, *near_scaled)
        scaled_gots = exchange(chans, scaled)
        near_values, far_values = call(
            functools.partial(coarse_values, ncl, grp, far_kinds),
            (wide((1 + len(kinds)) * ncl), wide(len(far_kinds) * ncl)),
            (mapping, *far_maps, gathered(coarse, ("grp", "sub"))),
        )
        ins = (spread, near_values, far_values, *scaled, *scaled_gots)
        if step + 1 < ITERS:
            state, *far_parts = call(
                functools.partial(between_far, chans, far, ncl),
                (half,) + plain,
                (schur, load, state, *ins),
                flops=flops,
            )
            near_parts = call(
                functools.partial(between_near, near), plain, (schur, load, state), flops=flops
            )
            parts = (*far_parts, *near_parts)
            gots = exchange(chans, parts)
        else:
            state = call(functools.partial(closing, chans, ncl), half, (state, *ins))
    return state[None, None]


def solution(mesh):
    return jax.shard_map(
        shards,
        mesh=mesh,
        in_specs=(
            P("grp", "sub", None, None),
            P("grp", "sub", None, None),
            P("grp", "sub", None),
            P("grp", "sub", None, None),
            P("grp", "sub", None),
            P("grp", None),
            P("grp", "sub", None, None),
            P("grp", "sub", None, None),
        ),
        out_specs=P("grp", "sub", None, None),
        check_vma=False,
    )
```

```python
import functools

import jax
import jax.numpy as jnp
from jax import lax
from jax.experimental import pallas as pl
from jax.experimental.pallas import tpu as pltpu
from jax.sharding import PartitionSpec as P

ITERS = 3
HIGHEST = lax.Precision.HIGHEST
EVEN, ODD, BOTH = range(3)
LANES = 128
MIB = 2**20
WHOLE = pl.BlockSpec(memory_space=pltpu.VMEM)
AWAY = pl.BlockSpec(memory_space=pltpu.HBM)
ANYWHERE = pl.BlockSpec(memory_space=pl.ANY)


def channels(grp, sub, face):
    found = []
    for axis, devices, base in (("grp", grp, 2 * face), ("sub", sub, 0)):
        if devices == 2:
            found.append((axis, BOTH, base, 2 * face))
        else:
            found += [(axis, ODD, base, face), (axis, EVEN, base, face)]
    return tuple(found)


def mate(kind, index, devices):
    if kind == BOTH:
        return 1 - index
    step = 1 - 2 * (index % 2)
    if kind == ODD:
        step = -step
    return (index + step + devices) % devices


def swap(array, channel):
    axis, kind = channel[:2]
    devices = lax.axis_size(axis)
    return lax.ppermute(array, axis, [(i, mate(kind, i, devices)) for i in range(devices)])


def exchange(chans, sends):
    return tuple(swap(send, channel) for channel, send in zip(chans, sends))


def first_row(channel):
    axis, kind, base, rows = channel
    if kind == BOTH:
        return base
    odd = lax.rem(lax.axis_index(axis), 2)
    return pl.multiple_of(base + (odd if kind == ODD else 1 - odd) * rows, rows)


def own_rows(channel):
    return pl.ds(first_row(channel), channel[3])


def row_blocks(channel):
    blocks = channel[3] // LANES
    for block in range(blocks):
        rows = pl.ds(pl.multiple_of(first_row(channel) + block * LANES, LANES), LANES)
        yield block, rows, (block + blocks // 2) % blocks if channel[1] == BOTH else block


def across(channel, got):
    rows = channel[3]
    if channel[1] == BOTH:
        return jnp.concatenate([got[rows // 2 : rows], got[0 : rows // 2]], axis=0)
    return got[0:rows]


def product(a, b):
    return jnp.dot(a, b, preferred_element_type=jnp.float32)


def split(values, axis):
    high = values.astype(jnp.bfloat16)
    low = (values - high.astype(jnp.float32)).astype(jnp.bfloat16)
    return jnp.concatenate([high, low, high], axis=axis)


def thrice(values):
    high = values.astype(jnp.bfloat16).astype(jnp.float32)
    return jnp.concatenate([high, high, values - high], axis=1).astype(jnp.bfloat16)


def call(body, outs, args, scratch=(), flops=0, away=0, after=(), grant=16 * MIB):
    moved = sum(a.size * a.dtype.itemsize for a in args)
    ahead = len(after)
    return pl.pallas_call(
        lambda *refs: body(*refs[ahead:]),
        out_shape=outs,
        in_specs=[ANYWHERE] * ahead + [AWAY] * away + [WHOLE] * (len(args) - away),
        out_specs=jax.tree.map(lambda _: WHOLE, outs),
        scratch_shapes=scratch,
        cost_estimate=pl.CostEstimate(flops=flops, bytes_accessed=moved, transcendentals=0),
        compiler_params=pltpu.CompilerParams(vmem_limit_bytes=grant),
    )(*after, *args)


class Values:
    def __init__(self, chans, ncl, near, far, second):
        self.chans, self.ncl = chans, ncl
        self.near, self.far, self.second = near, far, second
        self.order = near_order(chans)

    def at(self, *path):
        grp = [c for c in path if self.chans[c][0] == "grp"]
        sub = [c for c in path if self.chans[c][0] == "sub"]
        grp, sub = [[] if len(p) == 2 and p[0] == p[1] else p for p in (grp, sub)]
        if len(grp) == 2:
            return self.second[grp[0]][...]
        source = self.far[grp[0]] if grp else self.near
        place = self.order.index(tuple(sub)) * self.ncl
        return source[place : place + self.ncl]

    def around(self, *path):
        return [self.at(*path)] + [self.at(*path, c) for c in range(len(self.chans))]


def near_order(chans):
    kinds = [c for c, channel in enumerate(chans) if channel[0] == "sub"]
    return [()] + [(c,) for c in kinds] + [(c, d) for c in kinds for d in kinds if c != d]


def value_refs(chans, ncl, refs):
    far = sum(channel[0] == "grp" for channel in chans)
    second = far if far > 1 else 0
    values = Values(chans, ncl, refs[0], refs[1 : 1 + far], refs[1 + far : 1 + far + second])
    return values, refs[1 + far + second :]


def opening(chans, matrix, load, state, basis_across, *refs):
    sends, (rows, mine, now, basis, sems) = refs[:-5], refs[-5:]
    half = matrix.shape[0] // 2
    pairs = [(state, now), (load, mine)]
    pairs += [(matrix.at[pl.ds(at, half)], rows.at[pl.ds(at, half)]) for at in (half, 0)]
    pairs.append((basis_across, basis))
    copies = [pltpu.make_async_copy(a, b, sems.at[i]) for i, (a, b) in enumerate(pairs)]
    for copy in copies:
        copy.start()
    for copy in copies[:3]:
        copy.wait()
    waiting = copies[3:]
    for channel, send in zip(chans, sends):
        if channel[0] == "sub":
            while waiting:
                waiting.pop(0).wait()
        own = own_rows(channel)
        send[0 : channel[3]] = mine[own].astype(jnp.float32) - product(rows[own], now[...])
    ncl = basis.shape[0]
    for channel, send in zip(chans, sends):
        for block, columns, _ in row_blocks(channel):
            at = channel[3] + block * ncl
            send[at : at + ncl] = basis[:, columns].astype(jnp.float32)


def smooth(chans, far, matrix, weights, parts, gots, weighted, sends, correction=None):
    for at, (channel, part, got) in enumerate(zip(chans, parts, gots)):
        own = own_rows(channel)
        resid = part[0 : channel[3]] + across(channel, got)
        if correction is not None:
            resid -= correction(at, own)
        weighted[own] = (weights[own] * resid).astype(jnp.bfloat16)
    smoothing_near(far, matrix, weights, weighted, sends)


def smoothing_near(chans, matrix, weights, weighted, sends):
    for channel, send in zip(chans, sends):
        own = own_rows(channel)
        send[...] = weights[own] * product(matrix[own], weighted[...])


def smoothing_first(chans, far, matrix, weights, *refs):
    count = len(chans)
    parts, gots = refs[:count], refs[count : 2 * count]
    smooth(chans, far, matrix, weights, parts, gots, refs[2 * count], refs[2 * count + 1 :])


def smoothing_far(chans, far, ncl, matrix, weights, ahead, spread, reach, *refs):
    values, refs = value_refs(chans, ncl, refs)
    count = len(chans)
    parts, gots = refs[:count], refs[count : 2 * count]
    state, weighted, sends = refs[2 * count], refs[2 * count + 1], refs[2 * count + 2 :]
    here = values.around()

    def correction(at, own):
        pair = jnp.concatenate([here[0], values.at(at)], axis=0)
        state[own] = (ahead[own] + product(spread[own], split(pair, 0))).astype(state.dtype)
        both = jnp.concatenate(here + values.around(at), axis=0)
        return product(reach[own], split(both, 0))

    smooth(chans, far, matrix, weights, parts, gots, weighted, sends, correction)


def smoothing_sub(near, matrix, weights, weighted, basis_across, coarse, *sends):
    coarse[...] = product(basis_across[...], weighted[...])
    smoothing_near(near, matrix, weights, weighted, sends)


def spreading(chans, weights, basis_across, *refs):
    gots, thin, full = refs[:-2], refs[-2], refs[-1]
    ncl = basis_across.shape[0]
    width = full.shape[1] // 2
    for at, (channel, got) in enumerate(zip(chans, gots)):
        for _, own, block in row_blocks(channel):
            from_row = channel[3] + block * ncl
            weight = weights[own][:, 0:ncl]
            here = weight * basis_across[:, own].astype(jnp.float32).T
            there = (1.0 - weight) * got[from_row : from_row + ncl].T
            thin[own] = thrice(jnp.concatenate([here, there], axis=1))
            before = [jnp.zeros((LANES, at * ncl), jnp.float32)] if at else []
            behind = jnp.zeros((LANES, width - (at + 2) * ncl), jnp.float32)
            placed = jnp.concatenate([here, *before, there, behind], axis=1)
            high = placed.astype(jnp.bfloat16)
            full[own, 0:width] = high
            full[own, width:] = (placed - high.astype(jnp.float32)).astype(jnp.bfloat16)


def responding(chans, count, matrix, full, out, *sends):
    width = out.shape[1]
    both = product(matrix[...], full[...])
    out[...] = both[:, 0:width] + both[:, width:]
    for channel, send in zip(chans, sends):
        for block, own, _ in row_blocks(channel):
            send[block * count : (block + 1) * count] = out[own].T[0:count]


def reaching(chans, count, response, *refs):
    gots, out = refs[:-1], refs[-1]
    for channel, got in zip(chans, gots):
        for _, own, block in row_blocks(channel):
            theirs = got[block * count : (block + 1) * count].T
            out[own] = thrice(jnp.concatenate([response[own][:, 0:count], theirs], axis=1))


def padding(rows, out):
    out[...] = jnp.zeros_like(out)
    out[0 : rows.shape[0], 0 : rows.shape[1]] = rows[...]


def joining(first, second, out):
    out[...] = jnp.concatenate([first[...], second[...]], axis=0)


def coarse_map(chans, order, sub, ncl, numbers, kept, got, out, arranged, upright, relative):
    index = lax.axis_index("sub")
    rows_of = order // sub
    padded = kept.shape[0] * 2 // sub
    upright[...] = jnp.broadcast_to(numbers[...].astype(jnp.float32), (8, numbers.shape[1])).T
    for block, origin in enumerate(origins(sub)):
        origin = jnp.bitwise_xor(index, origin)
        half = sub // 2
        source = kept if block < half else got
        at = (block % half) * padded
        arranged[pl.ds(pl.multiple_of(origin * padded, 8), padded)] = source[at : at + padded]
        relative[block * ncl : (block + 1) * ncl] = upright[pl.ds(pl.multiple_of(origin * ncl, 8), ncl)]
    wanted = []
    for path in near_order(chans):
        place = index
        for c in path:
            place = mate(chans[c][1], place, sub)
        wanted.append(upright[pl.ds(pl.multiple_of(place * ncl, 8), ncl)])
    wanted = jnp.concatenate(wanted, axis=0)[:, 0:1].astype(jnp.int32)
    lane = lax.broadcasted_iota(jnp.int32, (wanted.shape[0], sub * padded), 1)
    inside = lane % padded
    held = jnp.where(inside < rows_of, (lane // padded) * rows_of + inside, -1)
    pick = jnp.where(wanted == held, 1.0, 0.0).astype(jnp.float32)
    chosen = jnp.dot(pick, arranged[...], precision=HIGHEST, preferred_element_type=jnp.float32)
    column = lax.broadcasted_iota(jnp.int32, (relative.shape[0], arranged.shape[1]), 1)
    place = jnp.where(relative[...][:, 0:1].astype(jnp.int32) == column, 1.0, 0.0).astype(jnp.float32)
    out[...] = lax.dot_general(
        chosen, place, (((1,), (1,)), ((), ())), precision=HIGHEST, preferred_element_type=jnp.float32
    )


def coarse_values(mapping, kept, got, out):
    half = kept.shape[0]
    total = jnp.dot(mapping[:, 0:half], kept[...], precision=HIGHEST, preferred_element_type=jnp.float32)
    total += jnp.dot(mapping[:, half:], got[...], precision=HIGHEST, preferred_element_type=jnp.float32)
    out[...] = total


def between_far(chans, far, matrix, load, state, *refs):
    count = len(chans)
    parts, gots = refs[:count], refs[count : 2 * count]
    ahead, rounded, sends = refs[2 * count], refs[2 * count + 1], refs[2 * count + 2 :]
    for channel, part, got in zip(chans, parts, gots):
        own = own_rows(channel)
        ahead[own] = state[own].astype(jnp.float32) + part[...] + across(channel, got)
        rounded[own] = ahead[own].astype(rounded.dtype)
    between_near(far, matrix, load, rounded, *sends)


def between_near(chans, matrix, load, state, *sends):
    for channel, send in zip(chans, sends):
        own = own_rows(channel)
        send[...] = load[own].astype(jnp.float32) - product(matrix[own], state[...])


def closing(chans, ncl, state, spread, *refs):
    values, refs = value_refs(chans, ncl, refs)
    count = len(chans)
    parts, gots, out = refs[:count], refs[count : 2 * count], refs[2 * count]
    for at, (channel, part, got) in enumerate(zip(chans, parts, gots)):
        own = own_rows(channel)
        pair = jnp.concatenate([values.at(), values.at(at)], axis=0)
        update = product(spread[own], split(pair, 0)) + part[...] + across(channel, got)
        out[own] = (state[own].astype(jnp.float32) + update).astype(out.dtype)


def steps(sub):
    found, step = [], sub // 2
    while step:
        found.append(step)
        step //= 2
    return found


def origins(sub):
    found = [0]
    for step in steps(sub):
        found += [origin ^ step for origin in found]
    return found


def gathered(piece, sub, hold=()):
    got = None
    for at, step in enumerate(steps(sub)):
        if got is not None and hold and at == len(steps(sub)) // 2:
            joined = jax.ShapeDtypeStruct((2 * piece.shape[0], piece.shape[1]), piece.dtype)
            piece = call(joining, joined, (piece, got), after=hold)
        elif got is not None:
            piece = jnp.concatenate([piece, got], axis=0)
        got = lax.ppermute(piece, "sub", [(i, i ^ step) for i in range(sub)])
    return piece, got


def shards(
    schur_t, neumann_t, face_weights, coarse_basis, coarse_inverse, coarse_number, loads, iterate
):
    schur, neumann = schur_t[0, 0], neumann_t[0, 0]
    basis_across = coarse_basis[0, 0].T
    load, state = loads[0, 0], iterate[0, 0]
    iface, columns = state.shape
    ncl = basis_across.shape[0]
    face = iface // 4
    grp, sub = lax.axis_size("grp"), lax.axis_size("sub")
    chans = channels(grp, sub, face)
    far = tuple(c for c in chans if c[0] == "grp")
    near = chans[len(far) :]
    around = (len(chans) + 1) * ncl
    order = coarse_inverse.shape[2]

    def wide(rows, width=columns):
        return jax.ShapeDtypeStruct((rows, width), jnp.float32)

    def short(rows, width=columns):
        return jax.ShapeDtypeStruct((rows, width), jnp.bfloat16)

    far_plain, near_plain = [tuple(wide(c[3]) for c in group) for group in (far, near)]
    half = short(iface)
    flops = iface * iface * columns

    parts = call(
        functools.partial(opening, chans),
        tuple(wide(c[3] + c[3] // LANES * ncl) for c in chans),
        (schur, load, state, basis_across),
        scratch=(
            pltpu.VMEM(schur.shape, schur.dtype),
            pltpu.VMEM(load.shape, load.dtype),
            pltpu.VMEM(state.shape, state.dtype),
            pltpu.VMEM(basis_across.shape, basis_across.dtype),
            pltpu.SemaphoreType.DMA((5,)),
        ),
        flops=2 * flops,
        away=4,
        grant=56 * MIB,
    )
    gots = exchange(chans, parts)

    weights = jnp.broadcast_to(face_weights[0, 0][:, None], (iface, columns))
    rows_of = coarse_inverse.shape[1]
    inverse = call(
        padding,
        wide(rows_of + -rows_of % 8, order + -order % LANES),
        (coarse_inverse[0],),
        after=parts[-1:],
    )
    inverse_kept, inverse_got = gathered(inverse, sub)
    mapping = call(
        functools.partial(coarse_map, chans, order, sub, ncl),
        wide(len(near_order(chans)) * ncl, sub * ncl),
        (coarse_number, inverse_kept, inverse_got),
        scratch=(
            pltpu.VMEM((sub * inverse.shape[0], inverse.shape[1]), jnp.float32),
            pltpu.VMEM((sub * ncl, 8), jnp.float32),
            pltpu.VMEM((sub * ncl, 8), jnp.float32),
        ),
    )

    def coarse_step(coarse, hold=()):
        own = call(coarse_values, wide(mapping.shape[0]), (mapping, *gathered(coarse, sub, hold)))
        known = own[0 : (1 + len(near)) * ncl]
        theirs = [swap(known, channel) for channel in far]
        beyond = []
        if len(far) > 1:
            beyond = [swap(theirs[1 - at][0:ncl], channel) for at, channel in enumerate(far)]
        return (own, *theirs, *beyond)

    for step in range(ITERS):
        if step == 0:
            weighted, *far_scaled = call(
                functools.partial(smoothing_first, chans, far),
                (half,) + far_plain,
                (neumann, weights, *parts, *gots),
                flops=flops,
            )
        else:
            values = coarse_step(coarse, hold=parts[:1])
            state, weighted, *far_scaled = call(
                functools.partial(smoothing_far, chans, far, ncl),
                (half, half) + far_plain,
                (neumann, weights, ahead, spread, reach, *values, *parts, *gots),
                flops=flops,
            )
        coarse, *near_scaled = call(
            functools.partial(smoothing_sub, near),
            (wide(ncl),) + near_plain,
            (neumann, weights, weighted, basis_across),
            flops=flops,
        )
        scaled = (*far_scaled, *near_scaled)
        scaled_gots = exchange(chans, scaled)
        if step == 0:
            width = around + -around % LANES
            spread, full = call(
                functools.partial(spreading, chans),
                (short(iface, 6 * ncl), short(iface, 2 * width)),
                (weights, basis_across, *gots),
                after=near_scaled[:1],
            )
            response, *sends = call(
                functools.partial(responding, chans, around),
                (wide(iface, width),) + tuple(wide(c[3] // LANES * around, LANES) for c in chans),
                (schur, full),
                flops=2 * flops,
            )
            reach = call(
                functools.partial(reaching, chans, around),
                short(iface, 6 * around),
                (response, *exchange(chans, sends)),
            )
        if step + 1 < ITERS:
            ahead, rounded, *far_parts = call(
                functools.partial(between_far, chans, far),
                (wide(iface), half) + far_plain,
                (schur, load, state, *scaled, *scaled_gots),
                flops=flops,
            )
            near_parts = call(
                functools.partial(between_near, near), near_plain, (schur, load, rounded), flops=flops
            )
            parts = (*far_parts, *near_parts)
            gots = exchange(chans, parts)
    values = coarse_step(coarse)
    out = call(
        functools.partial(closing, chans, ncl),
        half,
        (state, spread, *values, *scaled, *scaled_gots),
    )
    return out[None, None]


def solution(mesh):
    return jax.shard_map(
        shards,
        mesh=mesh,
        in_specs=(
            P("grp", "sub", None, None),
            P("grp", "sub", None, None),
            P("grp", "sub", None),
            P("grp", "sub", None, None),
            P("grp", "sub", None),
            P("grp", None),
            P("grp", "sub", None, None),
            P("grp", "sub", None, None),
        ),
        out_specs=P("grp", "sub", None, None),
        check_vma=False,
    )
```

```python
import functools

import jax
import jax.numpy as jnp
from jax import lax
from jax.experimental import pallas as pl
from jax.experimental.pallas import tpu as pltpu
from jax.sharding import PartitionSpec as P

ITERS = 3
HIGHEST = lax.Precision.HIGHEST
EVEN, ODD, BOTH = range(3)
LANES = 128
PIECES = 8
MIB = 2**20
WHOLE = pl.BlockSpec(memory_space=pltpu.VMEM)
AWAY = pl.BlockSpec(memory_space=pltpu.HBM)
ANYWHERE = pl.BlockSpec(memory_space=pl.ANY)


def channels(grp, sub, face):
    found = []
    for axis, devices, base in (("grp", grp, 2 * face), ("sub", sub, 0)):
        if devices == 2:
            found.append((axis, BOTH, base, 2 * face))
        else:
            found += [(axis, ODD, base, face), (axis, EVEN, base, face)]
    return tuple(found)


def mate(kind, index, devices):
    if kind == BOTH:
        return 1 - index
    step = 1 - 2 * (index % 2)
    if kind == ODD:
        step = -step
    return (index + step + devices) % devices


def swap(array, channel):
    axis, kind = channel[:2]
    devices = lax.axis_size(axis)
    return lax.ppermute(array, axis, [(i, mate(kind, i, devices)) for i in range(devices)])


def exchange(chans, sends):
    return tuple(swap(send, channel) for channel, send in zip(chans, sends))


def first_row(channel):
    axis, kind, base, rows = channel
    if kind == BOTH:
        return base
    odd = lax.rem(lax.axis_index(axis), 2)
    return pl.multiple_of(base + (odd if kind == ODD else 1 - odd) * rows, rows)


def own_rows(channel):
    return pl.ds(first_row(channel), channel[3])


def row_blocks(channel):
    blocks = channel[3] // LANES
    for block in range(blocks):
        rows = pl.ds(pl.multiple_of(first_row(channel) + block * LANES, LANES), LANES)
        yield block, rows, (block + blocks // 2) % blocks if channel[1] == BOTH else block


def across(channel, got):
    rows = channel[3]
    if channel[1] == BOTH:
        return jnp.concatenate([got[rows // 2 : rows], got[0 : rows // 2]], axis=0)
    return got[0:rows]


def product(a, b):
    return jnp.dot(a, b, preferred_element_type=jnp.float32)


def split(values, axis):
    high = values.astype(jnp.bfloat16)
    low = (values - high.astype(jnp.float32)).astype(jnp.bfloat16)
    return jnp.concatenate([high, low, high], axis=axis)


def thrice(values):
    high = values.astype(jnp.bfloat16).astype(jnp.float32)
    return jnp.concatenate([high, high, values - high], axis=1).astype(jnp.bfloat16)


def call(body, outs, args, scratch=(), flops=0, away=0, after=(), grant=16 * MIB):
    moved = sum(a.size * a.dtype.itemsize for a in args)
    ahead = len(after)
    return pl.pallas_call(
        lambda *refs: body(*refs[ahead:]),
        out_shape=outs,
        in_specs=[ANYWHERE] * ahead + [AWAY] * away + [WHOLE] * (len(args) - away),
        out_specs=jax.tree.map(lambda _: WHOLE, outs),
        scratch_shapes=scratch,
        cost_estimate=pl.CostEstimate(flops=flops, bytes_accessed=moved, transcendentals=0),
        compiler_params=pltpu.CompilerParams(vmem_limit_bytes=grant),
    )(*after, *args)


class Values:
    def __init__(self, chans, ncl, near, far, second):
        self.chans, self.ncl = chans, ncl
        self.near, self.far, self.second = near, far, second
        self.order = near_order(chans)

    def at(self, *path):
        grp = [c for c in path if self.chans[c][0] == "grp"]
        sub = [c for c in path if self.chans[c][0] == "sub"]
        grp, sub = [[] if len(p) == 2 and p[0] == p[1] else p for p in (grp, sub)]
        if len(grp) == 2:
            return self.second[grp[0]][...]
        source = self.far[grp[0]] if grp else self.near
        place = self.order.index(tuple(sub)) * self.ncl
        return source[place : place + self.ncl]

    def around(self, *path):
        return [self.at(*path)] + [self.at(*path, c) for c in range(len(self.chans))]


def near_order(chans):
    kinds = [c for c, channel in enumerate(chans) if channel[0] == "sub"]
    return [()] + [(c,) for c in kinds] + [(c, d) for c in kinds for d in kinds if c != d]


def value_refs(chans, ncl, refs):
    far = sum(channel[0] == "grp" for channel in chans)
    second = far if far > 1 else 0
    values = Values(chans, ncl, refs[0], refs[1 : 1 + far], refs[1 + far : 1 + far + second])
    return values, refs[1 + far + second :]


def opening(chans, matrix, load, state, basis_across, *refs):
    sends, (rows, mine, now, basis, sems) = refs[:-5], refs[-5:]
    piece = matrix.shape[0] // PIECES
    order = [(at + PIECES // 2) % PIECES * piece for at in range(PIECES)]
    pairs = [(state, now), (load, mine)]
    pairs += [(matrix.at[pl.ds(at, piece)], rows.at[pl.ds(at, piece)]) for at in order]
    pairs.append((basis_across, basis))
    copies = [pltpu.make_async_copy(a, b, sems.at[i]) for i, (a, b) in enumerate(pairs)]
    for copy in copies:
        copy.start()
    first = 2 + PIECES // 2
    for copy in copies[:first]:
        copy.wait()
    waiting = copies[first:]
    for channel, send in zip(chans, sends):
        if channel[0] == "sub":
            while waiting:
                waiting.pop(0).wait()
        own = own_rows(channel)
        send[0 : channel[3]] = mine[own].astype(jnp.float32) - product(rows[own], now[...])
    ncl = basis.shape[0]
    for channel, send in zip(chans, sends):
        for block, columns, _ in row_blocks(channel):
            at = channel[3] + block * ncl
            send[at : at + ncl] = basis[:, columns].astype(jnp.float32)


def smooth(chans, far, matrix, weights, parts, gots, weighted, sends, correction=None):
    for at, (channel, part, got) in enumerate(zip(chans, parts, gots)):
        own = own_rows(channel)
        resid = part[0 : channel[3]] + across(channel, got)
        if correction is not None:
            resid -= correction(at, own)
        weighted[own] = (weights[own] * resid).astype(jnp.bfloat16)
    smoothing_near(far, matrix, weights, weighted, sends)


def smoothing_near(chans, matrix, weights, weighted, sends):
    for channel, send in zip(chans, sends):
        own = own_rows(channel)
        send[...] = weights[own] * product(matrix[own], weighted[...])


def smoothing_first(chans, far, matrix, weights, *refs):
    count = len(chans)
    parts, gots = refs[:count], refs[count : 2 * count]
    smooth(chans, far, matrix, weights, parts, gots, refs[2 * count], refs[2 * count + 1 :])


def smoothing_far(chans, far, ncl, matrix, weights, ahead, spread, reach, *refs):
    values, refs = value_refs(chans, ncl, refs)
    count = len(chans)
    parts, gots = refs[:count], refs[count : 2 * count]
    state, weighted, sends = refs[2 * count], refs[2 * count + 1], refs[2 * count + 2 :]
    here = values.around()

    def correction(at, own):
        pair = jnp.concatenate([here[0], values.at(at)], axis=0)
        state[own] = (ahead[own] + product(spread[own], split(pair, 0))).astype(state.dtype)
        both = jnp.concatenate(here + values.around(at), axis=0)
        return product(reach[own], split(both, 0))

    smooth(chans, far, matrix, weights, parts, gots, weighted, sends, correction)


def smoothing_sub(near, matrix, weights, weighted, basis_across, *refs):
    inverse = refs[: -len(near) - 1]
    coarse, sends = refs[-len(near) - 1], refs[-len(near) :]
    ncl = basis_across.shape[0]
    coarse[0:ncl] = product(basis_across[...], weighted[...])
    for rows in inverse:
        padded = rows.shape[0] + -rows.shape[0] % 8
        coarse[ncl:] = jnp.zeros((coarse.shape[0] - ncl, coarse.shape[1]), jnp.float32)
        for at in range(0, rows.shape[1], LANES):
            start = ncl + at // LANES * padded
            columns = min(LANES, rows.shape[1] - at)
            coarse[start : start + rows.shape[0], 0:columns] = rows[:, at : at + columns]
    smoothing_near(near, matrix, weights, weighted, sends)


def spreading(chans, weights, basis_across, *refs):
    gots, thin, full = refs[:-2], refs[-2], refs[-1]
    ncl = basis_across.shape[0]
    width = full.shape[1] // 2
    for at, (channel, got) in enumerate(zip(chans, gots)):
        for _, own, block in row_blocks(channel):
            from_row = channel[3] + block * ncl
            weight = weights[own][:, 0:ncl]
            here = weight * basis_across[:, own].astype(jnp.float32).T
            there = (1.0 - weight) * got[from_row : from_row + ncl].T
            thin[own] = thrice(jnp.concatenate([here, there], axis=1))
            before = [jnp.zeros((LANES, at * ncl), jnp.float32)] if at else []
            behind = jnp.zeros((LANES, width - (at + 2) * ncl), jnp.float32)
            placed = jnp.concatenate([here, *before, there, behind], axis=1)
            high = placed.astype(jnp.bfloat16)
            full[own, 0:width] = high
            full[own, width:] = (placed - high.astype(jnp.float32)).astype(jnp.bfloat16)


def responding(matrix, full, out, turned):
    width = out.shape[1]
    both = product(matrix[...], full[...])
    out[...] = both[:, 0:width] + both[:, width:]
    for at in range(0, out.shape[0], LANES):
        turned[:, at : at + LANES] = out[at : at + LANES].T


def reaching(chans, count, response, *refs):
    gots, out = refs[:-1], refs[-1]
    for channel, got in zip(chans, gots):
        for _, own, block in row_blocks(channel):
            at = channel[3] + block * count
            theirs = got[at : at + count].T
            out[own] = thrice(jnp.concatenate([response[own][:, 0:count], theirs], axis=1))


def joining(first, second, out):
    out[...] = jnp.concatenate([first[...], second[...]], axis=0)


def coarse_first(chans, order, sub, ncl, numbers, kept, got, out, values, *scratch):
    arranged, upright, relative, pieces = scratch
    index = lax.axis_index("sub")
    rows_of = order // sub
    padded = rows_of + -rows_of % 8
    stride = kept.shape[0] * 2 // sub
    upright[...] = jnp.broadcast_to(numbers[...].astype(jnp.float32), (8, numbers.shape[1])).T
    for block, origin in enumerate(origins(sub)):
        origin = jnp.bitwise_xor(index, origin)
        half = sub // 2
        source = kept if block < half else got
        at = (block % half) * stride
        pieces[block * ncl : (block + 1) * ncl] = source[at : at + ncl]
        to = pl.ds(pl.multiple_of(origin * padded, 8), padded)
        for tile in range(arranged.shape[1] // LANES):
            start = at + ncl + tile * padded
            arranged[to, tile * LANES : (tile + 1) * LANES] = source[start : start + padded]
        relative[block * ncl : (block + 1) * ncl] = upright[pl.ds(pl.multiple_of(origin * ncl, 8), ncl)]
    wanted = []
    for path in near_order(chans):
        place = index
        for c in path:
            place = mate(chans[c][1], place, sub)
        wanted.append(upright[pl.ds(pl.multiple_of(place * ncl, 8), ncl)])
    wanted = jnp.concatenate(wanted, axis=0)[:, 0:1].astype(jnp.int32)
    lane = lax.broadcasted_iota(jnp.int32, (wanted.shape[0], sub * padded), 1)
    inside = lane % padded
    held = jnp.where(inside < rows_of, (lane // padded) * rows_of + inside, -1)
    pick = jnp.where(wanted == held, 1.0, 0.0).astype(jnp.float32)
    chosen = jnp.dot(pick, arranged[...], precision=HIGHEST, preferred_element_type=jnp.float32)
    column = lax.broadcasted_iota(jnp.int32, (relative.shape[0], arranged.shape[1]), 1)
    place = jnp.where(relative[...][:, 0:1].astype(jnp.int32) == column, 1.0, 0.0).astype(jnp.float32)
    out[...] = lax.dot_general(
        chosen, place, (((1,), (1,)), ((), ())), precision=HIGHEST, preferred_element_type=jnp.float32
    )
    values[...] = jnp.dot(out[...], pieces[...], precision=HIGHEST, preferred_element_type=jnp.float32)


def coarse_values(mapping, kept, got, out):
    half = kept.shape[0]
    total = jnp.dot(mapping[:, 0:half], kept[...], precision=HIGHEST, preferred_element_type=jnp.float32)
    total += jnp.dot(mapping[:, half:], got[...], precision=HIGHEST, preferred_element_type=jnp.float32)
    out[...] = total


def between(chans, count, matrix, load, state, *refs):
    size = len(chans)
    parts, gots = refs[:size], refs[size : 2 * size]
    response = refs[2 * size : -size - 2]
    ahead, rounded, sends = refs[-size - 2], refs[-size - 1], refs[-size:]
    for channel, part, got in zip(chans, parts, gots):
        own = own_rows(channel)
        ahead[own] = state[own].astype(jnp.float32) + part[...] + across(channel, got)
        rounded[own] = ahead[own].astype(rounded.dtype)
    for channel, send in zip(chans, sends):
        rows = channel[3]
        own = own_rows(channel)
        send[0:rows] = load[own].astype(jnp.float32) - product(matrix[own], rounded[...])
        for turned in response:
            for block, columns, _ in row_blocks(channel):
                send[rows + block * count : rows + (block + 1) * count] = turned[0:count, columns]


def closing(chans, ncl, state, spread, *refs):
    values, refs = value_refs(chans, ncl, refs)
    count = len(chans)
    parts, gots, out = refs[:count], refs[count : 2 * count], refs[2 * count]
    for at, (channel, part, got) in enumerate(zip(chans, parts, gots)):
        own = own_rows(channel)
        pair = jnp.concatenate([values.at(), values.at(at)], axis=0)
        update = product(spread[own], split(pair, 0)) + part[...] + across(channel, got)
        out[own] = (state[own].astype(jnp.float32) + update).astype(out.dtype)


def steps(sub):
    found, step = [], sub // 2
    while step:
        found.append(step)
        step //= 2
    return found


def origins(sub):
    found = [0]
    for step in steps(sub):
        found += [origin ^ step for origin in found]
    return found


def gathered(piece, sub, hold=()):
    got = None
    for at, step in enumerate(steps(sub)):
        if got is not None and hold and at == len(steps(sub)) // 2:
            joined = jax.ShapeDtypeStruct((2 * piece.shape[0], piece.shape[1]), piece.dtype)
            piece = call(joining, joined, (piece, got), after=hold)
        elif got is not None:
            piece = jnp.concatenate([piece, got], axis=0)
        got = lax.ppermute(piece, "sub", [(i, i ^ step) for i in range(sub)])
    return piece, got


def shards(
    schur_t, neumann_t, face_weights, coarse_basis, coarse_inverse, coarse_number, loads, iterate
):
    schur, neumann = schur_t[0, 0], neumann_t[0, 0]
    basis_across = coarse_basis[0, 0].T
    load, state = loads[0, 0], iterate[0, 0]
    iface, columns = state.shape
    ncl = basis_across.shape[0]
    face = iface // 4
    grp, sub = lax.axis_size("grp"), lax.axis_size("sub")
    chans = channels(grp, sub, face)
    far = tuple(c for c in chans if c[0] == "grp")
    near = chans[len(far) :]
    around = (len(chans) + 1) * ncl
    order = coarse_inverse.shape[2]

    def wide(rows, width=columns):
        return jax.ShapeDtypeStruct((rows, width), jnp.float32)

    def short(rows, width=columns):
        return jax.ShapeDtypeStruct((rows, width), jnp.bfloat16)

    far_plain, near_plain = [tuple(wide(c[3]) for c in group) for group in (far, near)]
    half = short(iface)
    flops = iface * iface * columns

    parts = call(
        functools.partial(opening, chans),
        tuple(wide(c[3] + c[3] // LANES * ncl) for c in chans),
        (schur, load, state, basis_across),
        scratch=(
            pltpu.VMEM(schur.shape, schur.dtype),
            pltpu.VMEM(load.shape, load.dtype),
            pltpu.VMEM(state.shape, state.dtype),
            pltpu.VMEM(basis_across.shape, basis_across.dtype),
            pltpu.SemaphoreType.DMA((3 + PIECES,)),
        ),
        flops=2 * flops,
        away=4,
        grant=56 * MIB,
    )
    gots = exchange(chans, parts)

    weights = jnp.broadcast_to(face_weights[0, 0][:, None], (iface, columns))
    rows_of = coarse_inverse.shape[1]
    tiles = (order + -order % LANES) // LANES
    inverse_rows = (rows_of + -rows_of % 8) * tiles
    mapping = None

    def coarse_step(coarse, mapping, hold=(), after=()):
        rows = len(near_order(chans)) * ncl
        kept, got = gathered(coarse, sub, hold)
        if mapping is None:
            mapping, own = call(
                functools.partial(coarse_first, chans, order, sub, ncl),
                (wide(rows, sub * ncl), wide(rows)),
                (coarse_number, kept, got),
                scratch=(
                    pltpu.VMEM((inverse_rows // tiles * sub, tiles * LANES), jnp.float32),
                    pltpu.VMEM((sub * ncl, 8), jnp.float32),
                    pltpu.VMEM((sub * ncl, 8), jnp.float32),
                    pltpu.VMEM((sub * ncl, columns), jnp.float32),
                ),
                after=after,
            )
        else:
            own = call(coarse_values, wide(rows), (mapping, kept, got), after=after)
        known = own[0 : (1 + len(near)) * ncl]
        theirs = [swap(known, channel) for channel in far]
        beyond = []
        if len(far) > 1:
            beyond = [swap(theirs[1 - at][0:ncl], channel) for at, channel in enumerate(far)]
        return mapping, (own, *theirs, *beyond)

    for step in range(ITERS):
        if step == 0:
            weighted, *far_scaled = call(
                functools.partial(smoothing_first, chans, far),
                (half,) + far_plain,
                (neumann, weights, *parts, *gots),
                flops=flops,
            )
        else:
            mapping, values = coarse_step(coarse, mapping, hold=parts[:1], after=gots[len(far) :])
            if step == 1:
                reach = call(
                    functools.partial(reaching, chans, around),
                    short(iface, 6 * around),
                    (response, *gots),
                )
            state, weighted, *far_scaled = call(
                functools.partial(smoothing_far, chans, far, ncl),
                (half, half) + far_plain,
                (neumann, weights, ahead, spread, reach, *values, *parts, *gots),
                flops=flops,
            )
        inverse = (coarse_inverse[0],) if step == 0 else ()
        coarse, *near_scaled = call(
            functools.partial(smoothing_sub, near),
            (wide(ncl + len(inverse) * inverse_rows),) + near_plain,
            (neumann, weights, weighted, basis_across, *inverse),
            flops=flops,
        )
        scaled = (*far_scaled, *near_scaled)
        scaled_gots = exchange(chans, scaled)
        behind, behind_rows = (), 0
        if step == 0:
            width = around + -around % LANES
            spread, full = call(
                functools.partial(spreading, chans),
                (short(iface, 6 * ncl), short(iface, 2 * width)),
                (weights, basis_across, *gots),
                after=near_scaled[:1],
            )
            response, turned = call(
                responding, (wide(iface, width), wide(width, iface)), (schur, full), flops=2 * flops
            )
            behind, behind_rows = (turned,), around
        if step + 1 < ITERS:
            ahead, rounded, *parts = call(
                functools.partial(between, chans, around),
                (wide(iface), half) + tuple(wide(c[3] + c[3] // LANES * behind_rows) for c in chans),
                (schur, load, state, *scaled, *scaled_gots, *behind),
                flops=2 * flops,
            )
            gots = exchange(chans, parts)
    mapping, values = coarse_step(coarse, mapping, after=scaled_gots)
    out = call(
        functools.partial(closing, chans, ncl),
        half,
        (state, spread, *values, *scaled, *scaled_gots),
    )
    return out[None, None]


def solution(mesh):
    return jax.shard_map(
        shards,
        mesh=mesh,
        in_specs=(
            P("grp", "sub", None, None),
            P("grp", "sub", None, None),
            P("grp", "sub", None),
            P("grp", "sub", None, None),
            P("grp", "sub", None),
            P("grp", None),
            P("grp", "sub", None, None),
            P("grp", "sub", None, None),
        ),
        out_specs=P("grp", "sub", None, None),
        check_vma=False,
    )
```

```python
import functools

import jax
import jax.numpy as jnp
from jax import lax
from jax.experimental import pallas as pl
from jax.experimental.pallas import tpu as pltpu
from jax.sharding import PartitionSpec as P

ITERS = 3
HIGHEST = lax.Precision.HIGHEST
EVEN, ODD, BOTH = range(3)
LANES = 128
PIECES = 8
WEIGHT = 4 * 10**9
MIB = 2**20
WHOLE = pl.BlockSpec(memory_space=pltpu.VMEM)
AWAY = pl.BlockSpec(memory_space=pltpu.HBM)
ANYWHERE = pl.BlockSpec(memory_space=pl.ANY)


def channels(grp, sub, face):
    found = []
    for axis, devices, base in (("grp", grp, 2 * face), ("sub", sub, 0)):
        if devices == 2:
            found.append((axis, BOTH, base, 2 * face))
        else:
            found += [(axis, ODD, base, face), (axis, EVEN, base, face)]
    return tuple(found)


def mate(kind, index, devices):
    if kind == BOTH:
        return 1 - index
    step = 1 - 2 * (index % 2)
    if kind == ODD:
        step = -step
    return (index + step + devices) % devices


def swap(array, channel):
    axis, kind = channel[:2]
    devices = lax.axis_size(axis)
    return lax.ppermute(array, axis, [(i, mate(kind, i, devices)) for i in range(devices)])


def exchange(chans, sends):
    return tuple(swap(send, channel) for channel, send in zip(chans, sends))


def first_row(channel):
    axis, kind, base, rows = channel
    if kind == BOTH:
        return base
    odd = lax.rem(lax.axis_index(axis), 2)
    return pl.multiple_of(base + (odd if kind == ODD else 1 - odd) * rows, rows)


def own_rows(channel):
    return pl.ds(first_row(channel), channel[3])


def row_blocks(channel):
    blocks = channel[3] // LANES
    for block in range(blocks):
        rows = pl.ds(pl.multiple_of(first_row(channel) + block * LANES, LANES), LANES)
        yield block, rows, (block + blocks // 2) % blocks if channel[1] == BOTH else block


def across(channel, got):
    rows = channel[3]
    if channel[1] == BOTH:
        return jnp.concatenate([got[rows // 2 : rows], got[0 : rows // 2]], axis=0)
    return got[0:rows]


def product(a, b):
    return jnp.dot(a, b, preferred_element_type=jnp.float32)


def split(values, axis):
    high = values.astype(jnp.bfloat16)
    low = (values - high.astype(jnp.float32)).astype(jnp.bfloat16)
    return jnp.concatenate([high, low, high], axis=axis)


def thrice(values):
    high = values.astype(jnp.bfloat16).astype(jnp.float32)
    return jnp.concatenate([high, high, values - high], axis=1).astype(jnp.bfloat16)


def call(body, outs, args, scratch=(), flops=0, away=0, after=(), grant=16 * MIB):
    moved = sum(a.size * a.dtype.itemsize for a in args)
    ahead = len(after)
    return pl.pallas_call(
        lambda *refs: body(*refs[ahead:]),
        out_shape=outs,
        in_specs=[ANYWHERE] * ahead + [AWAY] * away + [WHOLE] * (len(args) - away),
        out_specs=jax.tree.map(lambda _: WHOLE, outs),
        scratch_shapes=scratch,
        cost_estimate=pl.CostEstimate(flops=flops, bytes_accessed=moved, transcendentals=0),
        compiler_params=pltpu.CompilerParams(vmem_limit_bytes=grant),
    )(*after, *args)


class Values:
    def __init__(self, chans, ncl, near, far, second):
        self.chans, self.ncl = chans, ncl
        self.near, self.far, self.second = near, far, second
        self.order = near_order(chans)

    def at(self, *path):
        grp = [c for c in path if self.chans[c][0] == "grp"]
        sub = [c for c in path if self.chans[c][0] == "sub"]
        grp, sub = [[] if len(p) == 2 and p[0] == p[1] else p for p in (grp, sub)]
        if len(grp) == 2:
            return self.second[grp[0]][...]
        source = self.far[grp[0]] if grp else self.near
        place = self.order.index(tuple(sub)) * self.ncl
        return source[place : place + self.ncl]

    def around(self, *path):
        return [self.at(*path)] + [self.at(*path, c) for c in range(len(self.chans))]


def near_order(chans):
    kinds = [c for c, channel in enumerate(chans) if channel[0] == "sub"]
    return [()] + [(c,) for c in kinds] + [(c, d) for c in kinds for d in kinds if c != d]


def value_refs(chans, ncl, refs):
    far = sum(channel[0] == "grp" for channel in chans)
    second = far if far > 1 else 0
    values = Values(chans, ncl, refs[0], refs[1 : 1 + far], refs[1 + far : 1 + far + second])
    return values, refs[1 + far + second :]


def opening(chans, matrix, load, state, basis_across, *refs):
    sends, (rows, mine, now, basis, sems) = refs[:-5], refs[-5:]
    piece = matrix.shape[0] // PIECES
    order = [(at + PIECES // 2) % PIECES * piece for at in range(PIECES)]
    pairs = [(state, now), (load, mine)]
    pairs += [(matrix.at[pl.ds(at, piece)], rows.at[pl.ds(at, piece)]) for at in order]
    pairs.append((basis_across, basis))
    copies = [pltpu.make_async_copy(a, b, sems.at[i]) for i, (a, b) in enumerate(pairs)]
    for copy in copies:
        copy.start()
    first = 2 + PIECES // 2
    for copy in copies[:first]:
        copy.wait()
    waiting = copies[first:]
    for channel, send in zip(chans, sends):
        if channel[0] == "sub":
            while waiting:
                waiting.pop(0).wait()
        own = own_rows(channel)
        send[0 : channel[3]] = mine[own].astype(jnp.float32) - product(rows[own], now[...])
    ncl = basis.shape[0]
    for channel, send in zip(chans, sends):
        for block, columns, _ in row_blocks(channel):
            at = channel[3] + block * ncl
            send[at : at + ncl] = basis[:, columns].astype(jnp.float32)


def smooth(chans, far, matrix, weights, resid_on, weighted, sends):
    for at, channel in enumerate(chans):
        own = own_rows(channel)
        weighted[own] = (weights[own] * resid_on(at, own)).astype(jnp.bfloat16)
    smoothing_near(far, matrix, weights, weighted, sends)


def smoothing_near(chans, matrix, weights, weighted, sends):
    for channel, send in zip(chans, sends):
        own = own_rows(channel)
        send[...] = weights[own] * product(matrix[own], weighted[...])


def stash(*refs):
    count = len(refs) // 2
    for part, out in zip(refs[:count], refs[count:]):
        out[...] = part[0 : out.shape[0]]


def summing(chans, *refs):
    count = len(chans)
    parts, gots, out = refs[:count], refs[count : 2 * count], refs[2 * count]
    for channel, part, got in zip(chans, parts, gots):
        out[own_rows(channel)] = part[0 : channel[3]] + across(channel, got)


def smoothing_first(chans, far, matrix, weights, *refs):
    count = len(chans)
    parts, gots = refs[:count], refs[count : 2 * count]

    def resid_on(at, own):
        return parts[at][...] + across(chans[at], gots[at])

    smooth(chans, far, matrix, weights, resid_on, refs[2 * count], refs[2 * count + 1 :])


def smoothing_far(chans, far, ncl, matrix, weights, ahead, spread, reach, summed, *refs):
    values, refs = value_refs(chans, ncl, refs)
    state, weighted, sends = refs[0], refs[1], refs[2:]
    here = values.around()

    def resid_on(at, own):
        pair = jnp.concatenate([here[0], values.at(at)], axis=0)
        state[own] = (ahead[own] + product(spread[own], split(pair, 0))).astype(state.dtype)
        both = jnp.concatenate(here + values.around(at), axis=0)
        return summed[own] - product(reach[own], split(both, 0))

    smooth(chans, far, matrix, weights, resid_on, weighted, sends)


def smoothing_sub(near, matrix, weights, weighted, basis_across, *refs):
    inverse = refs[: -len(near) - 1]
    coarse, sends = refs[-len(near) - 1], refs[-len(near) :]
    ncl = basis_across.shape[0]
    coarse[0:ncl] = product(basis_across[...], weighted[...])
    for rows in inverse:
        padded = rows.shape[0] + -rows.shape[0] % 8
        coarse[ncl:] = jnp.zeros((coarse.shape[0] - ncl, coarse.shape[1]), jnp.float32)
        for at in range(0, rows.shape[1], LANES):
            start = ncl + at // LANES * padded
            columns = min(LANES, rows.shape[1] - at)
            coarse[start : start + rows.shape[0], 0:columns] = rows[:, at : at + columns]
    smoothing_near(near, matrix, weights, weighted, sends)


def spreading(chans, weights, basis_across, *refs):
    gots, thin, full = refs[:-2], refs[-2], refs[-1]
    ncl = basis_across.shape[0]
    width = full.shape[1] // 2
    for at, (channel, got) in enumerate(zip(chans, gots)):
        for _, own, block in row_blocks(channel):
            from_row = channel[3] + block * ncl
            weight = weights[own][:, 0:ncl]
            here = weight * basis_across[:, own].astype(jnp.float32).T
            there = (1.0 - weight) * got[from_row : from_row + ncl].T
            thin[own] = thrice(jnp.concatenate([here, there], axis=1))
            before = [jnp.zeros((LANES, at * ncl), jnp.float32)] if at else []
            behind = jnp.zeros((LANES, width - (at + 2) * ncl), jnp.float32)
            placed = jnp.concatenate([here, *before, there, behind], axis=1)
            high = placed.astype(jnp.bfloat16)
            full[own, 0:width] = high
            full[own, width:] = (placed - high.astype(jnp.float32)).astype(jnp.bfloat16)


def responding(matrix, full, out, turned):
    width = out.shape[1]
    both = product(matrix[...], full[...])
    out[...] = both[:, 0:width] + both[:, width:]
    for at in range(0, out.shape[0], LANES):
        turned[:, at : at + LANES] = out[at : at + LANES].T


def reaching(chans, count, response, *refs):
    gots, out = refs[:-1], refs[-1]
    for channel, got in zip(chans, gots):
        for _, own, block in row_blocks(channel):
            at = channel[3] + block * count
            theirs = got[at : at + count].T
            out[own] = thrice(jnp.concatenate([response[own][:, 0:count], theirs], axis=1))


def joining(first, second, out):
    out[...] = jnp.concatenate([first[...], second[...]], axis=0)


def coarse_first(chans, order, sub, ncl, numbers, kept, got, out, values, *scratch):
    arranged, upright, relative, pieces = scratch
    index = lax.axis_index("sub")
    rows_of = order // sub
    padded = rows_of + -rows_of % 8
    stride = kept.shape[0] * 2 // sub
    upright[...] = jnp.broadcast_to(numbers[...].astype(jnp.float32), (8, numbers.shape[1])).T
    for block, origin in enumerate(origins(sub)):
        origin = jnp.bitwise_xor(index, origin)
        half = sub // 2
        source = kept if block < half else got
        at = (block % half) * stride
        pieces[block * ncl : (block + 1) * ncl] = source[at : at + ncl]
        to = pl.ds(pl.multiple_of(origin * padded, 8), padded)
        for tile in range(arranged.shape[1] // LANES):
            start = at + ncl + tile * padded
            arranged[to, tile * LANES : (tile + 1) * LANES] = source[start : start + padded]
        relative[block * ncl : (block + 1) * ncl] = upright[pl.ds(pl.multiple_of(origin * ncl, 8), ncl)]
    wanted = []
    for path in near_order(chans):
        place = index
        for c in path:
            place = mate(chans[c][1], place, sub)
        wanted.append(upright[pl.ds(pl.multiple_of(place * ncl, 8), ncl)])
    wanted = jnp.concatenate(wanted, axis=0)[:, 0:1].astype(jnp.int32)
    lane = lax.broadcasted_iota(jnp.int32, (wanted.shape[0], sub * padded), 1)
    inside = lane % padded
    held = jnp.where(inside < rows_of, (lane // padded) * rows_of + inside, -1)
    pick = jnp.where(wanted == held, 1.0, 0.0).astype(jnp.float32)
    chosen = jnp.dot(pick, arranged[...], precision=HIGHEST, preferred_element_type=jnp.float32)
    column = lax.broadcasted_iota(jnp.int32, (relative.shape[0], arranged.shape[1]), 1)
    place = jnp.where(relative[...][:, 0:1].astype(jnp.int32) == column, 1.0, 0.0).astype(jnp.float32)
    out[...] = lax.dot_general(
        chosen, place, (((1,), (1,)), ((), ())), precision=HIGHEST, preferred_element_type=jnp.float32
    )
    values[...] = jnp.dot(out[...], pieces[...], precision=HIGHEST, preferred_element_type=jnp.float32)


def coarse_values(mapping, kept, got, out):
    half = kept.shape[0]
    total = jnp.dot(mapping[:, 0:half], kept[...], precision=HIGHEST, preferred_element_type=jnp.float32)
    total += jnp.dot(mapping[:, half:], got[...], precision=HIGHEST, preferred_element_type=jnp.float32)
    out[...] = total


def between(chans, count, matrix, load, state, *refs):
    size = len(chans)
    parts, gots = refs[:size], refs[size : 2 * size]
    response = refs[2 * size : -size - 2]
    ahead, rounded, sends = refs[-size - 2], refs[-size - 1], refs[-size:]
    for channel, part, got in zip(chans, parts, gots):
        own = own_rows(channel)
        ahead[own] = state[own].astype(jnp.float32) + part[...] + across(channel, got)
        rounded[own] = ahead[own].astype(rounded.dtype)
    for channel, send in zip(chans, sends):
        rows = channel[3]
        own = own_rows(channel)
        send[0:rows] = load[own].astype(jnp.float32) - product(matrix[own], rounded[...])
        for turned in response:
            for block, columns, _ in row_blocks(channel):
                send[rows + block * count : rows + (block + 1) * count] = turned[0:count, columns]


def closing(chans, ncl, state, spread, summed, *refs):
    values, refs = value_refs(chans, ncl, refs)
    out = refs[0]
    for at, channel in enumerate(chans):
        own = own_rows(channel)
        pair = jnp.concatenate([values.at(), values.at(at)], axis=0)
        update = product(spread[own], split(pair, 0)) + summed[own]
        out[own] = (state[own].astype(jnp.float32) + update).astype(out.dtype)


def steps(sub):
    found, step = [], sub // 2
    while step:
        found.append(step)
        step //= 2
    return found


def origins(sub):
    found = [0]
    for step in steps(sub):
        found += [origin ^ step for origin in found]
    return found


def gathered(piece, sub, hold=(), wide=False):
    def hop(move):
        return lax.ppermute(piece, "sub", [(i, i ^ move) for i in range(sub)])

    moves = steps(sub)
    if wide:
        first, second, *moves = moves
        pieces = [piece] + [hop(move) for move in (first, second, first ^ second)]
        piece = jnp.concatenate(pieces, axis=0)
    for at, move in enumerate(moves[:-1]):
        got = hop(move)
        if hold and at + 1 == len(moves) // 2:
            joined = jax.ShapeDtypeStruct((2 * piece.shape[0], piece.shape[1]), piece.dtype)
            piece = call(joining, joined, (piece, got), after=hold)
        else:
            piece = jnp.concatenate([piece, got], axis=0)
    return piece, hop(moves[-1])


def shards(
    schur_t, neumann_t, face_weights, coarse_basis, coarse_inverse, coarse_number, loads, iterate
):
    schur, neumann = schur_t[0, 0], neumann_t[0, 0]
    basis_across = coarse_basis[0, 0].T
    load, state = loads[0, 0], iterate[0, 0]
    iface, columns = state.shape
    ncl = basis_across.shape[0]
    face = iface // 4
    grp, sub = lax.axis_size("grp"), lax.axis_size("sub")
    chans = channels(grp, sub, face)
    far = tuple(c for c in chans if c[0] == "grp")
    near = chans[len(far) :]
    around = (len(chans) + 1) * ncl
    order = coarse_inverse.shape[2]

    def wide(rows, width=columns):
        return jax.ShapeDtypeStruct((rows, width), jnp.float32)

    def short(rows, width=columns):
        return jax.ShapeDtypeStruct((rows, width), jnp.bfloat16)

    far_plain, near_plain = [tuple(wide(c[3]) for c in group) for group in (far, near)]
    half = short(iface)
    flops = iface * iface * columns

    parts = call(
        functools.partial(opening, chans),
        tuple(wide(c[3] + c[3] // LANES * ncl) for c in chans),
        (schur, load, state, basis_across),
        scratch=(
            pltpu.VMEM(schur.shape, schur.dtype),
            pltpu.VMEM(load.shape, load.dtype),
            pltpu.VMEM(state.shape, state.dtype),
            pltpu.VMEM(basis_across.shape, basis_across.dtype),
            pltpu.SemaphoreType.DMA((3 + PIECES,)),
        ),
        flops=2 * flops,
        away=4,
        grant=56 * MIB,
    )
    gots = exchange(chans, parts)
    parts = call(stash, far_plain + near_plain, tuple(parts))

    weights = jnp.broadcast_to(face_weights[0, 0][:, None], (iface, columns))
    rows_of = coarse_inverse.shape[1]
    tiles = (order + -order % LANES) // LANES
    inverse_rows = (rows_of + -rows_of % 8) * tiles
    mapping = None

    def coarse_step(coarse, mapping, hold=(), after=()):
        rows = len(near_order(chans)) * ncl
        kept, got = gathered(coarse, sub, hold, wide=not hold)
        if mapping is None:
            mapping, own = call(
                functools.partial(coarse_first, chans, order, sub, ncl),
                (wide(rows, sub * ncl), wide(rows)),
                (coarse_number, kept, got),
                scratch=(
                    pltpu.VMEM((inverse_rows // tiles * sub, tiles * LANES), jnp.float32),
                    pltpu.VMEM((sub * ncl, 8), jnp.float32),
                    pltpu.VMEM((sub * ncl, 8), jnp.float32),
                    pltpu.VMEM((sub * ncl, columns), jnp.float32),
                ),
                after=after,
            )
        else:
            own = call(coarse_values, wide(rows), (mapping, kept, got), after=after)
        known = own[0 : (1 + len(near)) * ncl]
        theirs = [swap(known, channel) for channel in far]
        beyond = []
        if len(far) > 1:
            beyond = [swap(theirs[1 - at][0:ncl], channel) for at, channel in enumerate(far)]
        return mapping, (own, *theirs, *beyond)

    def sums(sent, got):
        return call(functools.partial(summing, chans), wide(iface), (*sent, *got), flops=WEIGHT)

    for step in range(ITERS):
        if step == 0:
            weighted, *far_scaled = call(
                functools.partial(smoothing_first, chans, far),
                (half,) + far_plain,
                (neumann, weights, *parts, *gots),
                flops=flops,
            )
        else:
            mapping, values = coarse_step(coarse, mapping, hold=parts[:1])
            if step == 1:
                reach = call(
                    functools.partial(reaching, chans, around),
                    short(iface, 6 * around),
                    (response, *gots),
                )
            state, weighted, *far_scaled = call(
                functools.partial(smoothing_far, chans, far, ncl),
                (half, half) + far_plain,
                (neumann, weights, ahead, spread, reach, sums(parts, gots), *values),
                flops=flops,
            )
        inverse = (coarse_inverse[0],) if step == 0 else ()
        coarse, *near_scaled = call(
            functools.partial(smoothing_sub, near),
            (wide(ncl + len(inverse) * inverse_rows),) + near_plain,
            (neumann, weights, weighted, basis_across, *inverse),
            flops=flops,
        )
        scaled = (*far_scaled, *near_scaled)
        scaled_gots = exchange(chans, scaled)
        behind, behind_rows = (), 0
        if step == 0:
            width = around + -around % LANES
            spread, full = call(
                functools.partial(spreading, chans),
                (short(iface, 6 * ncl), short(iface, 2 * width)),
                (weights, basis_across, *gots),
                after=near_scaled[:1],
            )
            response, turned = call(
                responding, (wide(iface, width), wide(width, iface)), (schur, full), flops=2 * flops
            )
            behind, behind_rows = (turned,), around
        if step + 1 < ITERS:
            ahead, rounded, *parts = call(
                functools.partial(between, chans, around),
                (wide(iface), half) + tuple(wide(c[3] + c[3] // LANES * behind_rows) for c in chans),
                (schur, load, state, *scaled, *scaled_gots, *behind),
                flops=2 * flops,
            )
            gots = exchange(chans, parts)
    mapping, values = coarse_step(coarse, mapping, after=scaled_gots[len(far) :])
    out = call(
        functools.partial(closing, chans, ncl),
        half,
        (state, spread, sums(scaled, scaled_gots), *values),
    )
    return out[None, None]


def solution(mesh):
    return jax.shard_map(
        shards,
        mesh=mesh,
        in_specs=(
            P("grp", "sub", None, None),
            P("grp", "sub", None, None),
            P("grp", "sub", None),
            P("grp", "sub", None, None),
            P("grp", "sub", None),
            P("grp", None),
            P("grp", "sub", None, None),
            P("grp", "sub", None, None),
        ),
        out_specs=P("grp", "sub", None, None),
        check_vma=False,
    )
```

```python
import functools

import jax
import jax.numpy as jnp
from jax import lax
from jax.experimental import pallas as pl
from jax.experimental.pallas import tpu as pltpu
from jax.sharding import PartitionSpec as P

ITERS = 3
HIGHEST = lax.Precision.HIGHEST
EVEN, ODD, BOTH = range(3)
LANES = 128
PIECES = 8
WEIGHT = 4 * 10**9
MIB = 2**20
WHOLE = pl.BlockSpec(memory_space=pltpu.VMEM)
AWAY = pl.BlockSpec(memory_space=pltpu.HBM)
ANYWHERE = pl.BlockSpec(memory_space=pl.ANY)


def channels(grp, sub, face):
    found = []
    for axis, devices, base in (("grp", grp, 2 * face), ("sub", sub, 0)):
        if devices == 2:
            found.append((axis, BOTH, base, 2 * face))
        else:
            found += [(axis, ODD, base, face), (axis, EVEN, base, face)]
    return tuple(found)


def mate(kind, index, devices):
    if kind == BOTH:
        return 1 - index
    step = 1 - 2 * (index % 2)
    if kind == ODD:
        step = -step
    return (index + step + devices) % devices


def swap(array, channel):
    axis, kind = channel[:2]
    devices = lax.axis_size(axis)
    return lax.ppermute(array, axis, [(i, mate(kind, i, devices)) for i in range(devices)])


def exchange(chans, sends):
    return tuple(swap(send, channel) for channel, send in zip(chans, sends))


def first_row(channel):
    axis, kind, base, rows = channel
    if kind == BOTH:
        return base
    odd = lax.rem(lax.axis_index(axis), 2)
    return pl.multiple_of(base + (odd if kind == ODD else 1 - odd) * rows, rows)


def own_rows(channel):
    return pl.ds(first_row(channel), channel[3])


def row_blocks(channel):
    blocks = channel[3] // LANES
    for block in range(blocks):
        rows = pl.ds(pl.multiple_of(first_row(channel) + block * LANES, LANES), LANES)
        yield block, rows, (block + blocks // 2) % blocks if channel[1] == BOTH else block


def across(channel, got):
    rows = channel[3]
    if channel[1] == BOTH:
        return jnp.concatenate([got[rows // 2 : rows], got[0 : rows // 2]], axis=0)
    return got[0:rows]


def product(a, b):
    return jnp.dot(a, b, preferred_element_type=jnp.float32)


def split(values, axis):
    high = values.astype(jnp.bfloat16)
    low = (values - high.astype(jnp.float32)).astype(jnp.bfloat16)
    return jnp.concatenate([high, low, high], axis=axis)


def thrice(values):
    high = values.astype(jnp.bfloat16).astype(jnp.float32)
    return jnp.concatenate([high, high, values - high], axis=1).astype(jnp.bfloat16)


def call(body, outs, args, scratch=(), flops=0, away=0, after=(), grant=16 * MIB):
    moved = sum(a.size * a.dtype.itemsize for a in args)
    ahead = len(after)
    return pl.pallas_call(
        lambda *refs: body(*refs[ahead:]),
        out_shape=outs,
        in_specs=[ANYWHERE] * ahead + [AWAY] * away + [WHOLE] * (len(args) - away),
        out_specs=jax.tree.map(lambda _: WHOLE, outs),
        scratch_shapes=scratch,
        cost_estimate=pl.CostEstimate(flops=flops, bytes_accessed=moved, transcendentals=0),
        compiler_params=pltpu.CompilerParams(vmem_limit_bytes=grant),
    )(*after, *args)


class Values:
    def __init__(self, chans, ncl, near, far, second):
        self.chans, self.ncl = chans, ncl
        self.near, self.far, self.second = near, far, second
        self.order = near_order(chans)

    def at(self, *path):
        grp = [c for c in path if self.chans[c][0] == "grp"]
        sub = [c for c in path if self.chans[c][0] == "sub"]
        grp, sub = [[] if len(p) == 2 and p[0] == p[1] else p for p in (grp, sub)]
        if len(grp) == 2:
            return self.second[grp[0]][...]
        source = self.far[grp[0]] if grp else self.near
        place = self.order.index(tuple(sub)) * self.ncl
        return source[place : place + self.ncl]

    def around(self, *path):
        return [self.at(*path)] + [self.at(*path, c) for c in range(len(self.chans))]


def near_order(chans):
    kinds = [c for c, channel in enumerate(chans) if channel[0] == "sub"]
    return [()] + [(c,) for c in kinds] + [(c, d) for c in kinds for d in kinds if c != d]


def value_refs(chans, ncl, refs):
    far = sum(channel[0] == "grp" for channel in chans)
    second = far if far > 1 else 0
    values = Values(chans, ncl, refs[0], refs[1 : 1 + far], refs[1 + far : 1 + far + second])
    return values, refs[1 + far + second :]


def opening(chans, matrix, load, state, basis_across, *refs):
    count = len(chans)
    sends, basis_sends = refs[:count], refs[count : 2 * count]
    rows, mine, now, basis, sems = refs[2 * count :]
    piece = matrix.shape[0] // PIECES
    order = [(at + PIECES // 2) % PIECES * piece for at in range(PIECES)]
    pairs = [(state, now), (load, mine)]
    pairs += [(matrix.at[pl.ds(at, piece)], rows.at[pl.ds(at, piece)]) for at in order]
    pairs.append((basis_across, basis))
    copies = [pltpu.make_async_copy(a, b, sems.at[i]) for i, (a, b) in enumerate(pairs)]
    for copy in copies:
        copy.start()
    first = 2 + PIECES // 2
    for copy in copies[:first]:
        copy.wait()
    waiting = copies[first:]
    for channel, send in zip(chans, sends):
        if channel[0] == "sub":
            while waiting:
                waiting.pop(0).wait()
        part_on(channel, rows, mine, now, send)
    ncl = basis.shape[0]
    for channel, send in zip(chans, basis_sends):
        for block, columns, _ in row_blocks(channel):
            send[block * ncl : (block + 1) * ncl] = basis[:, columns].astype(jnp.float32)


def part_on(channel, matrix, load, state, send):
    own = own_rows(channel)
    send[...] = load[own].astype(jnp.float32) - product(matrix[own], state[...])


def stash(*refs):
    count = len(refs) // 2
    for part, out in zip(refs[:count], refs[count:]):
        out[...] = part[...]


def send_turned(channel, turned, send, count):
    for block, columns, _ in row_blocks(channel):
        at = channel[3] + block * count
        send[at : at + count] = turned[0:count, columns]


def smooth(chans, far, matrix, weights, resid_on, weighted, sends):
    for at, channel in enumerate(chans):
        own = own_rows(channel)
        weighted[own] = (weights[own] * resid_on(at, own)).astype(jnp.bfloat16)
    smoothing_near(far, matrix, weights, weighted, sends)


def smoothing_near(chans, matrix, weights, weighted, sends):
    for channel, send in zip(chans, sends):
        own = own_rows(channel)
        send[0 : channel[3]] = weights[own] * product(matrix[own], weighted[...])


def summing(chans, *refs):
    count = len(chans)
    parts, gots, out = refs[:count], refs[count : 2 * count], refs[2 * count]
    for channel, part, got in zip(chans, parts, gots):
        out[own_rows(channel)] = part[0 : channel[3]] + across(channel, got)


def smoothing_first(chans, far, count, matrix, weights, turned, *refs):
    size = len(chans)
    parts, gots = refs[:size], refs[size : 2 * size]
    weighted, sends = refs[2 * size], refs[2 * size + 1 :]

    def resid_on(at, own):
        return parts[at][...] + across(chans[at], gots[at])

    smooth(chans, far, matrix, weights, resid_on, weighted, sends)
    for channel, send in zip(far, sends):
        send_turned(channel, turned, send, count)


def smoothing_far(chans, far, ncl, matrix, weights, ahead, spread, reach, summed, *refs):
    values, refs = value_refs(chans, ncl, refs)
    state, weighted, sends = refs[0], refs[1], refs[2:]
    here = values.around()

    def resid_on(at, own):
        pair = jnp.concatenate([here[0], values.at(at)], axis=0)
        state[own] = (ahead[own] + product(spread[own], split(pair, 0))).astype(state.dtype)
        both = jnp.concatenate(here + values.around(at), axis=0)
        return summed[own] - product(reach[own], split(both, 0))

    smooth(chans, far, matrix, weights, resid_on, weighted, sends)


def restricting(basis_across, weighted, *refs):
    inverse, coarse = refs[:-1], refs[-1]
    ncl = basis_across.shape[0]
    coarse[0:ncl] = product(basis_across[...], weighted[...])
    for rows in inverse:
        padded = rows.shape[0] + -rows.shape[0] % 8
        coarse[ncl:] = jnp.zeros((coarse.shape[0] - ncl, coarse.shape[1]), jnp.float32)
        for at in range(0, rows.shape[1], LANES):
            start = ncl + at // LANES * padded
            columns = min(LANES, rows.shape[1] - at)
            coarse[start : start + rows.shape[0], 0:columns] = rows[:, at : at + columns]


def smoothing_sub(near, count, matrix, weights, weighted, *refs):
    turned, sends = refs[: -len(near)], refs[-len(near) :]
    smoothing_near(near, matrix, weights, weighted, sends)
    for array in turned:
        for channel, send in zip(near, sends):
            send_turned(channel, array, send, count)


def smoothing_both(near, count, matrix, weights, weighted, basis_across, *refs):
    extra, coarse, sends = refs[: -len(near) - 1], refs[-len(near) - 1], refs[-len(near) :]
    restricting(basis_across, weighted, *extra[:1], coarse)
    smoothing_sub(near, count, matrix, weights, weighted, *extra[1:], *sends)


def spreading(chans, weights, basis_across, *refs):
    gots, thin, full = refs[:-2], refs[-2], refs[-1]
    ncl = basis_across.shape[0]
    width = full.shape[1] // 2
    for at, (channel, got) in enumerate(zip(chans, gots)):
        for _, own, block in row_blocks(channel):
            from_row = block * ncl
            weight = weights[own][:, 0:ncl]
            here = weight * basis_across[:, own].astype(jnp.float32).T
            there = (1.0 - weight) * got[from_row : from_row + ncl].T
            thin[own] = thrice(jnp.concatenate([here, there], axis=1))
            before = [jnp.zeros((LANES, at * ncl), jnp.float32)] if at else []
            behind = jnp.zeros((LANES, width - (at + 2) * ncl), jnp.float32)
            placed = jnp.concatenate([here, *before, there, behind], axis=1)
            high = placed.astype(jnp.bfloat16)
            full[own, 0:width] = high
            full[own, width:] = (placed - high.astype(jnp.float32)).astype(jnp.bfloat16)


def responding(matrix, full, out, turned):
    width = out.shape[1]
    both = product(matrix[...], full[...])
    out[...] = both[:, 0:width] + both[:, width:]
    for at in range(0, out.shape[0], LANES):
        turned[:, at : at + LANES] = out[at : at + LANES].T


def reaching(chans, count, response, *refs):
    gots, out = refs[:-1], refs[-1]
    for channel, got in zip(chans, gots):
        for _, own, block in row_blocks(channel):
            at = channel[3] + block * count
            theirs = got[at : at + count].T
            out[own] = thrice(jnp.concatenate([response[own][:, 0:count], theirs], axis=1))


def joining(first, second, out):
    out[...] = jnp.concatenate([first[...], second[...]], axis=0)


def coarse_first(chans, order, sub, ncl, numbers, kept, got, out, values, *scratch):
    arranged, upright, relative, pieces = scratch
    index = lax.axis_index("sub")
    rows_of = order // sub
    padded = rows_of + -rows_of % 8
    stride = kept.shape[0] * 2 // sub
    upright[...] = jnp.broadcast_to(numbers[...].astype(jnp.float32), (8, numbers.shape[1])).T
    for block, origin in enumerate(origins(sub)):
        origin = jnp.bitwise_xor(index, origin)
        half = sub // 2
        source = kept if block < half else got
        at = (block % half) * stride
        pieces[block * ncl : (block + 1) * ncl] = source[at : at + ncl]
        to = pl.ds(pl.multiple_of(origin * padded, 8), padded)
        for tile in range(arranged.shape[1] // LANES):
            start = at + ncl + tile * padded
            arranged[to, tile * LANES : (tile + 1) * LANES] = source[start : start + padded]
        relative[block * ncl : (block + 1) * ncl] = upright[pl.ds(pl.multiple_of(origin * ncl, 8), ncl)]
    wanted = []
    for path in near_order(chans):
        place = index
        for c in path:
            place = mate(chans[c][1], place, sub)
        wanted.append(upright[pl.ds(pl.multiple_of(place * ncl, 8), ncl)])
    wanted = jnp.concatenate(wanted, axis=0)[:, 0:1].astype(jnp.int32)
    lane = lax.broadcasted_iota(jnp.int32, (wanted.shape[0], sub * padded), 1)
    inside = lane % padded
    held = jnp.where(inside < rows_of, (lane // padded) * rows_of + inside, -1)
    pick = jnp.where(wanted == held, 1.0, 0.0).astype(jnp.float32)
    chosen = jnp.dot(pick, arranged[...], precision=HIGHEST, preferred_element_type=jnp.float32)
    column = lax.broadcasted_iota(jnp.int32, (relative.shape[0], arranged.shape[1]), 1)
    place = jnp.where(relative[...][:, 0:1].astype(jnp.int32) == column, 1.0, 0.0).astype(jnp.float32)
    out[...] = lax.dot_general(
        chosen, place, (((1,), (1,)), ((), ())), precision=HIGHEST, preferred_element_type=jnp.float32
    )
    values[...] = jnp.dot(out[...], pieces[...], precision=HIGHEST, preferred_element_type=jnp.float32)


def coarse_values(mapping, kept, got, out):
    half = kept.shape[0]
    total = jnp.dot(mapping[:, 0:half], kept[...], precision=HIGHEST, preferred_element_type=jnp.float32)
    total += jnp.dot(mapping[:, half:], got[...], precision=HIGHEST, preferred_element_type=jnp.float32)
    out[...] = total


def between(chans, matrix, load, state, *refs):
    size = len(chans)
    parts, gots = refs[:size], refs[size : 2 * size]
    ahead, rounded, sends = refs[2 * size], refs[2 * size + 1], refs[2 * size + 2 :]
    for channel, part, got in zip(chans, parts, gots):
        own = own_rows(channel)
        ahead[own] = state[own].astype(jnp.float32) + part[0 : channel[3]] + across(channel, got)
        rounded[own] = ahead[own].astype(rounded.dtype)
    for channel, send in zip(chans, sends):
        part_on(channel, matrix, load, rounded, send)


def closing(chans, ncl, state, spread, summed, *refs):
    values, refs = value_refs(chans, ncl, refs)
    out = refs[0]
    for at, channel in enumerate(chans):
        own = own_rows(channel)
        pair = jnp.concatenate([values.at(), values.at(at)], axis=0)
        update = product(spread[own], split(pair, 0)) + summed[own]
        out[own] = (state[own].astype(jnp.float32) + update).astype(out.dtype)


def steps(sub):
    found, step = [], sub // 2
    while step:
        found.append(step)
        step //= 2
    return found


def origins(sub):
    found = [0]
    for step in steps(sub):
        found += [origin ^ step for origin in found]
    return found


def gathered(piece, sub, hold=(), wide=False):
    def hop(move):
        return lax.ppermute(piece, "sub", [(i, i ^ move) for i in range(sub)])

    moves = steps(sub)
    first = None
    if wide:
        one, two, *moves = moves
        piece = first = jnp.concatenate([piece] + [hop(move) for move in (one, two, one ^ two)], axis=0)
    for at, move in enumerate(moves[:-1]):
        got = hop(move)
        if hold and at + 1 == len(moves) // 2:
            joined = jax.ShapeDtypeStruct((2 * piece.shape[0], piece.shape[1]), piece.dtype)
            piece = call(joining, joined, (piece, got), after=hold)
        else:
            piece = jnp.concatenate([piece, got], axis=0)
    return (piece, hop(moves[-1])), first


def shards(
    schur_t, neumann_t, face_weights, coarse_basis, coarse_inverse, coarse_number, loads, iterate
):
    schur, neumann = schur_t[0, 0], neumann_t[0, 0]
    basis_across = coarse_basis[0, 0].T
    load, state = loads[0, 0], iterate[0, 0]
    iface, columns = state.shape
    ncl = basis_across.shape[0]
    face = iface // 4
    grp, sub = lax.axis_size("grp"), lax.axis_size("sub")
    chans = channels(grp, sub, face)
    far = tuple(c for c in chans if c[0] == "grp")
    near = chans[len(far) :]
    around = (len(chans) + 1) * ncl
    order = coarse_inverse.shape[2]

    def wide(rows, width=columns):
        return jax.ShapeDtypeStruct((rows, width), jnp.float32)

    def short(rows, width=columns):
        return jax.ShapeDtypeStruct((rows, width), jnp.bfloat16)

    far_plain, near_plain = [tuple(wide(c[3]) for c in group) for group in (far, near)]
    half = short(iface)
    flops = iface * iface * columns

    opened = call(
        functools.partial(opening, chans),
        far_plain + near_plain + tuple(wide(c[3] // LANES * ncl) for c in chans),
        (schur, load, state, basis_across),
        scratch=(
            pltpu.VMEM(schur.shape, schur.dtype),
            pltpu.VMEM(load.shape, load.dtype),
            pltpu.VMEM(state.shape, state.dtype),
            pltpu.VMEM(basis_across.shape, basis_across.dtype),
            pltpu.SemaphoreType.DMA((3 + PIECES,)),
        ),
        flops=2 * flops,
        away=4,
        grant=56 * MIB,
    )
    parts, basis_sends = opened[: len(chans)], opened[len(chans) :]
    gots = exchange(chans, parts)
    basis_gots = exchange(chans, basis_sends)
    parts = call(stash, far_plain + near_plain, tuple(parts))

    weights = jnp.broadcast_to(face_weights[0, 0][:, None], (iface, columns))
    width = around + -around % LANES
    spread, full = call(
        functools.partial(spreading, chans),
        (short(iface, 6 * ncl), short(iface, 2 * width)),
        (weights, basis_across, *basis_gots),
    )
    response, turned = call(
        responding, (wide(iface, width), wide(width, iface)), (schur, full), flops=2 * flops
    )
    tiles = (order + -order % LANES) // LANES
    rows_of = coarse_inverse.shape[1]
    behind_inverse = (rows_of + -rows_of % 8) * tiles

    def coarse_step(pieces, mapping, after=()):
        rows = len(near_order(chans)) * ncl
        if mapping is None:
            mapping, own = call(
                functools.partial(coarse_first, chans, order, sub, ncl),
                (wide(rows, sub * ncl), wide(rows)),
                (coarse_number, *pieces),
                scratch=(
                    pltpu.VMEM((behind_inverse // tiles * sub, tiles * LANES), jnp.float32),
                    pltpu.VMEM((sub * ncl, 8), jnp.float32),
                    pltpu.VMEM((sub * ncl, 8), jnp.float32),
                    pltpu.VMEM((sub * ncl, columns), jnp.float32),
                ),
                after=after,
            )
        else:
            own = call(coarse_values, wide(rows), (mapping, *pieces), after=after)
        known = own[0 : (1 + len(near)) * ncl]
        theirs = [swap(known, channel) for channel in far]
        beyond = []
        if len(far) > 1:
            beyond = [swap(theirs[1 - at][0:ncl], channel) for at, channel in enumerate(far)]
        return mapping, (own, *theirs, *beyond)

    def sums(sent, got):
        return call(functools.partial(summing, chans), wide(iface), (*sent, *got), flops=WEIGHT)

    for step in range(ITERS):
        start, last = step == 0, step + 1 == ITERS
        behind = around if start else 0
        far_outs, near_outs = [
            tuple(wide(c[3] + c[3] // LANES * behind) for c in group) for group in (far, near)
        ]
        if start:
            weighted, *far_scaled = call(
                functools.partial(smoothing_first, chans, far, around),
                (half,) + far_outs,
                (neumann, weights, turned, *parts, *gots),
                flops=flops,
            )
        else:
            pieces, _ = gathered(coarse, sub, hold=parts[:1])
            mapping, values = coarse_step(pieces, mapping if step > 1 else None)
            state, weighted, *far_scaled = call(
                functools.partial(smoothing_far, chans, far, ncl),
                (half, half) + far_outs,
                (neumann, weights, ahead, spread, reach, sums(parts, gots), *values),
                flops=flops,
            )
        if last:
            coarse = call(restricting, wide(ncl), (basis_across, weighted))
            pieces, first = gathered(coarse, sub, wide=True)
            near_scaled = call(
                functools.partial(smoothing_sub, near, around),
                near_outs,
                (neumann, weights, weighted),
                flops=flops,
                after=(first,),
            )
        else:
            coarse, *near_scaled = call(
                functools.partial(smoothing_both, near, around),
                (wide(ncl + behind_inverse * start),) + near_outs,
                (neumann, weights, weighted, basis_across) + ((coarse_inverse[0], turned) if start else ()),
                flops=flops,
            )
        scaled = (*far_scaled, *near_scaled)
        scaled_gots = exchange(chans, scaled)
        if start:
            reach = call(
                functools.partial(reaching, chans, around),
                short(iface, 6 * around),
                (response, *scaled_gots),
            )
        if not last:
            ahead, rounded, *parts = call(
                functools.partial(between, chans),
                (wide(iface), half) + far_plain + near_plain,
                (schur, load, state, *scaled, *scaled_gots),
                flops=2 * flops,
            )
            gots = exchange(chans, parts)
    _, values = coarse_step(pieces, mapping)
    out = call(
        functools.partial(closing, chans, ncl),
        half,
        (state, spread, sums(scaled, scaled_gots), *values),
    )
    return out[None, None]


def solution(mesh):
    return jax.shard_map(
        shards,
        mesh=mesh,
        in_specs=(
            P("grp", "sub", None, None),
            P("grp", "sub", None, None),
            P("grp", "sub", None),
            P("grp", "sub", None, None),
            P("grp", "sub", None),
            P("grp", None),
            P("grp", "sub", None, None),
            P("grp", "sub", None, None),
        ),
        out_specs=P("grp", "sub", None, None),
        check_vma=False,
    )
```

```python
import functools

import jax
import jax.numpy as jnp
from jax import lax
from jax.experimental import pallas as pl
from jax.experimental.pallas import tpu as pltpu
from jax.sharding import PartitionSpec as P

ITERS = 3
HIGHEST = lax.Precision.HIGHEST
EVEN, ODD, BOTH = range(3)
LANES = 128
PIECES = 8
WEIGHT = 4 * 10**9
MIB = 2**20
WHOLE = pl.BlockSpec(memory_space=pltpu.VMEM)
AWAY = pl.BlockSpec(memory_space=pltpu.HBM)
ANYWHERE = pl.BlockSpec(memory_space=pl.ANY)


def channels(grp, sub, face):
    found = []
    for axis, devices, base in (("grp", grp, 2 * face), ("sub", sub, 0)):
        if devices == 2:
            found.append((axis, BOTH, base, 2 * face))
        else:
            found += [(axis, ODD, base, face), (axis, EVEN, base, face)]
    return tuple(found)


def mate(kind, index, devices):
    if kind == BOTH:
        return 1 - index
    step = 1 - 2 * (index % 2)
    if kind == ODD:
        step = -step
    return (index + step + devices) % devices


def swap(array, channel):
    axis, kind = channel[:2]
    devices = lax.axis_size(axis)
    return lax.ppermute(array, axis, [(i, mate(kind, i, devices)) for i in range(devices)])


def exchange(chans, sends):
    return tuple(swap(send, channel) for channel, send in zip(chans, sends))


def first_row(channel):
    axis, kind, base, rows = channel
    if kind == BOTH:
        return base
    odd = lax.rem(lax.axis_index(axis), 2)
    return pl.multiple_of(base + (odd if kind == ODD else 1 - odd) * rows, rows)


def own_rows(channel):
    return pl.ds(first_row(channel), channel[3])


def row_blocks(channel):
    blocks = channel[3] // LANES
    for block in range(blocks):
        rows = pl.ds(pl.multiple_of(first_row(channel) + block * LANES, LANES), LANES)
        yield block, rows, (block + blocks // 2) % blocks if channel[1] == BOTH else block


def across(channel, got):
    rows = channel[3]
    if channel[1] == BOTH:
        return jnp.concatenate([got[rows // 2 : rows], got[0 : rows // 2]], axis=0)
    return got[0:rows]


def product(a, b):
    return jnp.dot(a, b, preferred_element_type=jnp.float32)


def split(values, axis):
    high = values.astype(jnp.bfloat16)
    low = (values - high.astype(jnp.float32)).astype(jnp.bfloat16)
    return jnp.concatenate([high, low, high], axis=axis)


def thrice(values):
    high = values.astype(jnp.bfloat16).astype(jnp.float32)
    return jnp.concatenate([high, high, values - high], axis=1).astype(jnp.bfloat16)


def call(body, outs, args, scratch=(), flops=0, away=0, after=(), grant=16 * MIB):
    moved = sum(a.size * a.dtype.itemsize for a in args)
    ahead = len(after)
    return pl.pallas_call(
        lambda *refs: body(*refs[ahead:]),
        out_shape=outs,
        in_specs=[ANYWHERE] * ahead + [AWAY] * away + [WHOLE] * (len(args) - away),
        out_specs=jax.tree.map(lambda _: WHOLE, outs),
        scratch_shapes=scratch,
        cost_estimate=pl.CostEstimate(flops=flops, bytes_accessed=moved, transcendentals=0),
        compiler_params=pltpu.CompilerParams(vmem_limit_bytes=grant),
    )(*after, *args)


class Values:
    def __init__(self, chans, ncl, near, far, second):
        self.chans, self.ncl = chans, ncl
        self.near, self.far, self.second = near, far, second
        self.order = near_order(chans)

    def at(self, *path):
        grp = [c for c in path if self.chans[c][0] == "grp"]
        sub = [c for c in path if self.chans[c][0] == "sub"]
        grp, sub = [[] if len(p) == 2 and p[0] == p[1] else p for p in (grp, sub)]
        if len(grp) == 2:
            return self.second[grp[0]][...]
        source = self.far[grp[0]] if grp else self.near
        place = self.order.index(tuple(sub)) * self.ncl
        return source[place : place + self.ncl]

    def around(self, *path):
        return [self.at(*path)] + [self.at(*path, c) for c in range(len(self.chans))]


def near_order(chans):
    kinds = [c for c, channel in enumerate(chans) if channel[0] == "sub"]
    return [()] + [(c,) for c in kinds] + [(c, d) for c in kinds for d in kinds if c != d]


def value_refs(chans, ncl, refs):
    far = sum(channel[0] == "grp" for channel in chans)
    second = far if far > 1 else 0
    values = Values(chans, ncl, refs[0], refs[1 : 1 + far], refs[1 + far : 1 + far + second])
    return values, refs[1 + far + second :]


def opening(chans, matrix, load, state, basis_across, *refs):
    sends, (rows, mine, now, basis, sems) = refs[:-5], refs[-5:]
    piece = matrix.shape[0] // PIECES
    order = [(at + PIECES // 2) % PIECES * piece for at in range(PIECES)]
    pairs = [(state, now), (load, mine)]
    pairs += [(matrix.at[pl.ds(at, piece)], rows.at[pl.ds(at, piece)]) for at in order]
    pairs.append((basis_across, basis))
    copies = [pltpu.make_async_copy(a, b, sems.at[i]) for i, (a, b) in enumerate(pairs)]
    for copy in copies:
        copy.start()
    first = 2 + PIECES // 2
    for copy in copies[:first]:
        copy.wait()
    waiting = copies[first:]
    for channel, send in zip(chans, sends):
        if channel[0] == "sub":
            while waiting:
                waiting.pop(0).wait()
        own = own_rows(channel)
        send[0 : channel[3]] = mine[own].astype(jnp.float32) - product(rows[own], now[...])
    ncl = basis.shape[0]
    for channel, send in zip(chans, sends):
        for block, columns, _ in row_blocks(channel):
            at = channel[3] + block * ncl
            send[at : at + ncl] = basis[:, columns].astype(jnp.float32)


def smooth(chans, weights, resid_on, weighted):
    for at, channel in enumerate(chans):
        own = own_rows(channel)
        weighted[own] = (weights[own] * resid_on(at, own)).astype(jnp.bfloat16)


def smoothing_near(chans, matrix, weights, weighted, sends):
    for channel, send in zip(chans, sends):
        own = own_rows(channel)
        send[...] = weights[own] * product(matrix[own], weighted[...])


def stash(*refs):
    count = len(refs) // 2
    for part, out in zip(refs[:count], refs[count:]):
        out[...] = part[0 : out.shape[0]]


def summing(chans, *refs):
    count = len(chans)
    parts, gots, out = refs[:count], refs[count : 2 * count], refs[2 * count]
    for channel, part, got in zip(chans, parts, gots):
        out[own_rows(channel)] = part[0 : channel[3]] + across(channel, got)


def smoothing_first(chans, far, matrix, weights, *refs):
    count = len(chans)
    parts, gots = refs[:count], refs[count : 2 * count]

    def resid_on(at, own):
        return parts[at][...] + across(chans[at], gots[at])

    smooth(chans, weights, resid_on, refs[2 * count])
    smoothing_near(far, matrix, weights, refs[2 * count], refs[2 * count + 1 :])


def correct(chans, ncl, weights, ahead, spread, summed, refs):
    reach = refs[: len(chans)]
    values, refs = value_refs(chans, ncl, refs[len(chans) :])
    state, weighted, rest = refs[0], refs[1], refs[2:]
    here = values.around()

    def resid_on(at, own):
        pair = jnp.concatenate([here[0], values.at(at)], axis=0)
        state[own] = (ahead[own] + product(spread[own], split(pair, 0))).astype(state.dtype)
        both = jnp.concatenate(here + values.around(at), axis=0)
        return summed[own] - product(reach[at][...], split(both, 0))

    smooth(chans, weights, resid_on, weighted)
    return weighted, rest


def smoothing_far(chans, far, ncl, matrix, weights, ahead, spread, summed, *refs):
    weighted, sends = correct(chans, ncl, weights, ahead, spread, summed, refs)
    smoothing_near(far, matrix, weights, weighted, sends)


def smoothing_last(chans, ncl, basis_across, weights, ahead, spread, summed, *refs):
    weighted, (coarse,) = correct(chans, ncl, weights, ahead, spread, summed, refs)
    coarse[...] = product(basis_across[...], weighted[...])


def smoothing_rows(chans, matrix, weights, weighted, *sends):
    smoothing_near(chans, matrix, weights, weighted, sends)


def smoothing_sub(near, matrix, weights, weighted, basis_across, *refs):
    inverse = refs[: -len(near) - 1]
    coarse, sends = refs[-len(near) - 1], refs[-len(near) :]
    ncl = basis_across.shape[0]
    coarse[0:ncl] = product(basis_across[...], weighted[...])
    for rows in inverse:
        padded = rows.shape[0] + -rows.shape[0] % 8
        coarse[ncl:] = jnp.zeros((coarse.shape[0] - ncl, coarse.shape[1]), jnp.float32)
        for at in range(0, rows.shape[1], LANES):
            start = ncl + at // LANES * padded
            columns = min(LANES, rows.shape[1] - at)
            coarse[start : start + rows.shape[0], 0:columns] = rows[:, at : at + columns]
    smoothing_near(near, matrix, weights, weighted, sends)


def spreading(chans, weights, basis_across, *refs):
    gots, thin, full = refs[:-2], refs[-2], refs[-1]
    ncl = basis_across.shape[0]
    width = full.shape[1] // 2
    for at, (channel, got) in enumerate(zip(chans, gots)):
        for _, own, block in row_blocks(channel):
            from_row = channel[3] + block * ncl
            weight = weights[own][:, 0:ncl]
            here = weight * basis_across[:, own].astype(jnp.float32).T
            there = (1.0 - weight) * got[from_row : from_row + ncl].T
            thin[own] = thrice(jnp.concatenate([here, there], axis=1))
            before = [jnp.zeros((LANES, at * ncl), jnp.float32)] if at else []
            behind = jnp.zeros((LANES, width - (at + 2) * ncl), jnp.float32)
            placed = jnp.concatenate([here, *before, there, behind], axis=1)
            high = placed.astype(jnp.bfloat16)
            full[own, 0:width] = high
            full[own, width:] = (placed - high.astype(jnp.float32)).astype(jnp.bfloat16)


def responding(matrix, full, out, turned):
    width = out.shape[1]
    both = product(matrix[...], full[...])
    out[...] = both[:, 0:width] + both[:, width:]
    for at in range(0, out.shape[0], LANES):
        turned[:, at : at + LANES] = out[at : at + LANES].T


def reaching(channel, count, response, got, out):
    for block, own, from_block in row_blocks(channel):
        at = channel[3] + from_block * count
        theirs = got[at : at + count].T
        both = jnp.concatenate([response[own][:, 0:count], theirs], axis=1)
        out[block * LANES : (block + 1) * LANES] = thrice(both)


def joining(first, second, out):
    out[...] = jnp.concatenate([first[...], second[...]], axis=0)


def coarse_first(chans, order, sub, ncl, numbers, kept, got, out, values, *scratch):
    arranged, upright, relative, pieces = scratch
    index = lax.axis_index("sub")
    rows_of = order // sub
    padded = rows_of + -rows_of % 8
    stride = kept.shape[0] * 2 // sub
    upright[...] = jnp.broadcast_to(numbers[...].astype(jnp.float32), (8, numbers.shape[1])).T
    for block, origin in enumerate(origins(sub)):
        origin = jnp.bitwise_xor(index, origin)
        half = sub // 2
        source = kept if block < half else got
        at = (block % half) * stride
        pieces[block * ncl : (block + 1) * ncl] = source[at : at + ncl]
        to = pl.ds(pl.multiple_of(origin * padded, 8), padded)
        for tile in range(arranged.shape[1] // LANES):
            start = at + ncl + tile * padded
            arranged[to, tile * LANES : (tile + 1) * LANES] = source[start : start + padded]
        relative[block * ncl : (block + 1) * ncl] = upright[pl.ds(pl.multiple_of(origin * ncl, 8), ncl)]
    wanted = []
    for path in near_order(chans):
        place = index
        for c in path:
            place = mate(chans[c][1], place, sub)
        wanted.append(upright[pl.ds(pl.multiple_of(place * ncl, 8), ncl)])
    wanted = jnp.concatenate(wanted, axis=0)[:, 0:1].astype(jnp.int32)
    lane = lax.broadcasted_iota(jnp.int32, (wanted.shape[0], sub * padded), 1)
    inside = lane % padded
    held = jnp.where(inside < rows_of, (lane // padded) * rows_of + inside, -1)
    pick = jnp.where(wanted == held, 1.0, 0.0).astype(jnp.float32)
    chosen = jnp.dot(pick, arranged[...], precision=HIGHEST, preferred_element_type=jnp.float32)
    column = lax.broadcasted_iota(jnp.int32, (relative.shape[0], arranged.shape[1]), 1)
    place = jnp.where(relative[...][:, 0:1].astype(jnp.int32) == column, 1.0, 0.0).astype(jnp.float32)
    out[...] = lax.dot_general(
        chosen, place, (((1,), (1,)), ((), ())), precision=HIGHEST, preferred_element_type=jnp.float32
    )
    values[...] = jnp.dot(out[...], pieces[...], precision=HIGHEST, preferred_element_type=jnp.float32)


def coarse_values(mapping, kept, got, out):
    half = kept.shape[0]
    total = jnp.dot(mapping[:, 0:half], kept[...], precision=HIGHEST, preferred_element_type=jnp.float32)
    total += jnp.dot(mapping[:, half:], got[...], precision=HIGHEST, preferred_element_type=jnp.float32)
    out[...] = total


def between_far(chans, far, count, matrix, load, state, *refs):
    size = len(chans)
    parts, gots = refs[:size], refs[size : 2 * size]
    turned = refs[2 * size : -len(far) - 2]
    ahead, rounded, sends = refs[-len(far) - 2], refs[-len(far) - 1], refs[-len(far) :]
    for channel, part, got in zip(chans, parts, gots):
        own = own_rows(channel)
        ahead[own] = state[own].astype(jnp.float32) + part[...] + across(channel, got)
        rounded[own] = ahead[own].astype(rounded.dtype)
    between_near(far, count, matrix, load, rounded, *turned, *sends)


def between_near(chans, count, matrix, load, state, *refs):
    sends = refs[-len(chans) :]
    for channel, send in zip(chans, sends):
        rows = channel[3]
        own = own_rows(channel)
        send[0:rows] = load[own].astype(jnp.float32) - product(matrix[own], state[...])
        for turned in refs[: -len(chans)]:
            for block, columns, _ in row_blocks(channel):
                send[rows + block * count : rows + (block + 1) * count] = turned[0:count, columns]


def closing(chans, ncl, state, spread, summed, *refs):
    values, refs = value_refs(chans, ncl, refs)
    out = refs[0]
    for at, channel in enumerate(chans):
        own = own_rows(channel)
        pair = jnp.concatenate([values.at(), values.at(at)], axis=0)
        update = product(spread[own], split(pair, 0)) + summed[own]
        out[own] = (state[own].astype(jnp.float32) + update).astype(out.dtype)


def steps(sub):
    found, step = [], sub // 2
    while step:
        found.append(step)
        step //= 2
    return found


def origins(sub):
    found = [0]
    for step in steps(sub):
        found += [origin ^ step for origin in found]
    return found


def gathered(piece, sub, hold=(), wide=False, early=()):
    def hop(move):
        return lax.ppermute(piece, "sub", [(i, i ^ move) for i in range(sub)])

    moves = steps(sub)
    if wide:
        first, second, *moves = moves
        pieces = [piece] + [hop(move) for move in (first, second, first ^ second)]
        piece = jnp.concatenate(pieces, axis=0)
    for at, move in enumerate(moves[:-1]):
        got = hop(move)
        after = hold if at + 1 == len(moves) // 2 else early if at == 0 else ()
        if after:
            joined = jax.ShapeDtypeStruct((2 * piece.shape[0], piece.shape[1]), piece.dtype)
            piece = call(joining, joined, (piece, got), after=after)
        else:
            piece = jnp.concatenate([piece, got], axis=0)
    return piece, hop(moves[-1])


def shards(
    schur_t, neumann_t, face_weights, coarse_basis, coarse_inverse, coarse_number, loads, iterate
):
    schur, neumann = schur_t[0, 0], neumann_t[0, 0]
    basis_across = coarse_basis[0, 0].T
    load, state = loads[0, 0], iterate[0, 0]
    iface, columns = state.shape
    ncl = basis_across.shape[0]
    face = iface // 4
    grp, sub = lax.axis_size("grp"), lax.axis_size("sub")
    chans = channels(grp, sub, face)
    far = tuple(c for c in chans if c[0] == "grp")
    near = chans[len(far) :]
    around = (len(chans) + 1) * ncl
    order = coarse_inverse.shape[2]

    def wide(rows, width=columns):
        return jax.ShapeDtypeStruct((rows, width), jnp.float32)

    def short(rows, width=columns):
        return jax.ShapeDtypeStruct((rows, width), jnp.bfloat16)

    far_plain, near_plain = [tuple(wide(c[3]) for c in group) for group in (far, near)]
    half = short(iface)
    flops = iface * iface * columns

    parts = call(
        functools.partial(opening, chans),
        tuple(wide(c[3] + c[3] // LANES * ncl) for c in chans),
        (schur, load, state, basis_across),
        scratch=(
            pltpu.VMEM(schur.shape, schur.dtype),
            pltpu.VMEM(load.shape, load.dtype),
            pltpu.VMEM(state.shape, state.dtype),
            pltpu.VMEM(basis_across.shape, basis_across.dtype),
            pltpu.SemaphoreType.DMA((3 + PIECES,)),
        ),
        flops=2 * flops,
        away=4,
        grant=56 * MIB,
    )
    gots = exchange(chans, parts)
    parts = call(stash, far_plain + near_plain, tuple(parts))

    weights = jnp.broadcast_to(face_weights[0, 0][:, None], (iface, columns))
    rows_of = coarse_inverse.shape[1]
    tiles = (order + -order % LANES) // LANES
    inverse_rows = (rows_of + -rows_of % 8) * tiles
    mapping = None

    def coarse_step(coarse, mapping, hold=(), after=(), early=()):
        rows = len(near_order(chans)) * ncl
        kept, got = gathered(coarse, sub, hold, not hold, early)
        if mapping is None:
            mapping, own = call(
                functools.partial(coarse_first, chans, order, sub, ncl),
                (wide(rows, sub * ncl), wide(rows)),
                (coarse_number, kept, got),
                scratch=(
                    pltpu.VMEM((inverse_rows // tiles * sub, tiles * LANES), jnp.float32),
                    pltpu.VMEM((sub * ncl, 8), jnp.float32),
                    pltpu.VMEM((sub * ncl, 8), jnp.float32),
                    pltpu.VMEM((sub * ncl, columns), jnp.float32),
                ),
                after=after,
            )
        else:
            own = call(coarse_values, wide(rows), (mapping, kept, got), after=after)
        known = own[0 : (1 + len(near)) * ncl]
        theirs = [swap(known, channel) for channel in far]
        beyond = []
        if len(far) > 1:
            beyond = [swap(theirs[1 - at][0:ncl], channel) for at, channel in enumerate(far)]
        return mapping, (own, *theirs, *beyond)

    def sums(sent, got):
        return call(functools.partial(summing, chans), wide(iface), (*sent, *got), flops=WEIGHT)

    for step in range(ITERS):
        start, last = step == 0, step + 1 == ITERS
        if start:
            weighted, *far_scaled = call(
                functools.partial(smoothing_first, chans, far),
                (half,) + far_plain,
                (neumann, weights, *parts, *gots),
                flops=flops,
            )
        else:
            early = (response,) if step == 1 else ()
            mapping, values = coarse_step(coarse, mapping, hold=scaled_gots[len(far):], early=early)
            if step == 1:
                reach = [
                    call(
                        functools.partial(reaching, channel, around),
                        short(channel[3], 6 * around),
                        (response, got),
                    )
                    for channel, got in zip(chans, gots)
                ]
            known = (weights, ahead, spread, sums(parts, gots), *reach, *values)
            if last:
                state, weighted, coarse = call(
                    functools.partial(smoothing_last, chans, ncl),
                    (half, half, wide(ncl)),
                    (basis_across, *known),
                )
                far_scaled = call(
                    functools.partial(smoothing_rows, far),
                    far_plain,
                    (neumann, weights, weighted),
                    flops=flops,
                )
                near_scaled = call(
                    functools.partial(smoothing_rows, near),
                    near_plain,
                    (neumann, weights, weighted),
                    flops=flops,
                    after=far_scaled[:1],
                )
            else:
                state, weighted, *far_scaled = call(
                    functools.partial(smoothing_far, chans, far, ncl),
                    (half, half) + far_plain,
                    (neumann, *known),
                    flops=flops,
                )
        if not last:
            inverse = (coarse_inverse[0],) if start else ()
            coarse, *near_scaled = call(
                functools.partial(smoothing_sub, near),
                (wide(ncl + len(inverse) * inverse_rows),) + near_plain,
                (neumann, weights, weighted, basis_across, *inverse),
                flops=flops,
            )
        scaled = (*far_scaled, *near_scaled)
        scaled_gots = exchange(chans, scaled)
        behind, behind_rows = (), 0
        if start:
            width = around + -around % LANES
            spread, full = call(
                functools.partial(spreading, chans),
                (short(iface, 6 * ncl), short(iface, 2 * width)),
                (weights, basis_across, *gots),
                after=near_scaled[:1],
            )
            response, turned = call(
                responding, (wide(iface, width), wide(width, iface)), (schur, full), flops=2 * flops
            )
            behind, behind_rows = (turned,), around
        if not last:
            far_outs, near_outs = [
                tuple(wide(c[3] + c[3] // LANES * behind_rows) for c in group) for group in (far, near)
            ]
            ahead, rounded, *far_parts = call(
                functools.partial(between_far, chans, far, around),
                (wide(iface), half) + far_outs,
                (schur, load, state, *scaled, *scaled_gots, *behind),
                flops=flops,
            )
            near_parts = call(
                functools.partial(between_near, near, around),
                near_outs,
                (schur, load, rounded, *behind),
                flops=flops,
                after=far_parts[:1],
            )
            parts = (*far_parts, *near_parts)
            gots = exchange(chans, parts)
    mapping, values = coarse_step(coarse, mapping, after=scaled_gots[len(far) :])
    out = call(
        functools.partial(closing, chans, ncl),
        half,
        (state, spread, sums(scaled, scaled_gots), *values),
    )
    return out[None, None]


def solution(mesh):
    return jax.shard_map(
        shards,
        mesh=mesh,
        in_specs=(
            P("grp", "sub", None, None),
            P("grp", "sub", None, None),
            P("grp", "sub", None),
            P("grp", "sub", None, None),
            P("grp", "sub", None),
            P("grp", None),
            P("grp", "sub", None, None),
            P("grp", "sub", None, None),
        ),
        out_specs=P("grp", "sub", None, None),
        check_vma=False,
    )
```

```python
import functools

import jax
import jax.numpy as jnp
from jax import lax
from jax.experimental import pallas as pl
from jax.experimental.pallas import tpu as pltpu
from jax.sharding import PartitionSpec as P

ITERS = 3
HIGHEST = lax.Precision.HIGHEST
EVEN, ODD, BOTH = range(3)
LANES = 128
PIECES = 8
WEIGHT = 4 * 10**9
MIB = 2**20
WHOLE = pl.BlockSpec(memory_space=pltpu.VMEM)
AWAY = pl.BlockSpec(memory_space=pltpu.HBM)
ANYWHERE = pl.BlockSpec(memory_space=pl.ANY)


def channels(grp, sub, face):
    found = []
    for axis, devices, base in (("grp", grp, 2 * face), ("sub", sub, 0)):
        if devices == 2:
            found.append((axis, BOTH, base, 2 * face))
        else:
            found += [(axis, ODD, base, face), (axis, EVEN, base, face)]
    return tuple(found)


def mate(kind, index, devices):
    if kind == BOTH:
        return 1 - index
    step = 1 - 2 * (index % 2)
    if kind == ODD:
        step = -step
    return (index + step + devices) % devices


def swap(array, channel):
    axis, kind = channel[:2]
    devices = lax.axis_size(axis)
    return lax.ppermute(array, axis, [(i, mate(kind, i, devices)) for i in range(devices)])


def exchange(chans, sends):
    return tuple(swap(send, channel) for channel, send in zip(chans, sends))


def first_row(channel):
    axis, kind, base, rows = channel
    if kind == BOTH:
        return base
    odd = lax.rem(lax.axis_index(axis), 2)
    return pl.multiple_of(base + (odd if kind == ODD else 1 - odd) * rows, rows)


def own_rows(channel):
    return pl.ds(first_row(channel), channel[3])


def row_blocks(channel):
    blocks = channel[3] // LANES
    for block in range(blocks):
        rows = pl.ds(pl.multiple_of(first_row(channel) + block * LANES, LANES), LANES)
        yield block, rows, (block + blocks // 2) % blocks if channel[1] == BOTH else block


def across(channel, got):
    rows = channel[3]
    if channel[1] == BOTH:
        return jnp.concatenate([got[rows // 2 : rows], got[0 : rows // 2]], axis=0)
    return got[0:rows]


def product(a, b):
    return jnp.dot(a, b, preferred_element_type=jnp.float32)


def split(values, axis):
    high = values.astype(jnp.bfloat16)
    low = (values - high.astype(jnp.float32)).astype(jnp.bfloat16)
    return jnp.concatenate([high, low, high], axis=axis)


def thrice(values):
    high = values.astype(jnp.bfloat16).astype(jnp.float32)
    return jnp.concatenate([high, high, values - high], axis=1).astype(jnp.bfloat16)


def call(body, outs, args, scratch=(), flops=0, away=0, after=(), grant=16 * MIB):
    moved = sum(a.size * a.dtype.itemsize for a in args)
    ahead = len(after)
    return pl.pallas_call(
        lambda *refs: body(*refs[ahead:]),
        out_shape=outs,
        in_specs=[ANYWHERE] * ahead + [AWAY] * away + [WHOLE] * (len(args) - away),
        out_specs=jax.tree.map(lambda _: WHOLE, outs),
        scratch_shapes=scratch,
        cost_estimate=pl.CostEstimate(flops=flops, bytes_accessed=moved, transcendentals=0),
        compiler_params=pltpu.CompilerParams(vmem_limit_bytes=grant),
    )(*after, *args)


class Values:
    def __init__(self, chans, ncl, near, far, second):
        self.chans, self.ncl = chans, ncl
        self.near, self.far, self.second = near, far, second
        self.order = near_order(chans)

    def at(self, *path):
        grp = [c for c in path if self.chans[c][0] == "grp"]
        sub = [c for c in path if self.chans[c][0] == "sub"]
        grp, sub = [[] if len(p) == 2 and p[0] == p[1] else p for p in (grp, sub)]
        if len(grp) == 2:
            return self.second[grp[0]][...]
        source = self.far[grp[0]] if grp else self.near
        place = self.order.index(tuple(sub)) * self.ncl
        return source[place : place + self.ncl]

    def around(self, *path):
        return [self.at(*path)] + [self.at(*path, c) for c in range(len(self.chans))]


def near_order(chans):
    kinds = [c for c, channel in enumerate(chans) if channel[0] == "sub"]
    return [()] + [(c,) for c in kinds] + [(c, d) for c in kinds for d in kinds if c != d]


def value_refs(chans, ncl, refs):
    far = sum(channel[0] == "grp" for channel in chans)
    second = far if far > 1 else 0
    values = Values(chans, ncl, refs[0], refs[1 : 1 + far], refs[1 + far : 1 + far + second])
    return values, refs[1 + far + second :]


def opening(chans, matrix, load, state, basis_across, *refs):
    sends, (rows, mine, now, basis, sems) = refs[:-5], refs[-5:]
    piece = matrix.shape[0] // PIECES
    order = [(at + PIECES // 2) % PIECES * piece for at in range(PIECES)]
    pairs = [(state, now), (load, mine)]
    pairs += [(matrix.at[pl.ds(at, piece)], rows.at[pl.ds(at, piece)]) for at in order]
    pairs.append((basis_across, basis))
    copies = [pltpu.make_async_copy(a, b, sems.at[i]) for i, (a, b) in enumerate(pairs)]
    for copy in copies:
        copy.start()
    first = 2 + PIECES // 2
    for copy in copies[:first]:
        copy.wait()
    waiting = copies[first:]
    for channel, send in zip(chans, sends):
        if channel[0] == "sub":
            while waiting:
                waiting.pop(0).wait()
        own = own_rows(channel)
        send[0 : channel[3]] = mine[own].astype(jnp.float32) - product(rows[own], now[...])
    ncl = basis.shape[0]
    for channel, send in zip(chans, sends):
        for block, columns, _ in row_blocks(channel):
            at = channel[3] + block * ncl
            send[at : at + ncl] = basis[:, columns].astype(jnp.float32)


def smooth(chans, weights, resid_on, weighted):
    for at, channel in enumerate(chans):
        own = own_rows(channel)
        weighted[own] = (weights[own] * resid_on(at, own)).astype(jnp.bfloat16)


def smoothing_near(chans, matrix, weights, weighted, sends):
    for channel, send in zip(chans, sends):
        own = own_rows(channel)
        send[...] = weights[own] * product(matrix[own], weighted[...])


def stash(*refs):
    count = len(refs) // 2
    for part, out in zip(refs[:count], refs[count:]):
        out[...] = part[0 : out.shape[0]]


def summing(chans, *refs):
    count = len(chans)
    parts, gots, out = refs[:count], refs[count : 2 * count], refs[2 * count]
    for channel, part, got in zip(chans, parts, gots):
        out[own_rows(channel)] = part[0 : channel[3]] + across(channel, got)


def smoothing_first(chans, far, matrix, weights, *refs):
    count = len(chans)
    parts, gots = refs[:count], refs[count : 2 * count]

    def resid_on(at, own):
        return parts[at][...] + across(chans[at], gots[at])

    smooth(chans, weights, resid_on, refs[2 * count])
    smoothing_near(far, matrix, weights, refs[2 * count], refs[2 * count + 1 :])


def correct(chans, ncl, weights, ahead, spread, summed, refs):
    reach = refs[: len(chans)]
    values, refs = value_refs(chans, ncl, refs[len(chans) :])
    state, weighted, rest = refs[0], refs[1], refs[2:]
    here = values.around()

    def resid_on(at, own):
        pair = jnp.concatenate([here[0], values.at(at)], axis=0)
        state[own] = (ahead[own] + product(spread[own], split(pair, 0))).astype(state.dtype)
        both = jnp.concatenate(here + values.around(at), axis=0)
        return summed[own] - product(reach[at][...], split(both, 0))

    smooth(chans, weights, resid_on, weighted)
    return weighted, rest


def smoothing_far(chans, far, ncl, matrix, weights, ahead, spread, summed, *refs):
    weighted, sends = correct(chans, ncl, weights, ahead, spread, summed, refs)
    smoothing_near(far, matrix, weights, weighted, sends)


def smoothing_last(chans, ncl, basis_across, weights, ahead, spread, summed, *refs):
    weighted, (coarse,) = correct(chans, ncl, weights, ahead, spread, summed, refs)
    coarse[...] = product(basis_across[...], weighted[...])


def smoothing_rows(chans, matrix, weights, weighted, *sends):
    smoothing_near(chans, matrix, weights, weighted, sends)


def smoothing_sub(near, matrix, weights, weighted, basis_across, *refs):
    inverse = refs[: -len(near) - 1]
    coarse, sends = refs[-len(near) - 1], refs[-len(near) :]
    ncl = basis_across.shape[0]
    coarse[0:ncl] = product(basis_across[...], weighted[...])
    for rows in inverse:
        padded = rows.shape[0] + -rows.shape[0] % 8
        coarse[ncl:] = jnp.zeros((coarse.shape[0] - ncl, coarse.shape[1]), jnp.float32)
        for at in range(0, rows.shape[1], LANES):
            start = ncl + at // LANES * padded
            columns = min(LANES, rows.shape[1] - at)
            coarse[start : start + rows.shape[0], 0:columns] = rows[:, at : at + columns]
    smoothing_near(near, matrix, weights, weighted, sends)


def spreading(chans, weights, basis_across, *refs):
    gots, thin, full = refs[:-2], refs[-2], refs[-1]
    ncl = basis_across.shape[0]
    width = full.shape[1] // 2
    for at, (channel, got) in enumerate(zip(chans, gots)):
        for _, own, block in row_blocks(channel):
            from_row = channel[3] + block * ncl
            weight = weights[own][:, 0:ncl]
            here = weight * basis_across[:, own].astype(jnp.float32).T
            there = (1.0 - weight) * got[from_row : from_row + ncl].T
            thin[own] = thrice(jnp.concatenate([here, there], axis=1))
            before = [jnp.zeros((LANES, at * ncl), jnp.float32)] if at else []
            behind = jnp.zeros((LANES, width - (at + 2) * ncl), jnp.float32)
            placed = jnp.concatenate([here, *before, there, behind], axis=1)
            high = placed.astype(jnp.bfloat16)
            full[own, 0:width] = high
            full[own, width:] = (placed - high.astype(jnp.float32)).astype(jnp.bfloat16)


def responding(matrix, full, out, turned):
    width = out.shape[1]
    both = product(matrix[...], full[...])
    out[...] = both[:, 0:width] + both[:, width:]
    for at in range(0, out.shape[0], LANES):
        turned[:, at : at + LANES] = out[at : at + LANES].T


def reaching(channel, count, response, got, out):
    for block, own, from_block in row_blocks(channel):
        at = channel[3] + from_block * count
        theirs = got[at : at + count].T
        both = jnp.concatenate([response[own][:, 0:count], theirs], axis=1)
        out[block * LANES : (block + 1) * LANES] = thrice(both)


def joining(first, second, out):
    out[...] = jnp.concatenate([first[...], second[...]], axis=0)


def coarse_first(chans, order, sub, ncl, numbers, kept, got, out, values, *scratch):
    arranged, upright, relative, pieces = scratch
    index = lax.axis_index("sub")
    rows_of = order // sub
    padded = rows_of + -rows_of % 8
    stride = kept.shape[0] * 2 // sub
    upright[...] = jnp.broadcast_to(numbers[...].astype(jnp.float32), (8, numbers.shape[1])).T
    for block, origin in enumerate(origins(sub)):
        origin = jnp.bitwise_xor(index, origin)
        half = sub // 2
        source = kept if block < half else got
        at = (block % half) * stride
        pieces[block * ncl : (block + 1) * ncl] = source[at : at + ncl]
        to = pl.ds(pl.multiple_of(origin * padded, 8), padded)
        for tile in range(arranged.shape[1] // LANES):
            start = at + ncl + tile * padded
            arranged[to, tile * LANES : (tile + 1) * LANES] = source[start : start + padded]
        relative[block * ncl : (block + 1) * ncl] = upright[pl.ds(pl.multiple_of(origin * ncl, 8), ncl)]
    wanted = []
    for path in near_order(chans):
        place = index
        for c in path:
            place = mate(chans[c][1], place, sub)
        wanted.append(upright[pl.ds(pl.multiple_of(place * ncl, 8), ncl)])
    wanted = jnp.concatenate(wanted, axis=0)[:, 0:1].astype(jnp.int32)
    lane = lax.broadcasted_iota(jnp.int32, (wanted.shape[0], sub * padded), 1)
    inside = lane % padded
    held = jnp.where(inside < rows_of, (lane // padded) * rows_of + inside, -1)
    pick = jnp.where(wanted == held, 1.0, 0.0).astype(jnp.float32)
    chosen = jnp.dot(pick, arranged[...], precision=HIGHEST, preferred_element_type=jnp.float32)
    column = lax.broadcasted_iota(jnp.int32, (relative.shape[0], arranged.shape[1]), 1)
    place = jnp.where(relative[...][:, 0:1].astype(jnp.int32) == column, 1.0, 0.0).astype(jnp.float32)
    out[...] = lax.dot_general(
        chosen, place, (((1,), (1,)), ((), ())), precision=HIGHEST, preferred_element_type=jnp.float32
    )
    values[...] = jnp.dot(out[...], pieces[...], precision=HIGHEST, preferred_element_type=jnp.float32)


def coarse_values(mapping, kept, got, out):
    half = kept.shape[0]
    total = jnp.dot(mapping[:, 0:half], kept[...], precision=HIGHEST, preferred_element_type=jnp.float32)
    total += jnp.dot(mapping[:, half:], got[...], precision=HIGHEST, preferred_element_type=jnp.float32)
    out[...] = total


def between_far(chans, far, count, matrix, load, state, *refs):
    size = len(chans)
    parts, gots = refs[:size], refs[size : 2 * size]
    turned = refs[2 * size : -len(far) - 2]
    ahead, rounded, sends = refs[-len(far) - 2], refs[-len(far) - 1], refs[-len(far) :]
    for channel, part, got in zip(chans, parts, gots):
        own = own_rows(channel)
        ahead[own] = state[own].astype(jnp.float32) + part[...] + across(channel, got)
        rounded[own] = ahead[own].astype(rounded.dtype)
    between_near(far, count, matrix, load, rounded, *turned, *sends)


def between_near(chans, count, matrix, load, state, *refs):
    sends = refs[-len(chans) :]
    for channel, send in zip(chans, sends):
        rows = channel[3]
        own = own_rows(channel)
        send[0:rows] = load[own].astype(jnp.float32) - product(matrix[own], state[...])
        for turned in refs[: -len(chans)]:
            for block, columns, _ in row_blocks(channel):
                send[rows + block * count : rows + (block + 1) * count] = turned[0:count, columns]


def closing(chans, ncl, state, spread, summed, *refs):
    values, refs = value_refs(chans, ncl, refs)
    out = refs[0]
    for at, channel in enumerate(chans):
        own = own_rows(channel)
        pair = jnp.concatenate([values.at(), values.at(at)], axis=0)
        update = product(spread[own], split(pair, 0)) + summed[own]
        out[own] = (state[own].astype(jnp.float32) + update).astype(out.dtype)


def steps(sub):
    found, step = [], sub // 2
    while step:
        found.append(step)
        step //= 2
    return found


def origins(sub):
    found = [0]
    for step in steps(sub):
        found += [origin ^ step for origin in found]
    return found


def hop(piece, sub, move):
    return lax.ppermute(piece, "sub", [(i, i ^ move) for i in range(sub)])


def gathered(piece, sub, hold=(), wide=False, early=(), begun=None):
    moves = steps(sub)
    first = None
    if wide:
        one, two, *moves = moves
        piece = first = jnp.concatenate([piece] + [hop(piece, sub, move) for move in (one, two, one ^ two)], axis=0)
    for at, move in enumerate(moves[:-1]):
        got = hop(piece, sub, move) if at or begun is None else begun
        after = hold if at + 1 == len(moves) // 2 else early if at == 0 else ()
        if after:
            joined = jax.ShapeDtypeStruct((2 * piece.shape[0], piece.shape[1]), piece.dtype)
            piece = call(joining, joined, (piece, got), after=after, flops=2 * 10**9)
        else:
            piece = jnp.concatenate([piece, got], axis=0)
    return (piece, hop(piece, sub, moves[-1])), first


def shards(
    schur_t, neumann_t, face_weights, coarse_basis, coarse_inverse, coarse_number, loads, iterate
):
    schur, neumann = schur_t[0, 0], neumann_t[0, 0]
    basis_across = coarse_basis[0, 0].T
    load, state = loads[0, 0], iterate[0, 0]
    iface, columns = state.shape
    ncl = basis_across.shape[0]
    face = iface // 4
    grp, sub = lax.axis_size("grp"), lax.axis_size("sub")
    chans = channels(grp, sub, face)
    far = tuple(c for c in chans if c[0] == "grp")
    near = chans[len(far) :]
    around = (len(chans) + 1) * ncl
    order = coarse_inverse.shape[2]

    def wide(rows, width=columns):
        return jax.ShapeDtypeStruct((rows, width), jnp.float32)

    def short(rows, width=columns):
        return jax.ShapeDtypeStruct((rows, width), jnp.bfloat16)

    far_plain, near_plain = [tuple(wide(c[3]) for c in group) for group in (far, near)]
    half = short(iface)
    flops = iface * iface * columns

    parts = call(
        functools.partial(opening, chans),
        tuple(wide(c[3] + c[3] // LANES * ncl) for c in chans),
        (schur, load, state, basis_across),
        scratch=(
            pltpu.VMEM(schur.shape, schur.dtype),
            pltpu.VMEM(load.shape, load.dtype),
            pltpu.VMEM(state.shape, state.dtype),
            pltpu.VMEM(basis_across.shape, basis_across.dtype),
            pltpu.SemaphoreType.DMA((3 + PIECES,)),
        ),
        flops=2 * flops,
        away=4,
        grant=56 * MIB,
    )
    gots = exchange(chans, parts)
    parts = call(stash, far_plain + near_plain, tuple(parts))

    weights = jnp.broadcast_to(face_weights[0, 0][:, None], (iface, columns))
    rows_of = coarse_inverse.shape[1]
    tiles = (order + -order % LANES) // LANES
    inverse_rows = (rows_of + -rows_of % 8) * tiles
    mapping = None

    def coarse_step(pieces, mapping, after=()):
        rows = len(near_order(chans)) * ncl
        if mapping is None:
            mapping, own = call(
                functools.partial(coarse_first, chans, order, sub, ncl),
                (wide(rows, sub * ncl), wide(rows)),
                (coarse_number, *pieces),
                scratch=(
                    pltpu.VMEM((inverse_rows // tiles * sub, tiles * LANES), jnp.float32),
                    pltpu.VMEM((sub * ncl, 8), jnp.float32),
                    pltpu.VMEM((sub * ncl, 8), jnp.float32),
                    pltpu.VMEM((sub * ncl, columns), jnp.float32),
                ),
                after=after,
            )
        else:
            own = call(coarse_values, wide(rows), (mapping, *pieces), after=after)
        known = own[0 : (1 + len(near)) * ncl]
        theirs = [swap(known, channel) for channel in far]
        beyond = []
        if len(far) > 1:
            beyond = [swap(theirs[1 - at][0:ncl], channel) for at, channel in enumerate(far)]
        return mapping, (own, *theirs, *beyond)

    def sums(sent, got):
        return call(functools.partial(summing, chans), wide(iface), (*sent, *got), flops=WEIGHT)

    for step in range(ITERS):
        start, last = step == 0, step + 1 == ITERS
        if start:
            weighted, *far_scaled = call(
                functools.partial(smoothing_first, chans, far),
                (half,) + far_plain,
                (neumann, weights, *parts, *gots),
                flops=flops,
            )
        else:
            early = (response,) if step == 1 else near_scaled[:1]
            pieces, _ = gathered(coarse, sub, hold=far_parts[:1], early=early, begun=begun)
            mapping, values = coarse_step(pieces, mapping)
            if step == 1:
                reach = [
                    call(
                        functools.partial(reaching, channel, around),
                        short(channel[3], 6 * around),
                        (response, got),
                    )
                    for channel, got in zip(chans, gots)
                ]
            known = (weights, ahead, spread, sums(parts, gots), *reach, *values)
            if last:
                state, weighted, coarse = call(
                    functools.partial(smoothing_last, chans, ncl),
                    (half, half, wide(ncl)),
                    (basis_across, *known),
                )
                pieces, first = gathered(coarse, sub, wide=True)
                far_scaled = call(
                    functools.partial(smoothing_rows, far),
                    far_plain,
                    (neumann, weights, weighted),
                    flops=flops,
                    after=(first,),
                )
                near_scaled = call(
                    functools.partial(smoothing_rows, near),
                    near_plain,
                    (neumann, weights, weighted),
                    flops=flops,
                    after=far_scaled[:1],
                )
            else:
                state, weighted, *far_scaled = call(
                    functools.partial(smoothing_far, chans, far, ncl),
                    (half, half) + far_plain,
                    (neumann, *known),
                    flops=flops,
                )
        if not last:
            inverse = (coarse_inverse[0],) if start else ()
            coarse, *near_scaled = call(
                functools.partial(smoothing_sub, near),
                (wide(ncl + len(inverse) * inverse_rows),) + near_plain,
                (neumann, weights, weighted, basis_across, *inverse),
                flops=flops,
            )
            begun = hop(coarse, sub, steps(sub)[0])
        scaled = (*far_scaled, *near_scaled)
        scaled_gots = exchange(chans, scaled)
        behind, behind_rows = (), 0
        if start:
            width = around + -around % LANES
            spread, full = call(
                functools.partial(spreading, chans),
                (short(iface, 6 * ncl), short(iface, 2 * width)),
                (weights, basis_across, *gots),
                after=near_scaled[:1],
            )
            response, turned = call(
                responding, (wide(iface, width), wide(width, iface)), (schur, full), flops=2 * flops
            )
            behind, behind_rows = (turned,), around
        if not last:
            far_outs, near_outs = [
                tuple(wide(c[3] + c[3] // LANES * behind_rows) for c in group) for group in (far, near)
            ]
            ahead, rounded, *far_parts = call(
                functools.partial(between_far, chans, far, around),
                (wide(iface), half) + far_outs,
                (schur, load, state, *scaled, *scaled_gots, *behind),
                flops=flops,
            )
            near_parts = call(
                functools.partial(between_near, near, around),
                near_outs,
                (schur, load, rounded, *behind),
                flops=(12 if start else 4) * flops,
                after=far_parts[:1],
            )
            parts = (*far_parts, *near_parts)
            gots = exchange(chans, parts)
    _, values = coarse_step(pieces, mapping)
    out = call(
        functools.partial(closing, chans, ncl),
        half,
        (state, spread, sums(scaled, scaled_gots), *values),
    )
    return out[None, None]


def solution(mesh):
    return jax.shard_map(
        shards,
        mesh=mesh,
        in_specs=(
            P("grp", "sub", None, None),
            P("grp", "sub", None, None),
            P("grp", "sub", None),
            P("grp", "sub", None, None),
            P("grp", "sub", None),
            P("grp", None),
            P("grp", "sub", None, None),
            P("grp", "sub", None, None),
        ),
        out_specs=P("grp", "sub", None, None),
        check_vma=False,
    )
```

```python
import functools

import jax
import jax.numpy as jnp
from jax import lax
from jax.experimental import pallas as pl
from jax.experimental.pallas import tpu as pltpu
from jax.sharding import PartitionSpec as P

ITERS = 3
HIGHEST = lax.Precision.HIGHEST
EVEN, ODD, BOTH = range(3)
LANES = 128
PIECES = 4
WEIGHT = 4 * 10**9
MIB = 2**20
WHOLE = pl.BlockSpec(memory_space=pltpu.VMEM)
AWAY = pl.BlockSpec(memory_space=pltpu.HBM)
ANYWHERE = pl.BlockSpec(memory_space=pl.ANY)


def channels(grp, sub, face):
    found = []
    for axis, devices, base in (("grp", grp, 2 * face), ("sub", sub, 0)):
        if devices == 2:
            found.append((axis, BOTH, base, 2 * face))
        else:
            found += [(axis, ODD, base, face), (axis, EVEN, base, face)]
    return tuple(found)


def mate(kind, index, devices):
    if kind == BOTH:
        return 1 - index
    step = 1 - 2 * (index % 2)
    if kind == ODD:
        step = -step
    return (index + step + devices) % devices


def swap(array, channel):
    axis, kind = channel[:2]
    devices = lax.axis_size(axis)
    return lax.ppermute(array, axis, [(i, mate(kind, i, devices)) for i in range(devices)])


def exchange(chans, sends):
    return tuple(swap(send, channel) for channel, send in zip(chans, sends))


def first_row(channel):
    axis, kind, base, rows = channel
    if kind == BOTH:
        return base
    odd = lax.rem(lax.axis_index(axis), 2)
    return pl.multiple_of(base + (odd if kind == ODD else 1 - odd) * rows, rows)


def own_rows(channel):
    return pl.ds(first_row(channel), channel[3])


def row_blocks(channel):
    blocks = channel[3] // LANES
    for block in range(blocks):
        rows = pl.ds(pl.multiple_of(first_row(channel) + block * LANES, LANES), LANES)
        yield block, rows, (block + blocks // 2) % blocks if channel[1] == BOTH else block


def across(channel, got):
    rows = channel[3]
    if channel[1] == BOTH:
        return jnp.concatenate([got[rows // 2 : rows], got[0 : rows // 2]], axis=0)
    return got[0:rows]


def product(a, b):
    return jnp.dot(a, b, preferred_element_type=jnp.float32)


def split(values, axis):
    high = values.astype(jnp.bfloat16)
    low = (values - high.astype(jnp.float32)).astype(jnp.bfloat16)
    return jnp.concatenate([high, low, high], axis=axis)


def thrice(values):
    high = values.astype(jnp.bfloat16).astype(jnp.float32)
    return jnp.concatenate([high, high, values - high], axis=1).astype(jnp.bfloat16)


def call(body, outs, args, scratch=(), flops=0, away=0, after=(), grant=16 * MIB):
    moved = sum(a.size * a.dtype.itemsize for a in args)
    ahead = len(after)
    return pl.pallas_call(
        lambda *refs: body(*refs[ahead:]),
        out_shape=outs,
        in_specs=[ANYWHERE] * ahead + [AWAY] * away + [WHOLE] * (len(args) - away),
        out_specs=jax.tree.map(lambda _: WHOLE, outs),
        scratch_shapes=scratch,
        cost_estimate=pl.CostEstimate(flops=flops, bytes_accessed=moved, transcendentals=0),
        compiler_params=pltpu.CompilerParams(vmem_limit_bytes=grant),
    )(*after, *args)


class Values:
    def __init__(self, chans, ncl, near, far, second):
        self.chans, self.ncl = chans, ncl
        self.near, self.far, self.second = near, far, second
        self.order = near_order(chans)

    def at(self, *path):
        grp = [c for c in path if self.chans[c][0] == "grp"]
        sub = [c for c in path if self.chans[c][0] == "sub"]
        grp, sub = [[] if len(p) == 2 and p[0] == p[1] else p for p in (grp, sub)]
        if len(grp) == 2:
            return self.second[grp[0]][...]
        source = self.far[grp[0]] if grp else self.near
        place = self.order.index(tuple(sub)) * self.ncl
        return source[place : place + self.ncl]

    def around(self, *path):
        return [self.at(*path)] + [self.at(*path, c) for c in range(len(self.chans))]


def near_order(chans):
    kinds = [c for c, channel in enumerate(chans) if channel[0] == "sub"]
    return [()] + [(c,) for c in kinds] + [(c, d) for c in kinds for d in kinds if c != d]


def value_refs(chans, ncl, refs):
    far = sum(channel[0] == "grp" for channel in chans)
    second = far if far > 1 else 0
    values = Values(chans, ncl, refs[0], refs[1 : 1 + far], refs[1 + far : 1 + far + second])
    return values, refs[1 + far + second :]


def opening(chans, first, matrix, load, state, basis_across, *refs):
    sends, (rows, mine, now, basis, sems) = refs[:-5], refs[-5:]
    half = rows.shape[0]
    piece = half // PIECES
    pairs = [(state, now), (load.at[pl.ds(first, half)], mine), (basis_across, basis)]
    pairs += [
        (matrix.at[pl.ds(first + at, piece)], rows.at[pl.ds(at, piece)]) for at in range(0, half, piece)
    ]
    copies = [pltpu.make_async_copy(a, b, sems.at[i]) for i, (a, b) in enumerate(pairs)]
    for copy in copies:
        copy.start()
    for copy in copies:
        copy.wait()
    ncl = basis.shape[0]
    for channel, send in zip(chans, sends):
        own = pl.ds(pl.multiple_of(first_row(channel) - first, channel[3]), channel[3])
        send[0 : channel[3]] = mine[own].astype(jnp.float32) - product(rows[own], now[...])
        for block, columns, _ in row_blocks(channel):
            at = channel[3] + block * ncl
            send[at : at + ncl] = basis[:, columns].astype(jnp.float32)


def smooth(chans, weights, resid_on, weighted):
    for at, channel in enumerate(chans):
        own = own_rows(channel)
        weighted[own] = (weights[own] * resid_on(at, own)).astype(jnp.bfloat16)


def smoothing_near(chans, matrix, weights, weighted, sends):
    for channel, send in zip(chans, sends):
        own = own_rows(channel)
        send[...] = weights[own] * product(matrix[own], weighted[...])


def stash(*refs):
    count = len(refs) // 2
    for part, out in zip(refs[:count], refs[count:]):
        out[...] = part[0 : out.shape[0]]


def summing(chans, *refs):
    count = len(chans)
    parts, gots, out = refs[:count], refs[count : 2 * count], refs[2 * count]
    for channel, part, got in zip(chans, parts, gots):
        out[own_rows(channel)] = part[0 : channel[3]] + across(channel, got)


def smoothing_first(chans, far, matrix, weights, *refs):
    count = len(chans)
    parts, gots = refs[:count], refs[count : 2 * count]

    def resid_on(at, own):
        return parts[at][...] + across(chans[at], gots[at])

    smooth(chans, weights, resid_on, refs[2 * count])
    smoothing_near(far, matrix, weights, refs[2 * count], refs[2 * count + 1 :])


def correct(chans, ncl, weights, ahead, spread, summed, refs):
    reach = refs[: len(chans)]
    values, refs = value_refs(chans, ncl, refs[len(chans) :])
    state, weighted, rest = refs[0], refs[1], refs[2:]
    here = values.around()

    def resid_on(at, own):
        pair = jnp.concatenate([here[0], values.at(at)], axis=0)
        state[own] = (ahead[own] + product(spread[own], split(pair, 0))).astype(state.dtype)
        both = jnp.concatenate(here + values.around(at), axis=0)
        return summed[own] - product(reach[at][...], split(both, 0))

    smooth(chans, weights, resid_on, weighted)
    return weighted, rest


def smoothing_far(chans, far, ncl, matrix, weights, ahead, spread, summed, *refs):
    weighted, sends = correct(chans, ncl, weights, ahead, spread, summed, refs)
    smoothing_near(far, matrix, weights, weighted, sends)


def smoothing_last(chans, ncl, basis_across, weights, ahead, spread, summed, *refs):
    weighted, (coarse,) = correct(chans, ncl, weights, ahead, spread, summed, refs)
    coarse[...] = product(basis_across[...], weighted[...])


def smoothing_rows(chans, matrix, weights, weighted, *sends):
    smoothing_near(chans, matrix, weights, weighted, sends)


def smoothing_sub(near, matrix, weights, weighted, basis_across, *refs):
    inverse = refs[: -len(near) - 1]
    coarse, sends = refs[-len(near) - 1], refs[-len(near) :]
    ncl = basis_across.shape[0]
    coarse[0:ncl] = product(basis_across[...], weighted[...])
    for rows in inverse:
        padded = rows.shape[0] + -rows.shape[0] % 8
        coarse[ncl:] = jnp.zeros((coarse.shape[0] - ncl, coarse.shape[1]), jnp.float32)
        for at in range(0, rows.shape[1], LANES):
            start = ncl + at // LANES * padded
            columns = min(LANES, rows.shape[1] - at)
            coarse[start : start + rows.shape[0], 0:columns] = rows[:, at : at + columns]
    smoothing_near(near, matrix, weights, weighted, sends)


def spreading(chans, weights, basis_across, *refs):
    gots, thin, full = refs[:-2], refs[-2], refs[-1]
    ncl = basis_across.shape[0]
    width = full.shape[1] // 2
    for at, (channel, got) in enumerate(zip(chans, gots)):
        for _, own, block in row_blocks(channel):
            from_row = channel[3] + block * ncl
            weight = weights[own][:, 0:ncl]
            here = weight * basis_across[:, own].astype(jnp.float32).T
            there = (1.0 - weight) * got[from_row : from_row + ncl].T
            thin[own] = thrice(jnp.concatenate([here, there], axis=1))
            before = [jnp.zeros((LANES, at * ncl), jnp.float32)] if at else []
            behind = jnp.zeros((LANES, width - (at + 2) * ncl), jnp.float32)
            placed = jnp.concatenate([here, *before, there, behind], axis=1)
            high = placed.astype(jnp.bfloat16)
            full[own, 0:width] = high
            full[own, width:] = (placed - high.astype(jnp.float32)).astype(jnp.bfloat16)


def responding(matrix, full, out, turned):
    width = out.shape[1]
    both = product(matrix[...], full[...])
    out[...] = both[:, 0:width] + both[:, width:]
    for at in range(0, out.shape[0], LANES):
        turned[:, at : at + LANES] = out[at : at + LANES].T


def reaching(channel, count, response, got, out):
    for block, own, from_block in row_blocks(channel):
        at = channel[3] + from_block * count
        theirs = got[at : at + count].T
        both = jnp.concatenate([response[own][:, 0:count], theirs], axis=1)
        out[block * LANES : (block + 1) * LANES] = thrice(both)


def joining(first, second, out):
    out[...] = jnp.concatenate([first[...], second[...]], axis=0)


def coarse_first(chans, order, sub, ncl, numbers, kept, got, out, values, *scratch):
    arranged, upright, relative, pieces = scratch
    index = lax.axis_index("sub")
    rows_of = order // sub
    padded = rows_of + -rows_of % 8
    stride = kept.shape[0] * 2 // sub
    upright[...] = jnp.broadcast_to(numbers[...].astype(jnp.float32), (8, numbers.shape[1])).T
    for block, origin in enumerate(origins(sub)):
        origin = jnp.bitwise_xor(index, origin)
        half = sub // 2
        source = kept if block < half else got
        at = (block % half) * stride
        pieces[block * ncl : (block + 1) * ncl] = source[at : at + ncl]
        to = pl.ds(pl.multiple_of(origin * padded, 8), padded)
        for tile in range(arranged.shape[1] // LANES):
            start = at + ncl + tile * padded
            arranged[to, tile * LANES : (tile + 1) * LANES] = source[start : start + padded]
        relative[block * ncl : (block + 1) * ncl] = upright[pl.ds(pl.multiple_of(origin * ncl, 8), ncl)]
    wanted = []
    for path in near_order(chans):
        place = index
        for c in path:
            place = mate(chans[c][1], place, sub)
        wanted.append(upright[pl.ds(pl.multiple_of(place * ncl, 8), ncl)])
    wanted = jnp.concatenate(wanted, axis=0)[:, 0:1].astype(jnp.int32)
    lane = lax.broadcasted_iota(jnp.int32, (wanted.shape[0], sub * padded), 1)
    inside = lane % padded
    held = jnp.where(inside < rows_of, (lane // padded) * rows_of + inside, -1)
    pick = jnp.where(wanted == held, 1.0, 0.0).astype(jnp.float32)
    chosen = jnp.dot(pick, arranged[...], precision=HIGHEST, preferred_element_type=jnp.float32)
    column = lax.broadcasted_iota(jnp.int32, (relative.shape[0], arranged.shape[1]), 1)
    place = jnp.where(relative[...][:, 0:1].astype(jnp.int32) == column, 1.0, 0.0).astype(jnp.float32)
    out[...] = lax.dot_general(
        chosen, place, (((1,), (1,)), ((), ())), precision=HIGHEST, preferred_element_type=jnp.float32
    )
    values[...] = jnp.dot(out[...], pieces[...], precision=HIGHEST, preferred_element_type=jnp.float32)


def coarse_values(mapping, kept, got, out):
    half = kept.shape[0]
    total = jnp.dot(mapping[:, 0:half], kept[...], precision=HIGHEST, preferred_element_type=jnp.float32)
    total += jnp.dot(mapping[:, half:], got[...], precision=HIGHEST, preferred_element_type=jnp.float32)
    out[...] = total


def between(chans, count, matrix, load, state, *refs):
    size = len(chans)
    parts, gots = refs[:size], refs[size : 2 * size]
    responses = refs[2 * size : -size - 2]
    ahead, rounded, sends = refs[-size - 2], refs[-size - 1], refs[-size:]
    for channel, part, got in zip(chans, parts, gots):
        own = own_rows(channel)
        ahead[own] = state[own].astype(jnp.float32) + part[...] + across(channel, got)
        rounded[own] = ahead[own].astype(rounded.dtype)
    for channel, send in zip(chans, sends):
        rows = channel[3]
        own = own_rows(channel)
        send[0:rows] = load[own].astype(jnp.float32) - product(matrix[own], rounded[...])
        for turned in responses:
            for block, columns, _ in row_blocks(channel):
                send[rows + block * count : rows + (block + 1) * count] = turned[0:count, columns]


def closing(chans, ncl, state, spread, summed, *refs):
    values, refs = value_refs(chans, ncl, refs)
    out = refs[0]
    for at, channel in enumerate(chans):
        own = own_rows(channel)
        pair = jnp.concatenate([values.at(), values.at(at)], axis=0)
        update = product(spread[own], split(pair, 0)) + summed[own]
        out[own] = (state[own].astype(jnp.float32) + update).astype(out.dtype)


def steps(sub):
    found, step = [], sub // 2
    while step:
        found.append(step)
        step //= 2
    return found


def origins(sub):
    found = [0]
    for step in steps(sub):
        found += [origin ^ step for origin in found]
    return found


def gathered(piece, sub, hold=(), wide=False, early=()):
    def hop(move):
        return lax.ppermute(piece, "sub", [(i, i ^ move) for i in range(sub)])

    moves = steps(sub)
    if wide:
        first, second, *moves = moves
        pieces = [piece] + [hop(move) for move in (first, second, first ^ second)]
        piece = jnp.concatenate(pieces, axis=0)
    for at, move in enumerate(moves[:-1]):
        got = hop(move)
        after = hold if at + 1 == len(moves) // 2 else early if at == 0 else ()
        if after:
            joined = jax.ShapeDtypeStruct((2 * piece.shape[0], piece.shape[1]), piece.dtype)
            piece = call(joining, joined, (piece, got), after=after, flops=0 if after is hold else WEIGHT // 2)
        else:
            piece = jnp.concatenate([piece, got], axis=0)
    return piece, hop(moves[-1])


def shards(
    schur_t, neumann_t, face_weights, coarse_basis, coarse_inverse, coarse_number, loads, iterate
):
    schur, neumann = schur_t[0, 0], neumann_t[0, 0]
    basis_across = coarse_basis[0, 0].T
    load, state = loads[0, 0], iterate[0, 0]
    iface, columns = state.shape
    ncl = basis_across.shape[0]
    face = iface // 4
    grp, sub = lax.axis_size("grp"), lax.axis_size("sub")
    chans = channels(grp, sub, face)
    far = tuple(c for c in chans if c[0] == "grp")
    near = chans[len(far) :]
    around = (len(chans) + 1) * ncl
    order = coarse_inverse.shape[2]

    def wide(rows, width=columns):
        return jax.ShapeDtypeStruct((rows, width), jnp.float32)

    def short(rows, width=columns):
        return jax.ShapeDtypeStruct((rows, width), jnp.bfloat16)

    far_plain, near_plain = [tuple(wide(c[3]) for c in group) for group in (far, near)]
    half = short(iface)
    flops = iface * iface * columns

    def opened(group, first, after=()):
        return call(
            functools.partial(opening, group, first),
            tuple(wide(c[3] + c[3] // LANES * ncl) for c in group),
            (schur, load, state, basis_across),
            scratch=(
                pltpu.VMEM((iface // 2, iface), schur.dtype),
                pltpu.VMEM((iface // 2, columns), load.dtype),
                pltpu.VMEM(state.shape, state.dtype),
                pltpu.VMEM(basis_across.shape, basis_across.dtype),
                pltpu.SemaphoreType.DMA((3 + PIECES,)),
            ),
            flops=flops,
            away=4,
            grant=56 * MIB,
            after=after,
        )

    far_parts = opened(far, iface // 2)
    parts = (*far_parts, *opened(near, 0, far_parts[:1]))
    gots = exchange(chans, parts)
    parts = call(stash, far_plain + near_plain, tuple(parts))

    weights = jnp.broadcast_to(face_weights[0, 0][:, None], (iface, columns))
    rows_of = coarse_inverse.shape[1]
    tiles = (order + -order % LANES) // LANES
    inverse_rows = (rows_of + -rows_of % 8) * tiles
    mapping = None

    def coarse_step(coarse, mapping, hold=(), after=(), early=()):
        rows = len(near_order(chans)) * ncl
        kept, got = gathered(coarse, sub, hold, not hold, early)
        if mapping is None:
            mapping, own = call(
                functools.partial(coarse_first, chans, order, sub, ncl),
                (wide(rows, sub * ncl), wide(rows)),
                (coarse_number, kept, got),
                scratch=(
                    pltpu.VMEM((inverse_rows // tiles * sub, tiles * LANES), jnp.float32),
                    pltpu.VMEM((sub * ncl, 8), jnp.float32),
                    pltpu.VMEM((sub * ncl, 8), jnp.float32),
                    pltpu.VMEM((sub * ncl, columns), jnp.float32),
                ),
                after=after,
            )
        else:
            own = call(coarse_values, wide(rows), (mapping, kept, got), after=after)
        known = own[0 : (1 + len(near)) * ncl]
        theirs = [swap(known, channel) for channel in far]
        beyond = []
        if len(far) > 1:
            beyond = [swap(theirs[1 - at][0:ncl], channel) for at, channel in enumerate(far)]
        return mapping, (own, *theirs, *beyond)

    def sums(sent, got):
        return call(functools.partial(summing, chans), wide(iface), (*sent, *got), flops=WEIGHT)

    for step in range(ITERS):
        start, last = step == 0, step + 1 == ITERS
        if start:
            weighted, *far_scaled = call(
                functools.partial(smoothing_first, chans, far),
                (half,) + far_plain,
                (neumann, weights, *parts, *gots),
                flops=flops,
            )
        else:
            early = (response,) if step == 1 else near_scaled[:1]
            mapping, values = coarse_step(coarse, mapping, hold=parts[:1], early=early)
            if step == 1:
                reach = [
                    call(
                        functools.partial(reaching, channel, around),
                        short(channel[3], 6 * around),
                        (response, got),
                        after=values[:1],
                    )
                    for channel, got in zip(chans, gots)
                ]
            known = (weights, ahead, spread, sums(parts, gots), *reach, *values)
            if last:
                state, weighted, coarse = call(
                    functools.partial(smoothing_last, chans, ncl),
                    (half, half, wide(ncl)),
                    (basis_across, *known),
                )
                far_scaled = call(
                    functools.partial(smoothing_rows, far),
                    far_plain,
                    (neumann, weights, weighted),
                    flops=flops,
                )
                near_scaled = call(
                    functools.partial(smoothing_rows, near),
                    near_plain,
                    (neumann, weights, weighted),
                    flops=flops,
                    after=far_scaled[:1],
                )
            else:
                state, weighted, *far_scaled = call(
                    functools.partial(smoothing_far, chans, far, ncl),
                    (half, half) + far_plain,
                    (neumann, *known),
                    flops=flops,
                )
        if not last:
            inverse = (coarse_inverse[0],) if start else ()
            coarse, *near_scaled = call(
                functools.partial(smoothing_sub, near),
                (wide(ncl + len(inverse) * inverse_rows),) + near_plain,
                (neumann, weights, weighted, basis_across, *inverse),
                flops=flops,
            )
        scaled = (*far_scaled, *near_scaled)
        scaled_gots = exchange(chans, scaled)
        behind, behind_rows = (), 0
        if start:
            width = around + -around % LANES
            spread, full = call(
                functools.partial(spreading, chans),
                (short(iface, 6 * ncl), short(iface, 2 * width)),
                (weights, basis_across, *gots),
                after=near_scaled[:1],
            )
            response, turned = call(
                responding, (wide(iface, width), wide(width, iface)), (schur, full), flops=2 * flops
            )
            behind, behind_rows = (turned,), around
        if not last:
            ahead, rounded, *parts = call(
                functools.partial(between, chans, around),
                (wide(iface), half) + tuple(wide(c[3] + c[3] // LANES * behind_rows) for c in chans),
                (schur, load, state, *scaled, *scaled_gots, *behind),
                flops=2 * flops,
            )
            gots = exchange(chans, parts)
    mapping, values = coarse_step(coarse, mapping, after=scaled_gots[len(far) :])
    out = call(
        functools.partial(closing, chans, ncl),
        half,
        (state, spread, sums(scaled, scaled_gots), *values),
    )
    return out[None, None]


def solution(mesh):
    return jax.shard_map(
        shards,
        mesh=mesh,
        in_specs=(
            P("grp", "sub", None, None),
            P("grp", "sub", None, None),
            P("grp", "sub", None),
            P("grp", "sub", None, None),
            P("grp", "sub", None),
            P("grp", None),
            P("grp", "sub", None, None),
            P("grp", "sub", None, None),
        ),
        out_specs=P("grp", "sub", None, None),
        check_vma=False,
    )
```

```python
import functools

import jax
import jax.numpy as jnp
from jax import lax
from jax.experimental import pallas as pl
from jax.experimental.pallas import tpu as pltpu
from jax.sharding import PartitionSpec as P

ITERS = 3
HIGHEST = lax.Precision.HIGHEST
EVEN, ODD, BOTH = range(3)
LANES = 128
PIECES = 8
WEIGHT = 4 * 10**9
MIB = 2**20
WHOLE = pl.BlockSpec(memory_space=pltpu.VMEM)
AWAY = pl.BlockSpec(memory_space=pltpu.HBM)
ANYWHERE = pl.BlockSpec(memory_space=pl.ANY)


def channels(grp, sub, face):
    found = []
    for axis, devices, base in (("grp", grp, 2 * face), ("sub", sub, 0)):
        if devices == 2:
            found.append((axis, BOTH, base, 2 * face))
        else:
            found += [(axis, ODD, base, face), (axis, EVEN, base, face)]
    return tuple(found)


def mate(kind, index, devices):
    if kind == BOTH:
        return 1 - index
    step = 1 - 2 * (index % 2)
    if kind == ODD:
        step = -step
    return (index + step + devices) % devices


def swap(array, channel):
    axis, kind = channel[:2]
    devices = lax.axis_size(axis)
    return lax.ppermute(array, axis, [(i, mate(kind, i, devices)) for i in range(devices)])


def exchange(chans, sends):
    return tuple(swap(send, channel) for channel, send in zip(chans, sends))


def first_row(channel):
    axis, kind, base, rows = channel
    if kind == BOTH:
        return base
    odd = lax.rem(lax.axis_index(axis), 2)
    return pl.multiple_of(base + (odd if kind == ODD else 1 - odd) * rows, rows)


def own_rows(channel):
    return pl.ds(first_row(channel), channel[3])


def row_blocks(channel):
    blocks = channel[3] // LANES
    for block in range(blocks):
        rows = pl.ds(pl.multiple_of(first_row(channel) + block * LANES, LANES), LANES)
        yield block, rows, (block + blocks // 2) % blocks if channel[1] == BOTH else block


def across(channel, got):
    rows = channel[3]
    if channel[1] == BOTH:
        return jnp.concatenate([got[rows // 2 : rows], got[0 : rows // 2]], axis=0)
    return got[0:rows]


def product(a, b):
    return jnp.dot(a, b, preferred_element_type=jnp.float32)


def split(values, axis):
    high = values.astype(jnp.bfloat16)
    low = (values - high.astype(jnp.float32)).astype(jnp.bfloat16)
    return jnp.concatenate([high, low, high], axis=axis)


def thrice(values):
    high = values.astype(jnp.bfloat16).astype(jnp.float32)
    return jnp.concatenate([high, high, values - high], axis=1).astype(jnp.bfloat16)


def call(body, outs, args, scratch=(), flops=0, away=0, after=(), grant=16 * MIB):
    moved = sum(a.size * a.dtype.itemsize for a in args)
    ahead = len(after)
    return pl.pallas_call(
        lambda *refs: body(*refs[ahead:]),
        out_shape=outs,
        in_specs=[ANYWHERE] * ahead + [AWAY] * away + [WHOLE] * (len(args) - away),
        out_specs=jax.tree.map(lambda _: WHOLE, outs),
        scratch_shapes=scratch,
        cost_estimate=pl.CostEstimate(flops=flops, bytes_accessed=moved, transcendentals=0),
        compiler_params=pltpu.CompilerParams(vmem_limit_bytes=grant),
    )(*after, *args)


class Values:
    def __init__(self, chans, ncl, near, far, second):
        self.chans, self.ncl = chans, ncl
        self.near, self.far, self.second = near, far, second
        self.order = near_order(chans)

    def at(self, *path):
        grp = [c for c in path if self.chans[c][0] == "grp"]
        sub = [c for c in path if self.chans[c][0] == "sub"]
        grp, sub = [[] if len(p) == 2 and p[0] == p[1] else p for p in (grp, sub)]
        if len(grp) == 2:
            return self.second[grp[0]][...]
        source = self.far[grp[0]] if grp else self.near
        place = self.order.index(tuple(sub)) * self.ncl
        return source[place : place + self.ncl]

    def around(self, *path):
        return [self.at(*path)] + [self.at(*path, c) for c in range(len(self.chans))]


def near_order(chans):
    kinds = [c for c, channel in enumerate(chans) if channel[0] == "sub"]
    return [()] + [(c,) for c in kinds] + [(c, d) for c in kinds for d in kinds if c != d]


def value_refs(chans, ncl, refs):
    far = sum(channel[0] == "grp" for channel in chans)
    second = far if far > 1 else 0
    values = Values(chans, ncl, refs[0], refs[1 : 1 + far], refs[1 + far : 1 + far + second])
    return values, refs[1 + far + second :]


def opening(chans, matrix, load, state, basis_across, *refs):
    sends, (rows, mine, now, basis, sems) = refs[:-5], refs[-5:]
    piece = matrix.shape[0] // PIECES
    order = [(at + PIECES // 2) % PIECES * piece for at in range(PIECES)]
    pairs = [(state, now), (load, mine)]
    pairs += [(matrix.at[pl.ds(at, piece)], rows.at[pl.ds(at, piece)]) for at in order]
    pairs.append((basis_across, basis))
    copies = [pltpu.make_async_copy(a, b, sems.at[i]) for i, (a, b) in enumerate(pairs)]
    for copy in copies:
        copy.start()
    first = 2 + PIECES // 2
    for copy in copies[:first]:
        copy.wait()
    waiting = copies[first:]
    for channel, send in zip(chans, sends):
        if channel[0] == "sub":
            while waiting:
                waiting.pop(0).wait()
        own = own_rows(channel)
        send[0 : channel[3]] = mine[own].astype(jnp.float32) - product(rows[own], now[...])
    ncl = basis.shape[0]
    for channel, send in zip(chans, sends):
        for block, columns, _ in row_blocks(channel):
            at = channel[3] + block * ncl
            send[at : at + ncl] = basis[:, columns].astype(jnp.float32)


def smooth(chans, weights, resid_on, weighted):
    for at, channel in enumerate(chans):
        own = own_rows(channel)
        weighted[own] = (weights[own] * resid_on(at, own)).astype(jnp.bfloat16)


def smoothing_near(chans, matrix, weights, weighted, sends):
    for channel, send in zip(chans, sends):
        own = own_rows(channel)
        send[...] = weights[own] * product(matrix[own], weighted[...])


def stash(*refs):
    count = len(refs) // 2
    for part, out in zip(refs[:count], refs[count:]):
        out[...] = part[0 : out.shape[0]]


def summing(chans, *refs):
    count = len(chans)
    parts, gots, out = refs[:count], refs[count : 2 * count], refs[2 * count]
    for channel, part, got in zip(chans, parts, gots):
        out[own_rows(channel)] = part[0 : channel[3]] + across(channel, got)


def smoothing_first(chans, far, matrix, weights, *refs):
    count = len(chans)
    parts, gots = refs[:count], refs[count : 2 * count]

    def resid_on(at, own):
        return parts[at][...] + across(chans[at], gots[at])

    smooth(chans, weights, resid_on, refs[2 * count])
    smoothing_near(far, matrix, weights, refs[2 * count], refs[2 * count + 1 :])


def correct(chans, ncl, weights, ahead, spread, summed, refs):
    reach = refs[: len(chans)]
    values, refs = value_refs(chans, ncl, refs[len(chans) :])
    state, weighted, rest = refs[0], refs[1], refs[2:]
    here = values.around()

    def resid_on(at, own):
        pair = jnp.concatenate([here[0], values.at(at)], axis=0)
        state[own] = (ahead[own] + product(spread[own], split(pair, 0))).astype(state.dtype)
        both = jnp.concatenate(here + values.around(at), axis=0)
        return summed[own] - product(reach[at][...], split(both, 0)[0 : 2 * both.shape[0]])

    smooth(chans, weights, resid_on, weighted)
    return weighted, rest


def smoothing_far(chans, far, ncl, matrix, weights, ahead, spread, summed, *refs):
    weighted, sends = correct(chans, ncl, weights, ahead, spread, summed, refs)
    smoothing_near(far, matrix, weights, weighted, sends)


def smoothing_last(chans, ncl, basis_across, weights, ahead, spread, summed, *refs):
    weighted, (coarse,) = correct(chans, ncl, weights, ahead, spread, summed, refs)
    coarse[...] = product(basis_across[...], weighted[...])


def smoothing_rows(chans, matrix, weights, weighted, *sends):
    smoothing_near(chans, matrix, weights, weighted, sends)


def smoothing_sub(near, matrix, weights, weighted, basis_across, *refs):
    inverse = refs[: -len(near) - 1]
    coarse, sends = refs[-len(near) - 1], refs[-len(near) :]
    ncl = basis_across.shape[0]
    coarse[0:ncl] = product(basis_across[...], weighted[...])
    for rows in inverse:
        padded = rows.shape[0] + -rows.shape[0] % 8
        coarse[ncl:] = jnp.zeros((coarse.shape[0] - ncl, coarse.shape[1]), jnp.float32)
        for at in range(0, rows.shape[1], LANES):
            start = ncl + at // LANES * padded
            columns = min(LANES, rows.shape[1] - at)
            coarse[start : start + rows.shape[0], 0:columns] = rows[:, at : at + columns]
    smoothing_near(near, matrix, weights, weighted, sends)


def spreading(chans, weights, basis_across, *refs):
    gots, thin, full = refs[:-2], refs[-2], refs[-1]
    ncl = basis_across.shape[0]
    width = full.shape[1] // 2
    for at, (channel, got) in enumerate(zip(chans, gots)):
        for _, own, block in row_blocks(channel):
            from_row = channel[3] + block * ncl
            weight = weights[own][:, 0:ncl]
            here = weight * basis_across[:, own].astype(jnp.float32).T
            there = (1.0 - weight) * got[from_row : from_row + ncl].T
            thin[own] = thrice(jnp.concatenate([here, there], axis=1))
            before = [jnp.zeros((LANES, at * ncl), jnp.float32)] if at else []
            behind = jnp.zeros((LANES, width - (at + 2) * ncl), jnp.float32)
            placed = jnp.concatenate([here, *before, there, behind], axis=1)
            high = placed.astype(jnp.bfloat16)
            full[own, 0:width] = high
            full[own, width:] = (placed - high.astype(jnp.float32)).astype(jnp.bfloat16)


def responding(matrix, full, out, turned):
    width = out.shape[1]
    both = product(matrix[...], full[...])
    out[...] = both[:, 0:width] + both[:, width:]
    for at in range(0, out.shape[0], LANES):
        turned[:, at : at + LANES] = out[at : at + LANES].T


def reaching(channel, count, response, got, out):
    for block, own, from_block in row_blocks(channel):
        at = channel[3] + from_block * count
        theirs = got[at : at + count].T
        both = jnp.concatenate([response[own][:, 0:count], theirs], axis=1)
        out[block * LANES : (block + 1) * LANES] = jnp.concatenate([both, both], axis=1).astype(jnp.bfloat16)


def joining(first, second, out):
    out[...] = jnp.concatenate([first[...], second[...]], axis=0)


def coarse_first(chans, order, sub, ncl, numbers, kept, got, out, values, *scratch):
    arranged, upright, relative, pieces = scratch
    index = lax.axis_index("sub")
    rows_of = order // sub
    padded = rows_of + -rows_of % 8
    stride = kept.shape[0] * 2 // sub
    upright[...] = jnp.broadcast_to(numbers[...].astype(jnp.float32), (8, numbers.shape[1])).T
    for block, origin in enumerate(origins(sub)):
        origin = jnp.bitwise_xor(index, origin)
        half = sub // 2
        source = kept if block < half else got
        at = (block % half) * stride
        pieces[block * ncl : (block + 1) * ncl] = source[at : at + ncl]
        to = pl.ds(pl.multiple_of(origin * padded, 8), padded)
        for tile in range(arranged.shape[1] // LANES):
            start = at + ncl + tile * padded
            arranged[to, tile * LANES : (tile + 1) * LANES] = source[start : start + padded]
        relative[block * ncl : (block + 1) * ncl] = upright[pl.ds(pl.multiple_of(origin * ncl, 8), ncl)]
    wanted = []
    for path in near_order(chans):
        place = index
        for c in path:
            place = mate(chans[c][1], place, sub)
        wanted.append(upright[pl.ds(pl.multiple_of(place * ncl, 8), ncl)])
    wanted = jnp.concatenate(wanted, axis=0)[:, 0:1].astype(jnp.int32)
    lane = lax.broadcasted_iota(jnp.int32, (wanted.shape[0], sub * padded), 1)
    inside = lane % padded
    held = jnp.where(inside < rows_of, (lane // padded) * rows_of + inside, -1)
    pick = jnp.where(wanted == held, 1.0, 0.0).astype(jnp.float32)
    chosen = jnp.dot(pick, arranged[...], precision=HIGHEST, preferred_element_type=jnp.float32)
    column = lax.broadcasted_iota(jnp.int32, (relative.shape[0], arranged.shape[1]), 1)
    place = jnp.where(relative[...][:, 0:1].astype(jnp.int32) == column, 1.0, 0.0).astype(jnp.float32)
    out[...] = lax.dot_general(
        chosen, place, (((1,), (1,)), ((), ())), precision=HIGHEST, preferred_element_type=jnp.float32
    )
    values[...] = jnp.dot(out[...], pieces[...], precision=HIGHEST, preferred_element_type=jnp.float32)


def coarse_values(mapping, kept, got, out):
    half = kept.shape[0]
    total = jnp.dot(mapping[:, 0:half], kept[...], precision=HIGHEST, preferred_element_type=jnp.float32)
    total += jnp.dot(mapping[:, half:], got[...], precision=HIGHEST, preferred_element_type=jnp.float32)
    out[...] = total


def between(chans, count, matrix, load, state, *refs):
    size = len(chans)
    parts, gots = refs[:size], refs[size : 2 * size]
    responses = refs[2 * size : -size - 2]
    ahead, rounded, sends = refs[-size - 2], refs[-size - 1], refs[-size:]
    for channel, part, got in zip(chans, parts, gots):
        own = own_rows(channel)
        ahead[own] = state[own].astype(jnp.float32) + part[...] + across(channel, got)
        rounded[own] = ahead[own].astype(rounded.dtype)
    for channel, send in zip(chans, sends):
        rows = channel[3]
        own = own_rows(channel)
        send[0:rows] = load[own].astype(jnp.float32) - product(matrix[own], rounded[...])
        for turned in responses:
            for block, columns, _ in row_blocks(channel):
                send[rows + block * count : rows + (block + 1) * count] = turned[0:count, columns]


def closing(chans, ncl, state, spread, summed, *refs):
    values, refs = value_refs(chans, ncl, refs)
    out = refs[0]
    for at, channel in enumerate(chans):
        own = own_rows(channel)
        pair = jnp.concatenate([values.at(), values.at(at)], axis=0)
        update = product(spread[own], split(pair, 0)) + summed[own]
        out[own] = (state[own].astype(jnp.float32) + update).astype(out.dtype)


def steps(sub):
    found, step = [], sub // 2
    while step:
        found.append(step)
        step //= 2
    return found


def origins(sub):
    found = [0]
    for step in steps(sub):
        found += [origin ^ step for origin in found]
    return found


def gathered(piece, sub, hold=(), wide=False, early=()):
    def hop(move):
        return lax.ppermute(piece, "sub", [(i, i ^ move) for i in range(sub)])

    moves = steps(sub)
    if wide:
        first, second, *moves = moves
        pieces = [piece] + [hop(move) for move in (first, second, first ^ second)]
        piece = jnp.concatenate(pieces, axis=0)
    for at, move in enumerate(moves[:-1]):
        got = hop(move)
        after = hold if at + 1 == len(moves) // 2 else early if at == 0 else ()
        if after:
            joined = jax.ShapeDtypeStruct((2 * piece.shape[0], piece.shape[1]), piece.dtype)
            piece = call(joining, joined, (piece, got), after=after, flops=0 if after is hold else WEIGHT // 2)
        else:
            piece = jnp.concatenate([piece, got], axis=0)
    return piece, hop(moves[-1])


def shards(
    schur_t, neumann_t, face_weights, coarse_basis, coarse_inverse, coarse_number, loads, iterate
):
    schur, neumann = schur_t[0, 0], neumann_t[0, 0]
    basis_across = coarse_basis[0, 0].T
    load, state = loads[0, 0], iterate[0, 0]
    iface, columns = state.shape
    ncl = basis_across.shape[0]
    face = iface // 4
    grp, sub = lax.axis_size("grp"), lax.axis_size("sub")
    chans = channels(grp, sub, face)
    far = tuple(c for c in chans if c[0] == "grp")
    near = chans[len(far) :]
    around = (len(chans) + 1) * ncl
    order = coarse_inverse.shape[2]

    def wide(rows, width=columns):
        return jax.ShapeDtypeStruct((rows, width), jnp.float32)

    def short(rows, width=columns):
        return jax.ShapeDtypeStruct((rows, width), jnp.bfloat16)

    far_plain, near_plain = [tuple(wide(c[3]) for c in group) for group in (far, near)]
    half = short(iface)
    flops = iface * iface * columns

    parts = call(
        functools.partial(opening, chans),
        tuple(wide(c[3] + c[3] // LANES * ncl) for c in chans),
        (schur, load, state, basis_across),
        scratch=(
            pltpu.VMEM(schur.shape, schur.dtype),
            pltpu.VMEM(load.shape, load.dtype),
            pltpu.VMEM(state.shape, state.dtype),
            pltpu.VMEM(basis_across.shape, basis_across.dtype),
            pltpu.SemaphoreType.DMA((3 + PIECES,)),
        ),
        flops=2 * flops,
        away=4,
        grant=56 * MIB,
    )
    gots = exchange(chans, parts)
    parts = call(stash, far_plain + near_plain, tuple(parts))

    weights = jnp.broadcast_to(face_weights[0, 0][:, None], (iface, columns))
    rows_of = coarse_inverse.shape[1]
    tiles = (order + -order % LANES) // LANES
    inverse_rows = (rows_of + -rows_of % 8) * tiles
    mapping = None

    def coarse_step(coarse, mapping, hold=(), after=(), early=()):
        rows = len(near_order(chans)) * ncl
        kept, got = gathered(coarse, sub, hold, not hold, early)
        if mapping is None:
            mapping, own = call(
                functools.partial(coarse_first, chans, order, sub, ncl),
                (wide(rows, sub * ncl), wide(rows)),
                (coarse_number, kept, got),
                scratch=(
                    pltpu.VMEM((inverse_rows // tiles * sub, tiles * LANES), jnp.float32),
                    pltpu.VMEM((sub * ncl, 8), jnp.float32),
                    pltpu.VMEM((sub * ncl, 8), jnp.float32),
                    pltpu.VMEM((sub * ncl, columns), jnp.float32),
                ),
                after=after,
            )
        else:
            own = call(coarse_values, wide(rows), (mapping, kept, got), after=after)
        known = own[0 : (1 + len(near)) * ncl]
        theirs = [swap(known, channel) for channel in far]
        beyond = []
        if len(far) > 1:
            beyond = [swap(theirs[1 - at][0:ncl], channel) for at, channel in enumerate(far)]
        return mapping, (own, *theirs, *beyond)

    def sums(sent, got):
        return call(functools.partial(summing, chans), wide(iface), (*sent, *got), flops=WEIGHT)

    for step in range(ITERS):
        start, last = step == 0, step + 1 == ITERS
        if start:
            weighted, *far_scaled = call(
                functools.partial(smoothing_first, chans, far),
                (half,) + far_plain,
                (neumann, weights, *parts, *gots),
                flops=flops,
            )
        else:
            early = (response,) if step == 1 else near_scaled[:1]
            mapping, values = coarse_step(coarse, mapping, hold=parts[:1], early=early)
            if step == 1:
                reach = [
                    call(
                        functools.partial(reaching, channel, around),
                        short(channel[3], 4 * around),
                        (response, got),
                        after=values[:1],
                    )
                    for channel, got in zip(chans, gots)
                ]
            known = (weights, ahead, spread, sums(parts, gots), *reach, *values)
            if last:
                state, weighted, coarse = call(
                    functools.partial(smoothing_last, chans, ncl),
                    (half, half, wide(ncl)),
                    (basis_across, *known),
                )
                far_scaled = call(
                    functools.partial(smoothing_rows, far),
                    far_plain,
                    (neumann, weights, weighted),
                    flops=flops,
                )
                near_scaled = call(
                    functools.partial(smoothing_rows, near),
                    near_plain,
                    (neumann, weights, weighted),
                    flops=flops,
                    after=far_scaled[:1],
                )
            else:
                state, weighted, *far_scaled = call(
                    functools.partial(smoothing_far, chans, far, ncl),
                    (half, half) + far_plain,
                    (neumann, *known),
                    flops=flops,
                )
        if not last:
            inverse = (coarse_inverse[0],) if start else ()
            coarse, *near_scaled = call(
                functools.partial(smoothing_sub, near),
                (wide(ncl + len(inverse) * inverse_rows),) + near_plain,
                (neumann, weights, weighted, basis_across, *inverse),
                flops=flops,
            )
        scaled = (*far_scaled, *near_scaled)
        scaled_gots = exchange(chans, scaled)
        behind, behind_rows = (), 0
        if start:
            width = around + -around % LANES
            spread, full = call(
                functools.partial(spreading, chans),
                (short(iface, 6 * ncl), short(iface, 2 * width)),
                (weights, basis_across, *gots),
                after=near_scaled[:1],
            )
            response, turned = call(
                responding, (wide(iface, width), wide(width, iface)), (schur, full), flops=2 * flops
            )
            behind, behind_rows = (turned,), around
        if not last:
            ahead, rounded, *parts = call(
                functools.partial(between, chans, around),
                (wide(iface), half) + tuple(wide(c[3] + c[3] // LANES * behind_rows) for c in chans),
                (schur, load, state, *scaled, *scaled_gots, *behind),
                flops=2 * flops,
            )
            gots = exchange(chans, parts)
    mapping, values = coarse_step(coarse, mapping, after=scaled_gots[len(far) :])
    out = call(
        functools.partial(closing, chans, ncl),
        half,
        (state, spread, sums(scaled, scaled_gots), *values),
    )
    return out[None, None]


def solution(mesh):
    return jax.shard_map(
        shards,
        mesh=mesh,
        in_specs=(
            P("grp", "sub", None, None),
            P("grp", "sub", None, None),
            P("grp", "sub", None),
            P("grp", "sub", None, None),
            P("grp", "sub", None),
            P("grp", None),
            P("grp", "sub", None, None),
            P("grp", "sub", None, None),
        ),
        out_specs=P("grp", "sub", None, None),
        check_vma=False,
    )
```

```python
import functools

import jax
import jax.numpy as jnp
from jax import lax
from jax.experimental import pallas as pl
from jax.experimental.pallas import tpu as pltpu
from jax.sharding import PartitionSpec as P

ITERS = 3
HIGHEST = lax.Precision.HIGHEST
EVEN, ODD, BOTH = range(3)
LANES = 128
PIECES = 8
WEIGHT = 4 * 10**9
MIB = 2**20
WHOLE = pl.BlockSpec(memory_space=pltpu.VMEM)
AWAY = pl.BlockSpec(memory_space=pltpu.HBM)
ANYWHERE = pl.BlockSpec(memory_space=pl.ANY)


def channels(grp, sub, face):
    found = []
    for axis, devices, base in (("grp", grp, 2 * face), ("sub", sub, 0)):
        if devices == 2:
            found.append((axis, BOTH, base, 2 * face))
        else:
            found += [(axis, ODD, base, face), (axis, EVEN, base, face)]
    return tuple(found)


def mate(kind, index, devices):
    if kind == BOTH:
        return 1 - index
    step = 1 - 2 * (index % 2)
    if kind == ODD:
        step = -step
    return (index + step + devices) % devices


def swap(array, channel):
    axis, kind = channel[:2]
    devices = lax.axis_size(axis)
    return lax.ppermute(array, axis, [(i, mate(kind, i, devices)) for i in range(devices)])


def exchange(chans, sends):
    return tuple(swap(send, channel) for channel, send in zip(chans, sends))


def first_row(channel):
    axis, kind, base, rows = channel
    if kind == BOTH:
        return base
    odd = lax.rem(lax.axis_index(axis), 2)
    return pl.multiple_of(base + (odd if kind == ODD else 1 - odd) * rows, rows)


def own_rows(channel):
    return pl.ds(first_row(channel), channel[3])


def row_blocks(channel):
    blocks = channel[3] // LANES
    for block in range(blocks):
        rows = pl.ds(pl.multiple_of(first_row(channel) + block * LANES, LANES), LANES)
        yield block, rows, (block + blocks // 2) % blocks if channel[1] == BOTH else block


def across(channel, got):
    rows = channel[3]
    if channel[1] == BOTH:
        return jnp.concatenate([got[rows // 2 : rows], got[0 : rows // 2]], axis=0)
    return got[0:rows]


def product(a, b):
    return jnp.dot(a, b, preferred_element_type=jnp.float32)


def split(values, axis):
    high = values.astype(jnp.bfloat16)
    low = (values - high.astype(jnp.float32)).astype(jnp.bfloat16)
    return jnp.concatenate([high, low, high], axis=axis)


def thrice(values):
    high = values.astype(jnp.bfloat16).astype(jnp.float32)
    return jnp.concatenate([high, high, values - high], axis=1).astype(jnp.bfloat16)


def call(body, outs, args, scratch=(), flops=0, away=0, after=(), grant=16 * MIB):
    moved = sum(a.size * a.dtype.itemsize for a in args)
    ahead = len(after)
    return pl.pallas_call(
        lambda *refs: body(*refs[ahead:]),
        out_shape=outs,
        in_specs=[ANYWHERE] * ahead + [AWAY] * away + [WHOLE] * (len(args) - away),
        out_specs=jax.tree.map(lambda _: WHOLE, outs),
        scratch_shapes=scratch,
        cost_estimate=pl.CostEstimate(flops=flops, bytes_accessed=moved, transcendentals=0),
        compiler_params=pltpu.CompilerParams(vmem_limit_bytes=grant),
    )(*after, *args)


class Values:
    def __init__(self, chans, ncl, near, far, second):
        self.chans, self.ncl = chans, ncl
        self.near, self.far, self.second = near, far, second
        self.order = near_order(chans)

    def at(self, *path):
        grp = [c for c in path if self.chans[c][0] == "grp"]
        sub = [c for c in path if self.chans[c][0] == "sub"]
        grp, sub = [[] if len(p) == 2 and p[0] == p[1] else p for p in (grp, sub)]
        if len(grp) == 2:
            return self.second[grp[0]][...]
        source = self.far[grp[0]] if grp else self.near
        place = self.order.index(tuple(sub)) * self.ncl
        return source[place : place + self.ncl]

    def around(self, *path):
        return [self.at(*path)] + [self.at(*path, c) for c in range(len(self.chans))]


def near_order(chans):
    kinds = [c for c, channel in enumerate(chans) if channel[0] == "sub"]
    return [()] + [(c,) for c in kinds] + [(c, d) for c in kinds for d in kinds if c != d]


def value_refs(chans, ncl, refs):
    far = sum(channel[0] == "grp" for channel in chans)
    second = far if far > 1 else 0
    values = Values(chans, ncl, refs[0], refs[1 : 1 + far], refs[1 + far : 1 + far + second])
    return values, refs[1 + far + second :]


def opening(chans, matrix, load, state, basis_across, *refs):
    sends, (rows, mine, now, basis, sems) = refs[:-5], refs[-5:]
    piece = matrix.shape[0] // PIECES
    order = [(at + PIECES // 2) % PIECES * piece for at in range(PIECES)]
    pairs = [(state, now), (load, mine)]
    pairs += [(matrix.at[pl.ds(at, piece)], rows.at[pl.ds(at, piece)]) for at in order]
    pairs.append((basis_across, basis))
    copies = [pltpu.make_async_copy(a, b, sems.at[i]) for i, (a, b) in enumerate(pairs)]
    for copy in copies:
        copy.start()
    first = 2 + PIECES // 2
    for copy in copies[:first]:
        copy.wait()
    waiting = copies[first:]
    for channel, send in zip(chans, sends):
        if channel[0] == "sub":
            while waiting:
                waiting.pop(0).wait()
        own = own_rows(channel)
        send[0 : channel[3]] = mine[own].astype(jnp.float32) - product(rows[own], now[...])
    ncl = basis.shape[0]
    for channel, send in zip(chans, sends):
        for block, columns, _ in row_blocks(channel):
            at = channel[3] + block * ncl
            send[at : at + ncl] = basis[:, columns].astype(jnp.float32)


def smooth(chans, weights, resid_on, weighted):
    for at, channel in enumerate(chans):
        own = own_rows(channel)
        weighted[own] = (weights[own] * resid_on(at, own)).astype(jnp.bfloat16)


def smoothing_near(chans, matrix, weights, weighted, sends):
    for channel, send in zip(chans, sends):
        own = own_rows(channel)
        send[...] = weights[own] * product(matrix[own], weighted[...])


def stash(*refs):
    count = len(refs) // 2
    for part, out in zip(refs[:count], refs[count:]):
        out[...] = part[0 : out.shape[0]]


def summing(chans, *refs):
    count = len(chans)
    parts, gots, out = refs[:count], refs[count : 2 * count], refs[2 * count]
    for channel, part, got in zip(chans, parts, gots):
        out[own_rows(channel)] = part[0 : channel[3]] + across(channel, got)


def smoothing_first(chans, far, matrix, weights, *refs):
    count = len(chans)
    parts, gots = refs[:count], refs[count : 2 * count]

    def resid_on(at, own):
        return parts[at][...] + across(chans[at], gots[at])

    smooth(chans, weights, resid_on, refs[2 * count])
    smoothing_near(far, matrix, weights, refs[2 * count], refs[2 * count + 1 :])


def correct(chans, ncl, weights, ahead, spread, summed, refs):
    reach = refs[: len(chans)]
    values, refs = value_refs(chans, ncl, refs[len(chans) :])
    state, weighted, rest = refs[0], refs[1], refs[2:]
    here = values.around()

    def resid_on(at, own):
        pair = jnp.concatenate([here[0], values.at(at)], axis=0)
        state[own] = (ahead[own] + product(spread[own], split(pair, 0))).astype(state.dtype)
        both = jnp.concatenate(here + values.around(at), axis=0)
        return summed[own] - product(reach[at][...], split(both, 0)[0 : 2 * both.shape[0]])

    smooth(chans, weights, resid_on, weighted)
    return weighted, rest


def smoothing_far(chans, far, ncl, matrix, weights, ahead, spread, summed, *refs):
    weighted, sends = correct(chans, ncl, weights, ahead, spread, summed, refs)
    smoothing_near(far, matrix, weights, weighted, sends)


def smoothing_last(chans, ncl, basis_across, weights, ahead, spread, summed, *refs):
    weighted, (coarse,) = correct(chans, ncl, weights, ahead, spread, summed, refs)
    coarse[...] = product(basis_across[...], weighted[...])


def smoothing_rows(chans, matrix, weights, weighted, *sends):
    smoothing_near(chans, matrix, weights, weighted, sends)


def smoothing_sub(near, matrix, weights, weighted, basis_across, *refs):
    inverse = refs[: -len(near) - 1]
    coarse, sends = refs[-len(near) - 1], refs[-len(near) :]
    ncl = basis_across.shape[0]
    coarse[0:ncl] = product(basis_across[...], weighted[...])
    for rows in inverse:
        padded = rows.shape[0] + -rows.shape[0] % 8
        coarse[ncl:] = jnp.zeros((coarse.shape[0] - ncl, coarse.shape[1]), jnp.float32)
        for at in range(0, rows.shape[1], LANES):
            start = ncl + at // LANES * padded
            columns = min(LANES, rows.shape[1] - at)
            coarse[start : start + rows.shape[0], 0:columns] = rows[:, at : at + columns]
    smoothing_near(near, matrix, weights, weighted, sends)


def spreading(chans, weights, basis_across, *refs):
    gots, thin, full = refs[:-2], refs[-2], refs[-1]
    ncl = basis_across.shape[0]
    width = full.shape[1] // 2
    for at, (channel, got) in enumerate(zip(chans, gots)):
        for _, own, block in row_blocks(channel):
            from_row = channel[3] + block * ncl
            weight = weights[own][:, 0:ncl]
            here = weight * basis_across[:, own].astype(jnp.float32).T
            there = (1.0 - weight) * got[from_row : from_row + ncl].T
            thin[own] = thrice(jnp.concatenate([here, there], axis=1))
            before = [jnp.zeros((LANES, at * ncl), jnp.float32)] if at else []
            behind = jnp.zeros((LANES, width - (at + 2) * ncl), jnp.float32)
            placed = jnp.concatenate([here, *before, there, behind], axis=1)
            high = placed.astype(jnp.bfloat16)
            full[own, 0:width] = high
            full[own, width:] = (placed - high.astype(jnp.float32)).astype(jnp.bfloat16)


def responding(matrix, full, out, turned):
    width = out.shape[1]
    both = product(matrix[...], full[...])
    out[...] = both[:, 0:width] + both[:, width:]
    for at in range(0, out.shape[0], LANES):
        turned[:, at : at + LANES] = out[at : at + LANES].T


def reaching(channel, count, response, got, out):
    for block, own, from_block in row_blocks(channel):
        at = channel[3] + from_block * count
        theirs = got[at : at + count].T
        both = jnp.concatenate([response[own][:, 0:count], theirs], axis=1)
        out[block * LANES : (block + 1) * LANES] = jnp.concatenate([both, both], axis=1).astype(jnp.bfloat16)


def joining(first, second, out):
    out[...] = jnp.concatenate([first[...], second[...]], axis=0)


def coarse_first(chans, order, sub, ncl, numbers, kept, got, out, values, *scratch):
    arranged, upright, relative, pieces = scratch
    index = lax.axis_index("sub")
    rows_of = order // sub
    padded = rows_of + -rows_of % 8
    stride = kept.shape[0] * 2 // sub
    upright[...] = jnp.broadcast_to(numbers[...].astype(jnp.float32), (8, numbers.shape[1])).T
    for block, origin in enumerate(origins(sub)):
        origin = jnp.bitwise_xor(index, origin)
        half = sub // 2
        source = kept if block < half else got
        at = (block % half) * stride
        pieces[block * ncl : (block + 1) * ncl] = source[at : at + ncl]
        to = pl.ds(pl.multiple_of(origin * padded, 8), padded)
        for tile in range(arranged.shape[1] // LANES):
            start = at + ncl + tile * padded
            arranged[to, tile * LANES : (tile + 1) * LANES] = source[start : start + padded]
        relative[block * ncl : (block + 1) * ncl] = upright[pl.ds(pl.multiple_of(origin * ncl, 8), ncl)]
    wanted = []
    for path in near_order(chans):
        place = index
        for c in path:
            place = mate(chans[c][1], place, sub)
        wanted.append(upright[pl.ds(pl.multiple_of(place * ncl, 8), ncl)])
    wanted = jnp.concatenate(wanted, axis=0)[:, 0:1].astype(jnp.int32)
    lane = lax.broadcasted_iota(jnp.int32, (wanted.shape[0], sub * padded), 1)
    inside = lane % padded
    held = jnp.where(inside < rows_of, (lane // padded) * rows_of + inside, -1)
    pick = jnp.where(wanted == held, 1.0, 0.0).astype(jnp.float32)
    chosen = jnp.dot(pick, arranged[...], precision=HIGHEST, preferred_element_type=jnp.float32)
    column = lax.broadcasted_iota(jnp.int32, (relative.shape[0], arranged.shape[1]), 1)
    place = jnp.where(relative[...][:, 0:1].astype(jnp.int32) == column, 1.0, 0.0).astype(jnp.float32)
    out[...] = lax.dot_general(
        chosen, place, (((1,), (1,)), ((), ())), precision=HIGHEST, preferred_element_type=jnp.float32
    )
    values[...] = jnp.dot(out[...], pieces[...], precision=HIGHEST, preferred_element_type=jnp.float32)


def coarse_values(mapping, kept, got, out):
    half = kept.shape[0]
    total = jnp.dot(mapping[:, 0:half], kept[...], precision=HIGHEST, preferred_element_type=jnp.float32)
    total += jnp.dot(mapping[:, half:], got[...], precision=HIGHEST, preferred_element_type=jnp.float32)
    out[...] = total


def between(chans, count, matrix, load, state, *refs):
    size = len(chans)
    parts, gots = refs[:size], refs[size : 2 * size]
    responses = refs[2 * size : -size - 2]
    ahead, rounded, sends = refs[-size - 2], refs[-size - 1], refs[-size:]
    for channel, part, got in zip(chans, parts, gots):
        own = own_rows(channel)
        ahead[own] = state[own].astype(jnp.float32) + part[...] + across(channel, got)
        rounded[own] = ahead[own].astype(rounded.dtype)
    for channel, send in zip(chans, sends):
        rows = channel[3]
        own = own_rows(channel)
        send[0:rows] = load[own].astype(jnp.float32) - product(matrix[own], rounded[...])
        for turned in responses:
            for block, columns, _ in row_blocks(channel):
                send[rows + block * count : rows + (block + 1) * count] = turned[0:count, columns]


def closing(chans, ncl, state, spread, summed, *refs):
    values, refs = value_refs(chans, ncl, refs)
    out = refs[0]
    for at, channel in enumerate(chans):
        own = own_rows(channel)
        pair = jnp.concatenate([values.at(), values.at(at)], axis=0)
        update = product(spread[own], split(pair, 0)) + summed[own]
        out[own] = (state[own].astype(jnp.float32) + update).astype(out.dtype)


def steps(sub):
    found, step = [], sub // 2
    while step:
        found.append(step)
        step //= 2
    return found


def origins(sub):
    found = [0]
    for step in steps(sub):
        found += [origin ^ step for origin in found]
    return found


def gathered(piece, sub, hold=(), wide=False, early=()):
    def hop(move):
        return lax.ppermute(piece, "sub", [(i, i ^ move) for i in range(sub)])

    moves = steps(sub)
    if wide:
        first, second, *moves = moves
        pieces = [piece] + [hop(move) for move in (first, second, first ^ second)]
        piece = jnp.concatenate(pieces, axis=0)
    for at, move in enumerate(moves[:-1]):
        got = hop(move)
        after = hold if at + 1 == len(moves) // 2 else early if at == 0 else ()
        if after:
            joined = jax.ShapeDtypeStruct((2 * piece.shape[0], piece.shape[1]), piece.dtype)
            piece = call(joining, joined, (piece, got), after=after, flops=0 if after is hold else WEIGHT // 2)
        else:
            piece = jnp.concatenate([piece, got], axis=0)
    return piece, hop(moves[-1])


def shards(
    schur_t, neumann_t, face_weights, coarse_basis, coarse_inverse, coarse_number, loads, iterate
):
    schur, neumann = schur_t[0, 0], neumann_t[0, 0]
    basis_across = coarse_basis[0, 0].T
    load, state = loads[0, 0], iterate[0, 0]
    iface, columns = state.shape
    ncl = basis_across.shape[0]
    face = iface // 4
    grp, sub = lax.axis_size("grp"), lax.axis_size("sub")
    chans = channels(grp, sub, face)
    far = tuple(c for c in chans if c[0] == "grp")
    near = chans[len(far) :]
    around = (len(chans) + 1) * ncl
    order = coarse_inverse.shape[2]

    def wide(rows, width=columns):
        return jax.ShapeDtypeStruct((rows, width), jnp.float32)

    def short(rows, width=columns):
        return jax.ShapeDtypeStruct((rows, width), jnp.bfloat16)

    far_plain, near_plain = [tuple(wide(c[3]) for c in group) for group in (far, near)]
    half = short(iface)
    flops = iface * iface * columns

    parts = call(
        functools.partial(opening, chans),
        tuple(wide(c[3] + c[3] // LANES * ncl) for c in chans),
        (schur, load, state, basis_across),
        scratch=(
            pltpu.VMEM(schur.shape, schur.dtype),
            pltpu.VMEM(load.shape, load.dtype),
            pltpu.VMEM(state.shape, state.dtype),
            pltpu.VMEM(basis_across.shape, basis_across.dtype),
            pltpu.SemaphoreType.DMA((3 + PIECES,)),
        ),
        flops=2 * flops,
        away=4,
        grant=56 * MIB,
    )
    gots = exchange(chans, parts)
    parts = call(stash, far_plain + near_plain, tuple(parts))

    weights = jnp.broadcast_to(face_weights[0, 0][:, None], (iface, columns))
    rows_of = coarse_inverse.shape[1]
    tiles = (order + -order % LANES) // LANES
    inverse_rows = (rows_of + -rows_of % 8) * tiles
    mapping = None

    def coarse_step(coarse, mapping, hold=(), after=(), early=()):
        rows = len(near_order(chans)) * ncl
        kept, got = gathered(coarse, sub, hold, False, early)
        if mapping is None:
            mapping, own = call(
                functools.partial(coarse_first, chans, order, sub, ncl),
                (wide(rows, sub * ncl), wide(rows)),
                (coarse_number, kept, got),
                scratch=(
                    pltpu.VMEM((inverse_rows // tiles * sub, tiles * LANES), jnp.float32),
                    pltpu.VMEM((sub * ncl, 8), jnp.float32),
                    pltpu.VMEM((sub * ncl, 8), jnp.float32),
                    pltpu.VMEM((sub * ncl, columns), jnp.float32),
                ),
                after=after,
            )
        else:
            own = call(coarse_values, wide(rows), (mapping, kept, got), after=after)
        known = own[0 : (1 + len(near)) * ncl]
        theirs = [swap(known, channel) for channel in far]
        beyond = []
        if len(far) > 1:
            beyond = [swap(theirs[1 - at][0:ncl], channel) for at, channel in enumerate(far)]
        return mapping, (own, *theirs, *beyond)

    def sums(sent, got):
        return call(functools.partial(summing, chans), wide(iface), (*sent, *got), flops=WEIGHT)

    for step in range(ITERS):
        start, last = step == 0, step + 1 == ITERS
        if start:
            weighted, *far_scaled = call(
                functools.partial(smoothing_first, chans, far),
                (half,) + far_plain,
                (neumann, weights, *parts, *gots),
                flops=flops,
            )
        else:
            early = (response,) if step == 1 else near_scaled[:1]
            mapping, values = coarse_step(coarse, mapping, hold=parts[:1], early=early)
            if step == 1:
                reach = [
                    call(
                        functools.partial(reaching, channel, around),
                        short(channel[3], 4 * around),
                        (response, got),
                        after=values[:1],
                    )
                    for channel, got in zip(chans, gots)
                ]
            known = (weights, ahead, spread, sums(parts, gots), *reach, *values)
            if last:
                state, weighted, coarse = call(
                    functools.partial(smoothing_last, chans, ncl),
                    (half, half, wide(ncl)),
                    (basis_across, *known),
                )
                far_scaled = call(
                    functools.partial(smoothing_rows, far),
                    far_plain,
                    (neumann, weights, weighted),
                    flops=flops,
                )
                near_scaled = call(
                    functools.partial(smoothing_rows, near),
                    near_plain,
                    (neumann, weights, weighted),
                    flops=flops,
                    after=far_scaled[:1],
                )
            else:
                state, weighted, *far_scaled = call(
                    functools.partial(smoothing_far, chans, far, ncl),
                    (half, half) + far_plain,
                    (neumann, *known),
                    flops=flops,
                )
        if not last:
            inverse = (coarse_inverse[0],) if start else ()
            coarse, *near_scaled = call(
                functools.partial(smoothing_sub, near),
                (wide(ncl + len(inverse) * inverse_rows),) + near_plain,
                (neumann, weights, weighted, basis_across, *inverse),
                flops=flops,
            )
        scaled = (*far_scaled, *near_scaled)
        scaled_gots = exchange(chans, scaled)
        behind, behind_rows = (), 0
        if start:
            width = around + -around % LANES
            spread, full = call(
                functools.partial(spreading, chans),
                (short(iface, 6 * ncl), short(iface, 2 * width)),
                (weights, basis_across, *gots),
                after=near_scaled[:1],
            )
            response, turned = call(
                responding, (wide(iface, width), wide(width, iface)), (schur, full), flops=2 * flops
            )
            behind, behind_rows = (turned,), around
        if not last:
            ahead, rounded, *parts = call(
                functools.partial(between, chans, around),
                (wide(iface), half) + tuple(wide(c[3] + c[3] // LANES * behind_rows) for c in chans),
                (schur, load, state, *scaled, *scaled_gots, *behind),
                flops=2 * flops,
            )
            gots = exchange(chans, parts)
    mapping, values = coarse_step(coarse, mapping, after=scaled_gots[len(far) :])
    out = call(
        functools.partial(closing, chans, ncl),
        half,
        (state, spread, sums(scaled, scaled_gots), *values),
    )
    return out[None, None]


def solution(mesh):
    return jax.shard_map(
        shards,
        mesh=mesh,
        in_specs=(
            P("grp", "sub", None, None),
            P("grp", "sub", None, None),
            P("grp", "sub", None),
            P("grp", "sub", None, None),
            P("grp", "sub", None),
            P("grp", None),
            P("grp", "sub", None, None),
            P("grp", "sub", None, None),
        ),
        out_specs=P("grp", "sub", None, None),
        check_vma=False,
    )
```

```python
import functools

import jax
import jax.numpy as jnp
from jax import lax
from jax.experimental import pallas as pl
from jax.experimental.pallas import tpu as pltpu
from jax.sharding import PartitionSpec as P

ITERS = 3
HIGHEST = lax.Precision.HIGHEST
EVEN, ODD, BOTH = range(3)
LANES = 128
PIECES = 8
WEIGHT = 4 * 10**9
MIB = 2**20
WHOLE = pl.BlockSpec(memory_space=pltpu.VMEM)
AWAY = pl.BlockSpec(memory_space=pltpu.HBM)
ANYWHERE = pl.BlockSpec(memory_space=pl.ANY)


def channels(grp, sub, face):
    found = []
    for axis, devices, base in (("grp", grp, 2 * face), ("sub", sub, 0)):
        if devices == 2:
            found.append((axis, BOTH, base, 2 * face))
        else:
            found += [(axis, ODD, base, face), (axis, EVEN, base, face)]
    return tuple(found)


def mate(kind, index, devices):
    if kind == BOTH:
        return 1 - index
    step = 1 - 2 * (index % 2)
    if kind == ODD:
        step = -step
    return (index + step + devices) % devices


def swap(array, channel):
    axis, kind = channel[:2]
    devices = lax.axis_size(axis)
    return lax.ppermute(array, axis, [(i, mate(kind, i, devices)) for i in range(devices)])


def exchange(chans, sends):
    return tuple(swap(send, channel) for channel, send in zip(chans, sends))


def first_row(channel):
    axis, kind, base, rows = channel
    if kind == BOTH:
        return base
    odd = lax.rem(lax.axis_index(axis), 2)
    return pl.multiple_of(base + (odd if kind == ODD else 1 - odd) * rows, rows)


def own_rows(channel):
    return pl.ds(first_row(channel), channel[3])


def row_blocks(channel):
    blocks = channel[3] // LANES
    for block in range(blocks):
        rows = pl.ds(pl.multiple_of(first_row(channel) + block * LANES, LANES), LANES)
        yield block, rows, (block + blocks // 2) % blocks if channel[1] == BOTH else block


def across(channel, got):
    rows = channel[3]
    if channel[1] == BOTH:
        return jnp.concatenate([got[rows // 2 : rows], got[0 : rows // 2]], axis=0)
    return got[0:rows]


def product(a, b):
    return jnp.dot(a, b, preferred_element_type=jnp.float32)


def split(values, axis):
    high = values.astype(jnp.bfloat16)
    low = (values - high.astype(jnp.float32)).astype(jnp.bfloat16)
    return jnp.concatenate([high, low, high], axis=axis)


def thrice(values):
    high = values.astype(jnp.bfloat16).astype(jnp.float32)
    return jnp.concatenate([high, high, values - high], axis=1).astype(jnp.bfloat16)


def call(body, outs, args, scratch=(), flops=0, away=0, after=(), grant=16 * MIB, out=WHOLE):
    moved = sum(a.size * a.dtype.itemsize for a in args)
    ahead = len(after)
    return pl.pallas_call(
        lambda *refs: body(*refs[ahead:]),
        out_shape=outs,
        in_specs=[ANYWHERE] * ahead + [AWAY] * away + [WHOLE] * (len(args) - away),
        out_specs=jax.tree.map(lambda _: out, outs),
        scratch_shapes=scratch,
        cost_estimate=pl.CostEstimate(flops=flops, bytes_accessed=moved, transcendentals=0),
        compiler_params=pltpu.CompilerParams(vmem_limit_bytes=grant),
    )(*after, *args)


class Values:
    def __init__(self, chans, ncl, near, far, second):
        self.chans, self.ncl = chans, ncl
        self.near, self.far, self.second = near, far, second
        self.order = near_order(chans)

    def at(self, *path):
        grp = [c for c in path if self.chans[c][0] == "grp"]
        sub = [c for c in path if self.chans[c][0] == "sub"]
        grp, sub = [[] if len(p) == 2 and p[0] == p[1] else p for p in (grp, sub)]
        if len(grp) == 2:
            return self.second[grp[0]][...]
        source = self.far[grp[0]] if grp else self.near
        place = self.order.index(tuple(sub)) * self.ncl
        return source[place : place + self.ncl]

    def around(self, *path):
        return [self.at(*path)] + [self.at(*path, c) for c in range(len(self.chans))]


def near_order(chans):
    kinds = [c for c, channel in enumerate(chans) if channel[0] == "sub"]
    return [()] + [(c,) for c in kinds] + [(c, d) for c in kinds for d in kinds if c != d]


def value_refs(chans, ncl, refs):
    far = sum(channel[0] == "grp" for channel in chans)
    second = far if far > 1 else 0
    values = Values(chans, ncl, refs[0], refs[1 : 1 + far], refs[1 + far : 1 + far + second])
    return values, refs[1 + far + second :]


def opening(chans, matrix, load, state, basis_across, *refs):
    count = len(chans)
    outs, (rows, mine, now, basis, sems), sends = refs[:count], refs[count : count + 5], refs[count + 5 :]
    piece = matrix.shape[0] // PIECES
    order = [(at + PIECES // 2) % PIECES * piece for at in range(PIECES)]
    pairs = [(state, now), (load, mine), (basis_across, basis)]
    pairs += [(matrix.at[pl.ds(at, piece)], rows.at[pl.ds(at, piece)]) for at in order]
    copies = [pltpu.make_async_copy(a, b, sems.at[i]) for i, (a, b) in enumerate(pairs)]
    for copy in copies:
        copy.start()
    first = 3 + PIECES // 2
    for copy in copies[:first]:
        copy.wait()
    waiting = copies[first:]
    ncl = basis.shape[0]
    written = []
    for at, (channel, send, out) in enumerate(zip(chans, sends, outs)):
        if channel[0] == "sub":
            while waiting:
                waiting.pop(0).wait()
        own = own_rows(channel)
        send[0 : channel[3]] = mine[own].astype(jnp.float32) - product(rows[own], now[...])
        for block, columns, _ in row_blocks(channel):
            start = channel[3] + block * ncl
            send[start : start + ncl] = basis[:, columns].astype(jnp.float32)
        written.append(pltpu.make_async_copy(send, out, sems.at[len(pairs) + at]))
        written[-1].start()
    for copy in written:
        copy.wait()


def smooth(chans, weights, resid_on, weighted):
    for at, channel in enumerate(chans):
        own = own_rows(channel)
        weighted[own] = (weights[own] * resid_on(at, own)).astype(jnp.bfloat16)


def smoothing_near(chans, matrix, weights, weighted, sends):
    for channel, send in zip(chans, sends):
        own = own_rows(channel)
        send[...] = weights[own] * product(matrix[own], weighted[...])


def stash(*refs):
    count = len(refs) // 2
    for part, out in zip(refs[:count], refs[count:]):
        out[...] = part[0 : out.shape[0]]


def summing(chans, *refs):
    count = len(chans)
    parts, gots, out = refs[:count], refs[count : 2 * count], refs[2 * count]
    for channel, part, got in zip(chans, parts, gots):
        out[own_rows(channel)] = part[0 : channel[3]] + across(channel, got)


def smoothing_first(chans, far, matrix, weights, *refs):
    count = len(chans)
    parts, gots = refs[:count], refs[count : 2 * count]

    def resid_on(at, own):
        return parts[at][...] + across(chans[at], gots[at])

    smooth(chans, weights, resid_on, refs[2 * count])
    smoothing_near(far, matrix, weights, refs[2 * count], refs[2 * count + 1 :])


def correct(chans, ncl, weights, ahead, spread, summed, refs):
    reach = refs[: len(chans)]
    values, refs = value_refs(chans, ncl, refs[len(chans) :])
    state, weighted, rest = refs[0], refs[1], refs[2:]
    here = values.around()

    def resid_on(at, own):
        pair = jnp.concatenate([here[0], values.at(at)], axis=0)
        state[own] = (ahead[own] + product(spread[own], split(pair, 0))).astype(state.dtype)
        both = jnp.concatenate(here + values.around(at), axis=0)
        return summed[own] - product(reach[at][...], split(both, 0)[0 : 2 * both.shape[0]])

    smooth(chans, weights, resid_on, weighted)
    return weighted, rest


def smoothing_far(chans, far, ncl, matrix, weights, ahead, spread, summed, *refs):
    weighted, sends = correct(chans, ncl, weights, ahead, spread, summed, refs)
    smoothing_near(far, matrix, weights, weighted, sends)


def smoothing_last(chans, ncl, basis_across, weights, ahead, spread, summed, *refs):
    weighted, (coarse,) = correct(chans, ncl, weights, ahead, spread, summed, refs)
    coarse[...] = product(basis_across[...], weighted[...])


def smoothing_rows(chans, matrix, weights, weighted, *sends):
    smoothing_near(chans, matrix, weights, weighted, sends)


def smoothing_sub(near, matrix, weights, weighted, basis_across, *refs):
    inverse = refs[: -len(near) - 1]
    coarse, sends = refs[-len(near) - 1], refs[-len(near) :]
    ncl = basis_across.shape[0]
    coarse[0:ncl] = product(basis_across[...], weighted[...])
    for rows in inverse:
        padded = rows.shape[0] + -rows.shape[0] % 8
        coarse[ncl:] = jnp.zeros((coarse.shape[0] - ncl, coarse.shape[1]), jnp.float32)
        for at in range(0, rows.shape[1], LANES):
            start = ncl + at // LANES * padded
            columns = min(LANES, rows.shape[1] - at)
            coarse[start : start + rows.shape[0], 0:columns] = rows[:, at : at + columns]
    smoothing_near(near, matrix, weights, weighted, sends)


def spreading(chans, weights, basis_across, *refs):
    gots, thin, full = refs[:-2], refs[-2], refs[-1]
    ncl = basis_across.shape[0]
    width = full.shape[1] // 2
    for at, (channel, got) in enumerate(zip(chans, gots)):
        for _, own, block in row_blocks(channel):
            from_row = channel[3] + block * ncl
            weight = weights[own][:, 0:ncl]
            here = weight * basis_across[:, own].astype(jnp.float32).T
            there = (1.0 - weight) * got[from_row : from_row + ncl].T
            thin[own] = thrice(jnp.concatenate([here, there], axis=1))
            before = [jnp.zeros((LANES, at * ncl), jnp.float32)] if at else []
            behind = jnp.zeros((LANES, width - (at + 2) * ncl), jnp.float32)
            placed = jnp.concatenate([here, *before, there, behind], axis=1)
            high = placed.astype(jnp.bfloat16)
            full[own, 0:width] = high
            full[own, width:] = (placed - high.astype(jnp.float32)).astype(jnp.bfloat16)


def responding(matrix, full, out, turned):
    width = out.shape[1]
    both = product(matrix[...], full[...])
    out[...] = both[:, 0:width] + both[:, width:]
    for at in range(0, out.shape[0], LANES):
        turned[:, at : at + LANES] = out[at : at + LANES].T


def reaching(channel, count, response, got, out):
    for block, own, from_block in row_blocks(channel):
        at = channel[3] + from_block * count
        theirs = got[at : at + count].T
        both = jnp.concatenate([response[own][:, 0:count], theirs], axis=1)
        out[block * LANES : (block + 1) * LANES] = jnp.concatenate([both, both], axis=1).astype(jnp.bfloat16)


def joining(first, second, out):
    out[...] = jnp.concatenate([first[...], second[...]], axis=0)


def coarse_first(chans, order, sub, ncl, numbers, kept, got, out, values, *scratch):
    arranged, upright, relative, pieces = scratch
    index = lax.axis_index("sub")
    rows_of = order // sub
    padded = rows_of + -rows_of % 8
    stride = kept.shape[0] * 2 // sub
    upright[...] = jnp.broadcast_to(numbers[...].astype(jnp.float32), (8, numbers.shape[1])).T
    for block, origin in enumerate(origins(sub)):
        origin = jnp.bitwise_xor(index, origin)
        half = sub // 2
        source = kept if block < half else got
        at = (block % half) * stride
        pieces[block * ncl : (block + 1) * ncl] = source[at : at + ncl]
        to = pl.ds(pl.multiple_of(origin * padded, 8), padded)
        for tile in range(arranged.shape[1] // LANES):
            start = at + ncl + tile * padded
            arranged[to, tile * LANES : (tile + 1) * LANES] = source[start : start + padded]
        relative[block * ncl : (block + 1) * ncl] = upright[pl.ds(pl.multiple_of(origin * ncl, 8), ncl)]
    wanted = []
    for path in near_order(chans):
        place = index
        for c in path:
            place = mate(chans[c][1], place, sub)
        wanted.append(upright[pl.ds(pl.multiple_of(place * ncl, 8), ncl)])
    wanted = jnp.concatenate(wanted, axis=0)[:, 0:1].astype(jnp.int32)
    lane = lax.broadcasted_iota(jnp.int32, (wanted.shape[0], sub * padded), 1)
    inside = lane % padded
    held = jnp.where(inside < rows_of, (lane // padded) * rows_of + inside, -1)
    pick = jnp.where(wanted == held, 1.0, 0.0).astype(jnp.float32)
    chosen = jnp.dot(pick, arranged[...], precision=HIGHEST, preferred_element_type=jnp.float32)
    column = lax.broadcasted_iota(jnp.int32, (relative.shape[0], arranged.shape[1]), 1)
    place = jnp.where(relative[...][:, 0:1].astype(jnp.int32) == column, 1.0, 0.0).astype(jnp.float32)
    out[...] = lax.dot_general(
        chosen, place, (((1,), (1,)), ((), ())), precision=HIGHEST, preferred_element_type=jnp.float32
    )
    values[...] = jnp.dot(out[...], pieces[...], precision=HIGHEST, preferred_element_type=jnp.float32)


def coarse_values(mapping, kept, got, out):
    half = kept.shape[0]
    total = jnp.dot(mapping[:, 0:half], kept[...], precision=HIGHEST, preferred_element_type=jnp.float32)
    total += jnp.dot(mapping[:, half:], got[...], precision=HIGHEST, preferred_element_type=jnp.float32)
    out[...] = total


def between_far(chans, far, count, matrix, load, state, *refs):
    size = len(chans)
    parts, gots = refs[:size], refs[size : 2 * size]
    turned = refs[2 * size : -len(far) - 2]
    ahead, rounded, sends = refs[-len(far) - 2], refs[-len(far) - 1], refs[-len(far) :]
    for channel, part, got in zip(chans, parts, gots):
        own = own_rows(channel)
        ahead[own] = state[own].astype(jnp.float32) + part[...] + across(channel, got)
        rounded[own] = ahead[own].astype(rounded.dtype)
    between_near(far, count, matrix, load, rounded, *turned, *sends)


def between_near(chans, count, matrix, load, state, *refs):
    sends = refs[-len(chans) :]
    for channel, send in zip(chans, sends):
        rows = channel[3]
        own = own_rows(channel)
        send[0:rows] = load[own].astype(jnp.float32) - product(matrix[own], state[...])
        for turned in refs[: -len(chans)]:
            for block, columns, _ in row_blocks(channel):
                send[rows + block * count : rows + (block + 1) * count] = turned[0:count, columns]


def landing(chans, ncl, state, spread, near_values, *refs):
    count = len(chans)
    parts, gots, out = refs[:count], refs[count : 2 * count], refs[2 * count]
    values = Values(chans, ncl, near_values, (), ())
    for at, channel in enumerate(chans):
        own = own_rows(channel)
        theirs = values.at(at) if channel[0] == "sub" else jnp.zeros((ncl, state.shape[1]), jnp.float32)
        update = product(spread[own], split(jnp.concatenate([values.at(), theirs], axis=0), 0))
        update += parts[at][...] + across(channel, gots[at])
        out[own] = state[own].astype(jnp.float32) + update


def closing(chans, ncl, spread, landed, *refs):
    values, (out,) = value_refs(chans, ncl, refs)
    for at, channel in enumerate(chans):
        own = own_rows(channel)
        last = landed[own]
        if channel[0] == "grp":
            theirs = values.at(at)
            pair = jnp.concatenate([jnp.zeros_like(theirs), theirs], axis=0)
            last += product(spread[own], split(pair, 0))
        out[own] = last.astype(out.dtype)


def steps(sub):
    found, step = [], sub // 2
    while step:
        found.append(step)
        step //= 2
    return found


def origins(sub):
    found = [0]
    for step in steps(sub):
        found += [origin ^ step for origin in found]
    return found


def gathered(piece, sub, hold=(), wide=False, early=()):
    def hop(move):
        return lax.ppermute(piece, "sub", [(i, i ^ move) for i in range(sub)])

    moves = steps(sub)
    if wide:
        first, second, *moves = moves
        pieces = [piece] + [hop(move) for move in (first, second, first ^ second)]
        piece = jnp.concatenate(pieces, axis=0)
    for at, move in enumerate(moves[:-1]):
        got = hop(move)
        after = hold if at + 1 == len(moves) // 2 else early if at == 0 else ()
        if after:
            joined = jax.ShapeDtypeStruct((2 * piece.shape[0], piece.shape[1]), piece.dtype)
            piece = call(joining, joined, (piece, got), after=after, flops=0 if after is hold else WEIGHT // 2)
        else:
            piece = jnp.concatenate([piece, got], axis=0)
    return piece, hop(moves[-1])


def shards(
    schur_t, neumann_t, face_weights, coarse_basis, coarse_inverse, coarse_number, loads, iterate
):
    schur, neumann = schur_t[0, 0], neumann_t[0, 0]
    basis_across = coarse_basis[0, 0].T
    load, state = loads[0, 0], iterate[0, 0]
    iface, columns = state.shape
    ncl = basis_across.shape[0]
    face = iface // 4
    grp, sub = lax.axis_size("grp"), lax.axis_size("sub")
    chans = channels(grp, sub, face)
    far = tuple(c for c in chans if c[0] == "grp")
    near = chans[len(far) :]
    around = (len(chans) + 1) * ncl
    order = coarse_inverse.shape[2]

    def wide(rows, width=columns):
        return jax.ShapeDtypeStruct((rows, width), jnp.float32)

    def short(rows, width=columns):
        return jax.ShapeDtypeStruct((rows, width), jnp.bfloat16)

    far_plain, near_plain = [tuple(wide(c[3]) for c in group) for group in (far, near)]
    half = short(iface)
    flops = iface * iface * columns

    parts = call(
        functools.partial(opening, chans),
        tuple(wide(c[3] + c[3] // LANES * ncl) for c in chans),
        (schur, load, state, basis_across),
        scratch=(
            pltpu.VMEM(schur.shape, schur.dtype),
            pltpu.VMEM(load.shape, load.dtype),
            pltpu.VMEM(state.shape, state.dtype),
            pltpu.VMEM(basis_across.shape, basis_across.dtype),
            pltpu.SemaphoreType.DMA((3 + PIECES + len(chans),)),
            *(pltpu.VMEM((c[3] + c[3] // LANES * ncl, columns), jnp.float32) for c in chans),
        ),
        flops=2 * flops,
        away=4,
        grant=56 * MIB,
        out=AWAY,
    )
    gots = exchange(chans, parts)
    parts = call(stash, far_plain + near_plain, tuple(parts))

    weights = jnp.broadcast_to(face_weights[0, 0][:, None], (iface, columns))
    rows_of = coarse_inverse.shape[1]
    tiles = (order + -order % LANES) // LANES
    inverse_rows = (rows_of + -rows_of % 8) * tiles
    mapping = None

    def coarse_step(coarse, mapping, hold=(), after=(), early=(), sent=1 + len(near)):
        rows = len(near_order(chans)) * ncl
        kept, got = gathered(coarse, sub, hold, False, early)
        if mapping is None:
            mapping, own = call(
                functools.partial(coarse_first, chans, order, sub, ncl),
                (wide(rows, sub * ncl), wide(rows)),
                (coarse_number, kept, got),
                scratch=(
                    pltpu.VMEM((inverse_rows // tiles * sub, tiles * LANES), jnp.float32),
                    pltpu.VMEM((sub * ncl, 8), jnp.float32),
                    pltpu.VMEM((sub * ncl, 8), jnp.float32),
                    pltpu.VMEM((sub * ncl, columns), jnp.float32),
                ),
                after=after,
            )
        else:
            own = call(coarse_values, wide(rows), (mapping, kept, got), after=after)
        known = own[0 : sent * ncl]
        theirs = [swap(known, channel) for channel in far]
        beyond = []
        if len(far) > 1:
            beyond = [swap(theirs[1 - at][0:ncl], channel) for at, channel in enumerate(far)]
        return mapping, (own, *theirs, *beyond)

    def sums(sent, got):
        return call(functools.partial(summing, chans), wide(iface), (*sent, *got), flops=WEIGHT)

    for step in range(ITERS):
        start, last = step == 0, step + 1 == ITERS
        if start:
            weighted, *far_scaled = call(
                functools.partial(smoothing_first, chans, far),
                (half,) + far_plain,
                (neumann, weights, *parts, *gots),
                flops=flops,
            )
        else:
            early = (response,) if step == 1 else near_scaled[:1]
            mapping, values = coarse_step(coarse, mapping, hold=far_parts[:1], early=early)
            if step == 1:
                reach = [
                    call(
                        functools.partial(reaching, channel, around),
                        short(channel[3], 4 * around),
                        (response, got),
                        after=values[:1],
                    )
                    for channel, got in zip(chans, gots)
                ]
            known = (weights, ahead, spread, sums(parts, gots), *reach, *values)
            if last:
                state, weighted, coarse = call(
                    functools.partial(smoothing_last, chans, ncl),
                    (half, half, wide(ncl)),
                    (basis_across, *known),
                )
                far_scaled = call(
                    functools.partial(smoothing_rows, far),
                    far_plain,
                    (neumann, weights, weighted),
                    flops=flops,
                )
                near_scaled = call(
                    functools.partial(smoothing_rows, near),
                    near_plain,
                    (neumann, weights, weighted),
                    flops=flops,
                    after=far_scaled[:1],
                )
            else:
                state, weighted, *far_scaled = call(
                    functools.partial(smoothing_far, chans, far, ncl),
                    (half, half) + far_plain,
                    (neumann, *known),
                    flops=flops,
                )
        if not last:
            inverse = (coarse_inverse[0],) if start else ()
            coarse, *near_scaled = call(
                functools.partial(smoothing_sub, near),
                (wide(ncl + len(inverse) * inverse_rows),) + near_plain,
                (neumann, weights, weighted, basis_across, *inverse),
                flops=flops,
            )
        scaled = (*far_scaled, *near_scaled)
        scaled_gots = exchange(chans, scaled)
        behind, behind_rows = (), 0
        if start:
            width = around + -around % LANES
            spread, full = call(
                functools.partial(spreading, chans),
                (short(iface, 6 * ncl), short(iface, 2 * width)),
                (weights, basis_across, *gots),
                after=near_scaled[:1],
            )
            response, turned = call(
                responding, (wide(iface, width), wide(width, iface)), (schur, full), flops=2 * flops
            )
            behind, behind_rows = (turned,), around
        if not last:
            far_outs, near_outs = [
                tuple(wide(c[3] + c[3] // LANES * behind_rows) for c in group) for group in (far, near)
            ]
            ahead, rounded, *far_parts = call(
                functools.partial(between_far, chans, far, around),
                (wide(iface), half) + far_outs,
                (schur, load, state, *scaled, *scaled_gots, *behind),
                flops=flops,
            )
            near_parts = call(
                functools.partial(between_near, near, around),
                near_outs,
                (schur, load, rounded, *behind),
                flops=flops,
                after=far_parts[:1],
            )
            parts = (*far_parts, *near_parts)
            gots = exchange(chans, parts)
    mapping, values = coarse_step(coarse, mapping, after=scaled_gots[len(far) :], sent=1)
    landed = call(
        functools.partial(landing, chans, ncl),
        wide(iface),
        (state, spread, values[0], *scaled, *scaled_gots),
        flops=WEIGHT,
    )
    out = call(functools.partial(closing, chans, ncl), half, (spread, landed, *values))
    return out[None, None]


def solution(mesh):
    return jax.shard_map(
        shards,
        mesh=mesh,
        in_specs=(
            P("grp", "sub", None, None),
            P("grp", "sub", None, None),
            P("grp", "sub", None),
            P("grp", "sub", None, None),
            P("grp", "sub", None),
            P("grp", None),
            P("grp", "sub", None, None),
            P("grp", "sub", None, None),
        ),
        out_specs=P("grp", "sub", None, None),
        check_vma=False,
    )
```

```python
import functools

import jax
import jax.numpy as jnp
from jax import lax
from jax.experimental import pallas as pl
from jax.experimental.pallas import tpu as pltpu
from jax.sharding import PartitionSpec as P

ITERS = 3
HIGHEST = lax.Precision.HIGHEST
EVEN, ODD, BOTH = range(3)
LANES = 128
PIECES = 8
WEIGHT = 4 * 10**9
MIB = 2**20
WHOLE = pl.BlockSpec(memory_space=pltpu.VMEM)
AWAY = pl.BlockSpec(memory_space=pltpu.HBM)
ANYWHERE = pl.BlockSpec(memory_space=pl.ANY)


def channels(grp, sub, face):
    found = []
    for axis, devices, base in (("grp", grp, 2 * face), ("sub", sub, 0)):
        if devices == 2:
            found.append((axis, BOTH, base, 2 * face))
        else:
            found += [(axis, ODD, base, face), (axis, EVEN, base, face)]
    return tuple(found)


def mate(kind, index, devices):
    if kind == BOTH:
        return 1 - index
    step = 1 - 2 * (index % 2)
    if kind == ODD:
        step = -step
    return (index + step + devices) % devices


def swap(array, channel):
    axis, kind = channel[:2]
    devices = lax.axis_size(axis)
    return lax.ppermute(array, axis, [(i, mate(kind, i, devices)) for i in range(devices)])


def exchange(chans, sends):
    return tuple(swap(send, channel) for channel, send in zip(chans, sends))


def first_row(channel):
    axis, kind, base, rows = channel
    if kind == BOTH:
        return base
    odd = lax.rem(lax.axis_index(axis), 2)
    return pl.multiple_of(base + (odd if kind == ODD else 1 - odd) * rows, rows)


def own_rows(channel):
    return pl.ds(first_row(channel), channel[3])


def row_blocks(channel):
    blocks = channel[3] // LANES
    for block in range(blocks):
        rows = pl.ds(pl.multiple_of(first_row(channel) + block * LANES, LANES), LANES)
        yield block, rows, (block + blocks // 2) % blocks if channel[1] == BOTH else block


def across(channel, got):
    rows = channel[3]
    if channel[1] == BOTH:
        return jnp.concatenate([got[rows // 2 : rows], got[0 : rows // 2]], axis=0)
    return got[0:rows]


def product(a, b):
    return jnp.dot(a, b, preferred_element_type=jnp.float32)


def split(values, axis):
    high = values.astype(jnp.bfloat16)
    low = (values - high.astype(jnp.float32)).astype(jnp.bfloat16)
    return jnp.concatenate([high, low, high], axis=axis)


def thrice(values):
    high = values.astype(jnp.bfloat16).astype(jnp.float32)
    return jnp.concatenate([high, high, values - high], axis=1).astype(jnp.bfloat16)


def call(body, outs, args, scratch=(), flops=0, away=0, after=(), grant=16 * MIB, out=WHOLE):
    moved = sum(a.size * a.dtype.itemsize for a in args)
    ahead = len(after)
    return pl.pallas_call(
        lambda *refs: body(*refs[ahead:]),
        out_shape=outs,
        in_specs=[ANYWHERE] * ahead + [AWAY] * away + [WHOLE] * (len(args) - away),
        out_specs=jax.tree.map(lambda _: out, outs),
        scratch_shapes=scratch,
        cost_estimate=pl.CostEstimate(flops=flops, bytes_accessed=moved, transcendentals=0),
        compiler_params=pltpu.CompilerParams(vmem_limit_bytes=grant),
    )(*after, *args)


class Values:
    def __init__(self, chans, ncl, near, far, second):
        self.chans, self.ncl = chans, ncl
        self.near, self.far, self.second = near, far, second
        self.order = near_order(chans)

    def at(self, *path):
        grp = [c for c in path if self.chans[c][0] == "grp"]
        sub = [c for c in path if self.chans[c][0] == "sub"]
        grp, sub = [[] if len(p) == 2 and p[0] == p[1] else p for p in (grp, sub)]
        if len(grp) == 2:
            return self.second[grp[0]][...]
        source = self.far[grp[0]] if grp else self.near
        place = self.order.index(tuple(sub)) * self.ncl
        return source[place : place + self.ncl]

    def around(self, *path):
        return [self.at(*path)] + [self.at(*path, c) for c in range(len(self.chans))]


def near_order(chans):
    kinds = [c for c, channel in enumerate(chans) if channel[0] == "sub"]
    return [()] + [(c,) for c in kinds] + [(c, d) for c in kinds for d in kinds if c != d]


def value_refs(chans, ncl, refs):
    far = sum(channel[0] == "grp" for channel in chans)
    second = far if far > 1 else 0
    values = Values(chans, ncl, refs[0], refs[1 : 1 + far], refs[1 + far : 1 + far + second])
    return values, refs[1 + far + second :]


def opening(chans, matrix, load, state, basis_across, *refs):
    count = len(refs) // 2 - 2
    outs, (rows, mine, now, basis, sems), sends = refs[:count], refs[count : count + 5], refs[count + 5 :]
    piece = matrix.shape[0] // PIECES
    order = [(at + PIECES // 2) % PIECES * piece for at in range(PIECES)]
    pairs = [(state, now), (load, mine), (basis_across, basis)]
    pairs += [(matrix.at[pl.ds(at, piece)], rows.at[pl.ds(at, piece)]) for at in order]
    copies = [pltpu.make_async_copy(a, b, sems.at[i]) for i, (a, b) in enumerate(pairs)]
    for copy in copies:
        copy.start()
    first = 3 + PIECES // 2
    for copy in copies[:first]:
        copy.wait()
    waiting = copies[first:]
    written = []

    def write(send):
        at = len(written)
        written.append(pltpu.make_async_copy(send, outs[at], sems.at[len(pairs) + at]))
        written[-1].start()

    for channel, send in zip(chans, sends):
        if channel[0] == "sub":
            while waiting:
                waiting.pop(0).wait()
        own = own_rows(channel)
        send[0 : channel[3]] = mine[own].astype(jnp.float32) - product(rows[own], now[...])
        if channel[0] == "sub":
            basis_on(channel, basis, send, channel[3])
        write(send)
    for channel, send in zip(chans, sends[len(chans) :]):
        basis_on(channel, basis, send, 0)
        write(send)
    for copy in written:
        copy.wait()


def basis_on(channel, basis, send, start):
    ncl = basis.shape[0]
    for block, columns, _ in row_blocks(channel):
        at = start + block * ncl
        send[at : at + ncl] = basis[:, columns].astype(jnp.float32)


def smooth(chans, weights, resid_on, weighted):
    for at, channel in enumerate(chans):
        own = own_rows(channel)
        weighted[own] = (weights[own] * resid_on(at, own)).astype(jnp.bfloat16)


def smoothing_near(chans, matrix, weights, weighted, sends):
    for channel, send in zip(chans, sends):
        own = own_rows(channel)
        send[...] = weights[own] * product(matrix[own], weighted[...])


def stash(*refs):
    count = len(refs) // 2
    for part, out in zip(refs[:count], refs[count:]):
        out[...] = part[0 : out.shape[0]]


def summing(chans, *refs):
    count = len(chans)
    parts, gots, out = refs[:count], refs[count : 2 * count], refs[2 * count]
    for channel, part, got in zip(chans, parts, gots):
        out[own_rows(channel)] = part[0 : channel[3]] + across(channel, got)


def smoothing_first(chans, far, matrix, weights, *refs):
    count = len(chans)
    parts, gots = refs[:count], refs[count : 2 * count]

    def resid_on(at, own):
        return parts[at][...] + across(chans[at], gots[at])

    smooth(chans, weights, resid_on, refs[2 * count])
    smoothing_near(far, matrix, weights, refs[2 * count], refs[2 * count + 1 :])


def correct(chans, ncl, weights, ahead, spread, summed, refs):
    reach = refs[: len(chans)]
    values, refs = value_refs(chans, ncl, refs[len(chans) :])
    state, weighted, rest = refs[0], refs[1], refs[2:]
    here = values.around()

    def resid_on(at, own):
        pair = jnp.concatenate([here[0], values.at(at)], axis=0)
        state[own] = (ahead[own] + product(spread[own], split(pair, 0))).astype(state.dtype)
        both = jnp.concatenate(here + values.around(at), axis=0)
        return summed[own] - product(reach[at][...], split(both, 0)[0 : 2 * both.shape[0]])

    smooth(chans, weights, resid_on, weighted)
    return weighted, rest


def smoothing_far(chans, far, ncl, matrix, weights, ahead, spread, summed, *refs):
    weighted, sends = correct(chans, ncl, weights, ahead, spread, summed, refs)
    smoothing_near(far, matrix, weights, weighted, sends)


def smoothing_last(chans, ncl, basis_across, weights, ahead, spread, summed, *refs):
    weighted, (coarse,) = correct(chans, ncl, weights, ahead, spread, summed, refs)
    coarse[...] = product(basis_across[...], weighted[...])


def smoothing_rows(chans, matrix, weights, weighted, *sends):
    smoothing_near(chans, matrix, weights, weighted, sends)


def smoothing_sub(near, matrix, weights, weighted, basis_across, *refs):
    inverse = refs[: -len(near) - 1]
    coarse, sends = refs[-len(near) - 1], refs[-len(near) :]
    ncl = basis_across.shape[0]
    coarse[0:ncl] = product(basis_across[...], weighted[...])
    for rows in inverse:
        padded = rows.shape[0] + -rows.shape[0] % 8
        coarse[ncl:] = jnp.zeros((coarse.shape[0] - ncl, coarse.shape[1]), jnp.float32)
        for at in range(0, rows.shape[1], LANES):
            start = ncl + at // LANES * padded
            columns = min(LANES, rows.shape[1] - at)
            coarse[start : start + rows.shape[0], 0:columns] = rows[:, at : at + columns]
    smoothing_near(near, matrix, weights, weighted, sends)


def spreading(chans, weights, basis_across, *refs):
    gots, thin, full = refs[:-2], refs[-2], refs[-1]
    ncl = basis_across.shape[0]
    width = full.shape[1] // 2
    for at, (channel, got) in enumerate(zip(chans, gots)):
        for _, own, block in row_blocks(channel):
            from_row = block * ncl + (channel[3] if channel[0] == "sub" else 0)
            weight = weights[own][:, 0:ncl]
            here = weight * basis_across[:, own].astype(jnp.float32).T
            there = (1.0 - weight) * got[from_row : from_row + ncl].T
            thin[own] = thrice(jnp.concatenate([here, there], axis=1))
            before = [jnp.zeros((LANES, at * ncl), jnp.float32)] if at else []
            behind = jnp.zeros((LANES, width - (at + 2) * ncl), jnp.float32)
            placed = jnp.concatenate([here, *before, there, behind], axis=1)
            high = placed.astype(jnp.bfloat16)
            full[own, 0:width] = high
            full[own, width:] = (placed - high.astype(jnp.float32)).astype(jnp.bfloat16)


def responding(matrix, full, out, turned):
    width = out.shape[1]
    both = product(matrix[...], full[...])
    out[...] = both[:, 0:width] + both[:, width:]
    for at in range(0, out.shape[0], LANES):
        turned[:, at : at + LANES] = out[at : at + LANES].T


def reaching(channel, count, response, got, out):
    for block, own, from_block in row_blocks(channel):
        at = channel[3] + from_block * count
        theirs = got[at : at + count].T
        both = jnp.concatenate([response[own][:, 0:count], theirs], axis=1)
        out[block * LANES : (block + 1) * LANES] = jnp.concatenate([both, both], axis=1).astype(jnp.bfloat16)


def joining(first, second, out):
    out[...] = jnp.concatenate([first[...], second[...]], axis=0)


def coarse_first(chans, order, sub, ncl, numbers, kept, got, out, values, *scratch):
    arranged, upright, relative, pieces = scratch
    index = lax.axis_index("sub")
    rows_of = order // sub
    padded = rows_of + -rows_of % 8
    stride = kept.shape[0] * 2 // sub
    upright[...] = jnp.broadcast_to(numbers[...].astype(jnp.float32), (8, numbers.shape[1])).T
    for block, origin in enumerate(origins(sub)):
        origin = jnp.bitwise_xor(index, origin)
        half = sub // 2
        source = kept if block < half else got
        at = (block % half) * stride
        pieces[block * ncl : (block + 1) * ncl] = source[at : at + ncl]
        to = pl.ds(pl.multiple_of(origin * padded, 8), padded)
        for tile in range(arranged.shape[1] // LANES):
            start = at + ncl + tile * padded
            arranged[to, tile * LANES : (tile + 1) * LANES] = source[start : start + padded]
        relative[block * ncl : (block + 1) * ncl] = upright[pl.ds(pl.multiple_of(origin * ncl, 8), ncl)]
    wanted = []
    for path in near_order(chans):
        place = index
        for c in path:
            place = mate(chans[c][1], place, sub)
        wanted.append(upright[pl.ds(pl.multiple_of(place * ncl, 8), ncl)])
    wanted = jnp.concatenate(wanted, axis=0)[:, 0:1].astype(jnp.int32)
    lane = lax.broadcasted_iota(jnp.int32, (wanted.shape[0], sub * padded), 1)
    inside = lane % padded
    held = jnp.where(inside < rows_of, (lane // padded) * rows_of + inside, -1)
    pick = jnp.where(wanted == held, 1.0, 0.0).astype(jnp.float32)
    chosen = jnp.dot(pick, arranged[...], precision=HIGHEST, preferred_element_type=jnp.float32)
    column = lax.broadcasted_iota(jnp.int32, (relative.shape[0], arranged.shape[1]), 1)
    place = jnp.where(relative[...][:, 0:1].astype(jnp.int32) == column, 1.0, 0.0).astype(jnp.float32)
    out[...] = lax.dot_general(
        chosen, place, (((1,), (1,)), ((), ())), precision=HIGHEST, preferred_element_type=jnp.float32
    )
    values[...] = jnp.dot(out[...], pieces[...], precision=HIGHEST, preferred_element_type=jnp.float32)


def coarse_values(mapping, kept, got, out):
    half = kept.shape[0]
    total = jnp.dot(mapping[:, 0:half], kept[...], precision=HIGHEST, preferred_element_type=jnp.float32)
    total += jnp.dot(mapping[:, half:], got[...], precision=HIGHEST, preferred_element_type=jnp.float32)
    out[...] = total


def between_far(chans, far, count, matrix, load, state, *refs):
    size = len(chans)
    parts, gots = refs[:size], refs[size : 2 * size]
    turned = refs[2 * size : -len(far) - 2]
    ahead, rounded, sends = refs[-len(far) - 2], refs[-len(far) - 1], refs[-len(far) :]
    for channel, part, got in zip(chans, parts, gots):
        own = own_rows(channel)
        ahead[own] = state[own].astype(jnp.float32) + part[...] + across(channel, got)
        rounded[own] = ahead[own].astype(rounded.dtype)
    between_near(far, count, matrix, load, rounded, *turned, *sends)


def between_near(chans, count, matrix, load, state, *refs):
    sends = refs[-len(chans) :]
    for channel, send in zip(chans, sends):
        rows = channel[3]
        own = own_rows(channel)
        send[0:rows] = load[own].astype(jnp.float32) - product(matrix[own], state[...])
        for turned in refs[: -len(chans)]:
            for block, columns, _ in row_blocks(channel):
                send[rows + block * count : rows + (block + 1) * count] = turned[0:count, columns]


def landing(chans, ncl, state, spread, near_values, *refs):
    count = len(chans)
    parts, gots, out = refs[:count], refs[count : 2 * count], refs[2 * count]
    values = Values(chans, ncl, near_values, (), ())
    for at, channel in enumerate(chans):
        own = own_rows(channel)
        theirs = values.at(at) if channel[0] == "sub" else jnp.zeros((ncl, state.shape[1]), jnp.float32)
        update = product(spread[own], split(jnp.concatenate([values.at(), theirs], axis=0), 0))
        update += parts[at][...] + across(channel, gots[at])
        out[own] = state[own].astype(jnp.float32) + update


def closing(chans, ncl, spread, landed, *refs):
    values, (out,) = value_refs(chans, ncl, refs)
    for at, channel in enumerate(chans):
        own = own_rows(channel)
        last = landed[own]
        if channel[0] == "grp":
            theirs = values.at(at)
            pair = jnp.concatenate([jnp.zeros_like(theirs), theirs], axis=0)
            last += product(spread[own], split(pair, 0))
        out[own] = last.astype(out.dtype)


def steps(sub):
    found, step = [], sub // 2
    while step:
        found.append(step)
        step //= 2
    return found


def origins(sub):
    found = [0]
    for step in steps(sub):
        found += [origin ^ step for origin in found]
    return found


def gathered(piece, sub, hold=(), wide=False, early=()):
    def hop(move):
        return lax.ppermute(piece, "sub", [(i, i ^ move) for i in range(sub)])

    moves = steps(sub)
    if wide:
        first, second, *moves = moves
        pieces = [piece] + [hop(move) for move in (first, second, first ^ second)]
        piece = jnp.concatenate(pieces, axis=0)
    for at, move in enumerate(moves[:-1]):
        got = hop(move)
        after = hold if at + 1 == len(moves) // 2 else early if at == 0 else ()
        if after:
            joined = jax.ShapeDtypeStruct((2 * piece.shape[0], piece.shape[1]), piece.dtype)
            piece = call(joining, joined, (piece, got), after=after, flops=0 if after is hold else WEIGHT // 2)
        else:
            piece = jnp.concatenate([piece, got], axis=0)
    return piece, hop(moves[-1])


def shards(
    schur_t, neumann_t, face_weights, coarse_basis, coarse_inverse, coarse_number, loads, iterate
):
    schur, neumann = schur_t[0, 0], neumann_t[0, 0]
    basis_across = coarse_basis[0, 0].T
    load, state = loads[0, 0], iterate[0, 0]
    iface, columns = state.shape
    ncl = basis_across.shape[0]
    face = iface // 4
    grp, sub = lax.axis_size("grp"), lax.axis_size("sub")
    chans = channels(grp, sub, face)
    far = tuple(c for c in chans if c[0] == "grp")
    near = chans[len(far) :]
    around = (len(chans) + 1) * ncl
    order = coarse_inverse.shape[2]

    def wide(rows, width=columns):
        return jax.ShapeDtypeStruct((rows, width), jnp.float32)

    def short(rows, width=columns):
        return jax.ShapeDtypeStruct((rows, width), jnp.bfloat16)

    far_plain, near_plain = [tuple(wide(c[3]) for c in group) for group in (far, near)]
    half = short(iface)
    flops = iface * iface * columns

    opened = (
        *far_plain,
        *(wide(c[3] + c[3] // LANES * ncl) for c in near),
        *(wide(c[3] // LANES * ncl) for c in far),
    )
    parts = call(
        functools.partial(opening, chans),
        opened,
        (schur, load, state, basis_across),
        scratch=(
            pltpu.VMEM(schur.shape, schur.dtype),
            pltpu.VMEM(load.shape, load.dtype),
            pltpu.VMEM(state.shape, state.dtype),
            pltpu.VMEM(basis_across.shape, basis_across.dtype),
            pltpu.SemaphoreType.DMA((3 + PIECES + len(opened),)),
            *(pltpu.VMEM(out.shape, out.dtype) for out in opened),
        ),
        flops=2 * flops,
        away=4,
        grant=56 * MIB,
        out=AWAY,
    )
    parts, far_basis = parts[: len(chans)], parts[len(chans) :]
    gots = exchange(chans, parts)
    basis_gots = (*exchange(far, far_basis), *gots[len(far) :])
    parts = call(stash, far_plain + near_plain, tuple(parts))

    weights = jnp.broadcast_to(face_weights[0, 0][:, None], (iface, columns))
    rows_of = coarse_inverse.shape[1]
    tiles = (order + -order % LANES) // LANES
    inverse_rows = (rows_of + -rows_of % 8) * tiles
    mapping = None

    def coarse_step(coarse, mapping, hold=(), after=(), early=(), sent=1 + len(near)):
        rows = len(near_order(chans)) * ncl
        kept, got = gathered(coarse, sub, hold, False, early)
        if mapping is None:
            mapping, own = call(
                functools.partial(coarse_first, chans, order, sub, ncl),
                (wide(rows, sub * ncl), wide(rows)),
                (coarse_number, kept, got),
                scratch=(
                    pltpu.VMEM((inverse_rows // tiles * sub, tiles * LANES), jnp.float32),
                    pltpu.VMEM((sub * ncl, 8), jnp.float32),
                    pltpu.VMEM((sub * ncl, 8), jnp.float32),
                    pltpu.VMEM((sub * ncl, columns), jnp.float32),
                ),
                after=after,
            )
        else:
            own = call(coarse_values, wide(rows), (mapping, kept, got), after=after)
        known = own[0 : sent * ncl]
        theirs = [swap(known, channel) for channel in far]
        beyond = []
        if len(far) > 1:
            beyond = [swap(theirs[1 - at][0:ncl], channel) for at, channel in enumerate(far)]
        return mapping, (own, *theirs, *beyond)

    def sums(sent, got):
        return call(functools.partial(summing, chans), wide(iface), (*sent, *got), flops=WEIGHT)

    for step in range(ITERS):
        start, last = step == 0, step + 1 == ITERS
        if start:
            weighted, *far_scaled = call(
                functools.partial(smoothing_first, chans, far),
                (half,) + far_plain,
                (neumann, weights, *parts, *gots),
                flops=flops,
            )
        else:
            early = (response,) if step == 1 else near_scaled[:1]
            mapping, values = coarse_step(coarse, mapping, hold=far_parts[:1], early=early)
            if step == 1:
                reach = [
                    call(
                        functools.partial(reaching, channel, around),
                        short(channel[3], 4 * around),
                        (response, got),
                        after=values[:1],
                    )
                    for channel, got in zip(chans, gots)
                ]
            known = (weights, ahead, spread, sums(parts, gots), *reach, *values)
            if last:
                state, weighted, coarse = call(
                    functools.partial(smoothing_last, chans, ncl),
                    (half, half, wide(ncl)),
                    (basis_across, *known),
                )
                far_scaled = call(
                    functools.partial(smoothing_rows, far),
                    far_plain,
                    (neumann, weights, weighted),
                    flops=flops,
                )
                near_scaled = call(
                    functools.partial(smoothing_rows, near),
                    near_plain,
                    (neumann, weights, weighted),
                    flops=flops,
                    after=far_scaled[:1],
                )
            else:
                state, weighted, *far_scaled = call(
                    functools.partial(smoothing_far, chans, far, ncl),
                    (half, half) + far_plain,
                    (neumann, *known),
                    flops=flops,
                )
        if not last:
            inverse = (coarse_inverse[0],) if start else ()
            coarse, *near_scaled = call(
                functools.partial(smoothing_sub, near),
                (wide(ncl + len(inverse) * inverse_rows),) + near_plain,
                (neumann, weights, weighted, basis_across, *inverse),
                flops=flops,
            )
        scaled = (*far_scaled, *near_scaled)
        scaled_gots = exchange(chans, scaled)
        behind, behind_rows = (), 0
        if start:
            width = around + -around % LANES
            spread, full = call(
                functools.partial(spreading, chans),
                (short(iface, 6 * ncl), short(iface, 2 * width)),
                (weights, basis_across, *basis_gots),
                after=near_scaled[:1],
            )
            response, turned = call(
                responding, (wide(iface, width), wide(width, iface)), (schur, full), flops=2 * flops
            )
            behind, behind_rows = (turned,), around
        if not last:
            far_outs, near_outs = [
                tuple(wide(c[3] + c[3] // LANES * behind_rows) for c in group) for group in (far, near)
            ]
            ahead, rounded, *far_parts = call(
                functools.partial(between_far, chans, far, around),
                (wide(iface), half) + far_outs,
                (schur, load, state, *scaled, *scaled_gots, *behind),
                flops=flops,
            )
            near_parts = call(
                functools.partial(between_near, near, around),
                near_outs,
                (schur, load, rounded, *behind),
                flops=flops,
                after=far_parts[:1],
            )
            parts = (*far_parts, *near_parts)
            gots = exchange(chans, parts)
    mapping, values = coarse_step(coarse, mapping, after=scaled_gots[len(far) :], sent=1)
    landed = call(
        functools.partial(landing, chans, ncl),
        wide(iface),
        (state, spread, values[0], *scaled, *scaled_gots),
        flops=WEIGHT,
    )
    out = call(functools.partial(closing, chans, ncl), half, (spread, landed, *values))
    return out[None, None]


def solution(mesh):
    return jax.shard_map(
        shards,
        mesh=mesh,
        in_specs=(
            P("grp", "sub", None, None),
            P("grp", "sub", None, None),
            P("grp", "sub", None),
            P("grp", "sub", None, None),
            P("grp", "sub", None),
            P("grp", None),
            P("grp", "sub", None, None),
            P("grp", "sub", None, None),
        ),
        out_specs=P("grp", "sub", None, None),
        check_vma=False,
    )
```

```python
import functools

import jax
import jax.numpy as jnp
from jax import lax
from jax.experimental import pallas as pl
from jax.experimental.pallas import tpu as pltpu
from jax.sharding import PartitionSpec as P

ITERS = 3
HIGHEST = lax.Precision.HIGHEST
EVEN, ODD, BOTH = range(3)
LANES = 128
PIECES = 8
WEIGHT = 4 * 10**9
MIB = 2**20
WHOLE = pl.BlockSpec(memory_space=pltpu.VMEM)
AWAY = pl.BlockSpec(memory_space=pltpu.HBM)
ANYWHERE = pl.BlockSpec(memory_space=pl.ANY)


def channels(grp, sub, face):
    found = []
    for axis, devices, base in (("grp", grp, 2 * face), ("sub", sub, 0)):
        if devices == 2:
            found.append((axis, BOTH, base, 2 * face))
        else:
            found += [(axis, ODD, base, face), (axis, EVEN, base, face)]
    return tuple(found)


def mate(kind, index, devices):
    if kind == BOTH:
        return 1 - index
    step = 1 - 2 * (index % 2)
    if kind == ODD:
        step = -step
    return (index + step + devices) % devices


def swap(array, channel):
    axis, kind = channel[:2]
    devices = lax.axis_size(axis)
    return lax.ppermute(array, axis, [(i, mate(kind, i, devices)) for i in range(devices)])


def exchange(chans, sends):
    return tuple(swap(send, channel) for channel, send in zip(chans, sends))


def first_row(channel):
    axis, kind, base, rows = channel
    if kind == BOTH:
        return base
    odd = lax.rem(lax.axis_index(axis), 2)
    return pl.multiple_of(base + (odd if kind == ODD else 1 - odd) * rows, rows)


def own_rows(channel):
    return pl.ds(first_row(channel), channel[3])


def row_blocks(channel):
    blocks = channel[3] // LANES
    for block in range(blocks):
        rows = pl.ds(pl.multiple_of(first_row(channel) + block * LANES, LANES), LANES)
        yield block, rows, (block + blocks // 2) % blocks if channel[1] == BOTH else block


def across(channel, got):
    rows = channel[3]
    if channel[1] == BOTH:
        return jnp.concatenate([got[rows // 2 : rows], got[0 : rows // 2]], axis=0)
    return got[0:rows]


def product(a, b):
    return jnp.dot(a, b, preferred_element_type=jnp.float32)


def split(values, axis):
    high = values.astype(jnp.bfloat16)
    low = (values - high.astype(jnp.float32)).astype(jnp.bfloat16)
    return jnp.concatenate([high, low, high], axis=axis)


def thrice(values):
    high = values.astype(jnp.bfloat16).astype(jnp.float32)
    return jnp.concatenate([high, high, values - high], axis=1).astype(jnp.bfloat16)


def call(body, outs, args, scratch=(), flops=0, away=0, after=(), grant=16 * MIB, out=WHOLE):
    moved = sum(a.size * a.dtype.itemsize for a in args)
    ahead = len(after)
    return pl.pallas_call(
        lambda *refs: body(*refs[ahead:]),
        out_shape=outs,
        in_specs=[ANYWHERE] * ahead + [AWAY] * away + [WHOLE] * (len(args) - away),
        out_specs=jax.tree.map(lambda _: out, outs),
        scratch_shapes=scratch,
        cost_estimate=pl.CostEstimate(flops=flops, bytes_accessed=moved, transcendentals=0),
        compiler_params=pltpu.CompilerParams(vmem_limit_bytes=grant),
    )(*after, *args)


class Values:
    def __init__(self, chans, ncl, near, far, second):
        self.chans, self.ncl = chans, ncl
        self.near, self.far, self.second = near, far, second
        self.order = near_order(chans)

    def at(self, *path):
        grp = [c for c in path if self.chans[c][0] == "grp"]
        sub = [c for c in path if self.chans[c][0] == "sub"]
        grp, sub = [[] if len(p) == 2 and p[0] == p[1] else p for p in (grp, sub)]
        if len(grp) == 2:
            return self.second[grp[0]][...]
        source = self.far[grp[0]] if grp else self.near
        place = self.order.index(tuple(sub)) * self.ncl
        return source[place : place + self.ncl]

    def around(self, *path):
        return [self.at(*path)] + [self.at(*path, c) for c in range(len(self.chans))]


def near_order(chans):
    kinds = [c for c, channel in enumerate(chans) if channel[0] == "sub"]
    return [()] + [(c,) for c in kinds] + [(c, d) for c in kinds for d in kinds if c != d]


def value_refs(chans, ncl, refs):
    far = sum(channel[0] == "grp" for channel in chans)
    second = far if far > 1 else 0
    values = Values(chans, ncl, refs[0], refs[1 : 1 + far], refs[1 + far : 1 + far + second])
    return values, refs[1 + far + second :]


def opening(chans, matrix, load, state, basis_across, *refs):
    count = len(refs) // 2 - 2
    outs, (rows, mine, now, basis, sems), sends = refs[:count], refs[count : count + 5], refs[count + 5 :]
    piece = matrix.shape[0] // PIECES
    order = [(at + PIECES // 2) % PIECES * piece for at in range(PIECES)]
    pairs = [(state, now), (load, mine), (basis_across, basis)]
    pairs += [(matrix.at[pl.ds(at, piece)], rows.at[pl.ds(at, piece)]) for at in order]
    copies = [pltpu.make_async_copy(a, b, sems.at[i]) for i, (a, b) in enumerate(pairs)]
    for copy in copies:
        copy.start()
    first = 3 + PIECES // 2
    for copy in copies[:first]:
        copy.wait()
    waiting = copies[first:]
    written = []

    def write(send):
        at = len(written)
        written.append(pltpu.make_async_copy(send, outs[at], sems.at[len(pairs) + at]))
        written[-1].start()

    for channel, send in zip(chans, sends):
        if channel[0] == "sub":
            while waiting:
                waiting.pop(0).wait()
        own = own_rows(channel)
        send[0 : channel[3]] = mine[own].astype(jnp.float32) - product(rows[own], now[...])
        if channel[0] == "sub":
            basis_on(channel, basis, send, channel[3])
        write(send)
    for channel, send in zip(chans, sends[len(chans) :]):
        basis_on(channel, basis, send, 0)
        write(send)
    for copy in written:
        copy.wait()


def basis_on(channel, basis, send, start):
    ncl = basis.shape[0]
    for block, columns, _ in row_blocks(channel):
        at = start + block * ncl
        send[at : at + ncl] = basis[:, columns].astype(jnp.float32)


def smooth(chans, weights, resid_on, weighted):
    for at, channel in enumerate(chans):
        own = own_rows(channel)
        weighted[own] = (weights[own] * resid_on(at, own)).astype(jnp.bfloat16)


def smoothing_near(chans, matrix, weights, weighted, sends):
    for channel, send in zip(chans, sends):
        own = own_rows(channel)
        send[...] = weights[own] * product(matrix[own], weighted[...])


def stash(*refs):
    count = len(refs) // 2
    for part, out in zip(refs[:count], refs[count:]):
        out[...] = part[0 : out.shape[0]]


def summing(chans, *refs):
    count = len(chans)
    parts, gots, out = refs[:count], refs[count : 2 * count], refs[2 * count]
    for channel, part, got in zip(chans, parts, gots):
        out[own_rows(channel)] = part[0 : channel[3]] + across(channel, got)


def smoothing_first(chans, far, matrix, weights, *refs):
    count = len(chans)
    parts, gots = refs[:count], refs[count : 2 * count]

    def resid_on(at, own):
        return parts[at][...] + across(chans[at], gots[at])

    smooth(chans, weights, resid_on, refs[2 * count])
    smoothing_near(far, matrix, weights, refs[2 * count], refs[2 * count + 1 :])


def correct(chans, ncl, weights, ahead, spread, summed, refs):
    reach = refs[: len(chans)]
    values, refs = value_refs(chans, ncl, refs[len(chans) :])
    state, weighted, rest = refs[0], refs[1], refs[2:]
    here = values.around()

    def resid_on(at, own):
        pair = jnp.concatenate([here[0], values.at(at)], axis=0)
        state[own] = (ahead[own] + product(spread[own], split(pair, 0))).astype(state.dtype)
        both = jnp.concatenate(here + values.around(at), axis=0)
        return summed[own] - product(reach[at][...], split(both, 0)[0 : 2 * both.shape[0]])

    smooth(chans, weights, resid_on, weighted)
    return weighted, rest


def smoothing_far(chans, far, ncl, matrix, weights, ahead, spread, summed, *refs):
    weighted, sends = correct(chans, ncl, weights, ahead, spread, summed, refs)
    smoothing_near(far, matrix, weights, weighted, sends)


def smoothing_last(chans, ncl, basis_across, weights, ahead, spread, summed, *refs):
    weighted, (coarse,) = correct(chans, ncl, weights, ahead, spread, summed, refs)
    coarse[...] = product(basis_across[...], weighted[...])


def smoothing_rows(chans, matrix, weights, weighted, *sends):
    smoothing_near(chans, matrix, weights, weighted, sends)


def smoothing_sub(near, matrix, weights, weighted, basis_across, *refs):
    inverse = refs[: -len(near) - 1]
    coarse, sends = refs[-len(near) - 1], refs[-len(near) :]
    ncl = basis_across.shape[0]
    coarse[0:ncl] = product(basis_across[...], weighted[...])
    for rows in inverse:
        padded = rows.shape[0] + -rows.shape[0] % 8
        coarse[ncl:] = jnp.zeros((coarse.shape[0] - ncl, coarse.shape[1]), jnp.float32)
        for at in range(0, rows.shape[1], LANES):
            start = ncl + at // LANES * padded
            columns = min(LANES, rows.shape[1] - at)
            coarse[start : start + rows.shape[0], 0:columns] = rows[:, at : at + columns]
    smoothing_near(near, matrix, weights, weighted, sends)


def spreading(chans, weights, basis_across, *refs):
    gots, thin, full = refs[:-2], refs[-2], refs[-1]
    ncl = basis_across.shape[0]
    width = full.shape[1] // 2
    for at, (channel, got) in enumerate(zip(chans, gots)):
        for _, own, block in row_blocks(channel):
            from_row = block * ncl + (channel[3] if channel[0] == "sub" else 0)
            weight = weights[own][:, 0:ncl]
            here = weight * basis_across[:, own].astype(jnp.float32).T
            there = (1.0 - weight) * got[from_row : from_row + ncl].T
            thin[own] = thrice(jnp.concatenate([here, there], axis=1))
            before = [jnp.zeros((LANES, at * ncl), jnp.float32)] if at else []
            behind = jnp.zeros((LANES, width - (at + 2) * ncl), jnp.float32)
            placed = jnp.concatenate([here, *before, there, behind], axis=1)
            high = placed.astype(jnp.bfloat16)
            full[own, 0:width] = high
            full[own, width:] = (placed - high.astype(jnp.float32)).astype(jnp.bfloat16)


def responding(matrix, full, out, turned):
    width = out.shape[1]
    both = product(matrix[...], full[...])
    out[...] = both[:, 0:width] + both[:, width:]
    for at in range(0, out.shape[0], LANES):
        turned[:, at : at + LANES] = out[at : at + LANES].T


def reaching(channel, count, response, got, out):
    for block, own, from_block in row_blocks(channel):
        at = channel[3] + from_block * count
        theirs = got[at : at + count].T
        both = jnp.concatenate([response[own][:, 0:count], theirs], axis=1)
        out[block * LANES : (block + 1) * LANES] = jnp.concatenate([both, both], axis=1).astype(jnp.bfloat16)


def joining(first, second, out):
    out[...] = jnp.concatenate([first[...], second[...]], axis=0)


def coarse_first(chans, order, sub, ncl, numbers, kept, got, out, values, *scratch):
    arranged, upright, relative, pieces = scratch
    index = lax.axis_index("sub")
    rows_of = order // sub
    padded = rows_of + -rows_of % 8
    stride = kept.shape[0] * 2 // sub
    upright[...] = jnp.broadcast_to(numbers[...].astype(jnp.float32), (8, numbers.shape[1])).T
    for block, origin in enumerate(origins(sub)):
        origin = jnp.bitwise_xor(index, origin)
        half = sub // 2
        source = kept if block < half else got
        at = (block % half) * stride
        pieces[block * ncl : (block + 1) * ncl] = source[at : at + ncl]
        to = pl.ds(pl.multiple_of(origin * padded, 8), padded)
        for tile in range(arranged.shape[1] // LANES):
            start = at + ncl + tile * padded
            arranged[to, tile * LANES : (tile + 1) * LANES] = source[start : start + padded]
        relative[block * ncl : (block + 1) * ncl] = upright[pl.ds(pl.multiple_of(origin * ncl, 8), ncl)]
    wanted = []
    for path in near_order(chans):
        place = index
        for c in path:
            place = mate(chans[c][1], place, sub)
        wanted.append(upright[pl.ds(pl.multiple_of(place * ncl, 8), ncl)])
    wanted = jnp.concatenate(wanted, axis=0)[:, 0:1].astype(jnp.int32)
    lane = lax.broadcasted_iota(jnp.int32, (wanted.shape[0], sub * padded), 1)
    inside = lane % padded
    held = jnp.where(inside < rows_of, (lane // padded) * rows_of + inside, -1)
    pick = jnp.where(wanted == held, 1.0, 0.0).astype(jnp.float32)
    chosen = jnp.dot(pick, arranged[...], precision=HIGHEST, preferred_element_type=jnp.float32)
    column = lax.broadcasted_iota(jnp.int32, (relative.shape[0], arranged.shape[1]), 1)
    place = jnp.where(relative[...][:, 0:1].astype(jnp.int32) == column, 1.0, 0.0).astype(jnp.float32)
    out[...] = lax.dot_general(
        chosen, place, (((1,), (1,)), ((), ())), precision=HIGHEST, preferred_element_type=jnp.float32
    )
    values[...] = jnp.dot(out[...], pieces[...], precision=HIGHEST, preferred_element_type=jnp.float32)


def coarse_values(mapping, kept, got, out):
    half = kept.shape[0]
    total = jnp.dot(mapping[:, 0:half], kept[...], precision=HIGHEST, preferred_element_type=jnp.float32)
    total += jnp.dot(mapping[:, half:], got[...], precision=HIGHEST, preferred_element_type=jnp.float32)
    out[...] = total


def between_far(chans, far, count, matrix, load, state, *refs):
    size = len(chans)
    parts, gots = refs[:size], refs[size : 2 * size]
    turned = refs[2 * size : -len(far) - 2]
    ahead, rounded, sends = refs[-len(far) - 2], refs[-len(far) - 1], refs[-len(far) :]
    for channel, part, got in zip(chans, parts, gots):
        own = own_rows(channel)
        ahead[own] = state[own].astype(jnp.float32) + part[...] + across(channel, got)
        rounded[own] = ahead[own].astype(rounded.dtype)
    between_near(far, count, matrix, load, rounded, *turned, *sends)


def between_near(chans, count, matrix, load, state, *refs):
    sends = refs[-len(chans) :]
    for channel, send in zip(chans, sends):
        rows = channel[3]
        own = own_rows(channel)
        send[0:rows] = load[own].astype(jnp.float32) - product(matrix[own], state[...])
        for turned in refs[: -len(chans)]:
            for block, columns, _ in row_blocks(channel):
                send[rows + block * count : rows + (block + 1) * count] = turned[0:count, columns]


def landing(chans, ncl, state, spread, near_values, *refs):
    count = len(chans)
    parts, gots, out = refs[:count], refs[count : 2 * count], refs[2 * count]
    values = Values(chans, ncl, near_values, (), ())
    for at, channel in enumerate(chans):
        own = own_rows(channel)
        theirs = values.at(at) if channel[0] == "sub" else jnp.zeros((ncl, state.shape[1]), jnp.float32)
        update = product(spread[own], split(jnp.concatenate([values.at(), theirs], axis=0), 0))
        update += parts[at][...] + across(channel, gots[at])
        out[own] = state[own].astype(jnp.float32) + update


def closing(chans, ncl, spread, landed, *refs):
    values, (out,) = value_refs(chans, ncl, refs)
    for at, channel in enumerate(chans):
        own = own_rows(channel)
        last = landed[own]
        if channel[0] == "grp":
            theirs = values.at(at)
            pair = jnp.concatenate([jnp.zeros_like(theirs), theirs], axis=0)
            last += product(spread[own], split(pair, 0))
        out[own] = last.astype(out.dtype)


def steps(sub):
    found, step = [], sub // 2
    while step:
        found.append(step)
        step //= 2
    return found


def origins(sub):
    found = [0]
    for step in steps(sub):
        found += [origin ^ step for origin in found]
    return found


def gathered(piece, sub, hold=(), wide=False, early=(), done=0):
    def hop(move):
        return lax.ppermute(piece, "sub", [(i, i ^ move) for i in range(sub)])

    moves = steps(sub)
    if wide:
        first, second, *moves = moves
        pieces = [piece] + [hop(move) for move in (first, second, first ^ second)]
        piece = jnp.concatenate(pieces, axis=0)
    for at, move in enumerate(moves[:-1]):
        if at < done:
            continue
        got = hop(move)
        after = hold if at + 1 == len(moves) // 2 else early if at == 0 else ()
        if after:
            joined = jax.ShapeDtypeStruct((2 * piece.shape[0], piece.shape[1]), piece.dtype)
            piece = call(joining, joined, (piece, got), after=after, flops=0 if after is hold else WEIGHT // 2)
        else:
            piece = jnp.concatenate([piece, got], axis=0)
    return piece, hop(moves[-1])


def shards(
    schur_t, neumann_t, face_weights, coarse_basis, coarse_inverse, coarse_number, loads, iterate
):
    schur, neumann = schur_t[0, 0], neumann_t[0, 0]
    basis_across = coarse_basis[0, 0].T
    load, state = loads[0, 0], iterate[0, 0]
    iface, columns = state.shape
    ncl = basis_across.shape[0]
    face = iface // 4
    grp, sub = lax.axis_size("grp"), lax.axis_size("sub")
    chans = channels(grp, sub, face)
    far = tuple(c for c in chans if c[0] == "grp")
    near = chans[len(far) :]
    around = (len(chans) + 1) * ncl
    order = coarse_inverse.shape[2]

    def wide(rows, width=columns):
        return jax.ShapeDtypeStruct((rows, width), jnp.float32)

    def short(rows, width=columns):
        return jax.ShapeDtypeStruct((rows, width), jnp.bfloat16)

    far_plain, near_plain = [tuple(wide(c[3]) for c in group) for group in (far, near)]
    half = short(iface)
    flops = iface * iface * columns

    opened = (
        *far_plain,
        *(wide(c[3] + c[3] // LANES * ncl) for c in near),
        *(wide(c[3] // LANES * ncl) for c in far),
    )
    parts = call(
        functools.partial(opening, chans),
        opened,
        (schur, load, state, basis_across),
        scratch=(
            pltpu.VMEM(schur.shape, schur.dtype),
            pltpu.VMEM(load.shape, load.dtype),
            pltpu.VMEM(state.shape, state.dtype),
            pltpu.VMEM(basis_across.shape, basis_across.dtype),
            pltpu.SemaphoreType.DMA((3 + PIECES + len(opened),)),
            *(pltpu.VMEM(out.shape, out.dtype) for out in opened),
        ),
        flops=2 * flops,
        away=4,
        grant=56 * MIB,
        out=AWAY,
    )
    parts, far_basis = parts[: len(chans)], parts[len(chans) :]
    gots = exchange(chans, parts)
    basis_gots = (*exchange(far, far_basis), *gots[len(far) :])
    parts = call(stash, far_plain + near_plain, tuple(parts))

    weights = jnp.broadcast_to(face_weights[0, 0][:, None], (iface, columns))
    rows_of = coarse_inverse.shape[1]
    tiles = (order + -order % LANES) // LANES
    inverse_rows = (rows_of + -rows_of % 8) * tiles
    mapping = None

    def coarse_step(coarse, mapping, hold=(), after=(), early=(), sent=1 + len(near), done=0):
        rows = len(near_order(chans)) * ncl
        kept, got = gathered(coarse, sub, hold, False, early, done)
        if mapping is None:
            mapping, own = call(
                functools.partial(coarse_first, chans, order, sub, ncl),
                (wide(rows, sub * ncl), wide(rows)),
                (coarse_number, kept, got),
                scratch=(
                    pltpu.VMEM((inverse_rows // tiles * sub, tiles * LANES), jnp.float32),
                    pltpu.VMEM((sub * ncl, 8), jnp.float32),
                    pltpu.VMEM((sub * ncl, 8), jnp.float32),
                    pltpu.VMEM((sub * ncl, columns), jnp.float32),
                ),
                after=after,
            )
        else:
            own = call(coarse_values, wide(rows), (mapping, kept, got), after=after)
        known = own[0 : sent * ncl]
        theirs = [swap(known, channel) for channel in far]
        beyond = []
        if len(far) > 1:
            beyond = [swap(theirs[1 - at][0:ncl], channel) for at, channel in enumerate(far)]
        return mapping, (own, *theirs, *beyond)

    def sums(sent, got):
        return call(functools.partial(summing, chans), wide(iface), (*sent, *got), flops=WEIGHT)

    for step in range(ITERS):
        start, last = step == 0, step + 1 == ITERS
        if start:
            weighted, *far_scaled = call(
                functools.partial(smoothing_first, chans, far),
                (half,) + far_plain,
                (neumann, weights, *parts, *gots),
                flops=flops,
            )
        else:
            early = (response,) if step == 1 else near_scaled[:1]
            mapping, values = coarse_step(coarse, mapping, hold=far_parts[:1], early=early)
            if step == 1:
                reach = [
                    call(
                        functools.partial(reaching, channel, around),
                        short(channel[3], 4 * around),
                        (response, got),
                        after=values[:1],
                    )
                    for channel, got in zip(chans, gots)
                ]
            known = (weights, ahead, spread, sums(parts, gots), *reach, *values)
            if last:
                state, weighted, coarse = call(
                    functools.partial(smoothing_last, chans, ncl),
                    (half, half, wide(ncl)),
                    (basis_across, *known),
                )
                far_scaled = call(
                    functools.partial(smoothing_rows, far),
                    far_plain,
                    (neumann, weights, weighted),
                    flops=flops,
                )
                hop = lax.ppermute(coarse, "sub", [(i, i ^ steps(sub)[0]) for i in range(sub)])
                coarse = call(
                    joining, wide(2 * ncl), (coarse, hop), after=far_scaled[:1], flops=0
                )
                near_scaled = call(
                    functools.partial(smoothing_rows, near),
                    near_plain,
                    (neumann, weights, weighted),
                    flops=flops,
                    after=(coarse,),
                )
            else:
                state, weighted, *far_scaled = call(
                    functools.partial(smoothing_far, chans, far, ncl),
                    (half, half) + far_plain,
                    (neumann, *known),
                    flops=flops,
                )
        if not last:
            inverse = (coarse_inverse[0],) if start else ()
            coarse, *near_scaled = call(
                functools.partial(smoothing_sub, near),
                (wide(ncl + len(inverse) * inverse_rows),) + near_plain,
                (neumann, weights, weighted, basis_across, *inverse),
                flops=flops,
            )
        scaled = (*far_scaled, *near_scaled)
        scaled_gots = exchange(chans, scaled)
        behind, behind_rows = (), 0
        if start:
            width = around + -around % LANES
            spread, full = call(
                functools.partial(spreading, chans),
                (short(iface, 6 * ncl), short(iface, 2 * width)),
                (weights, basis_across, *basis_gots),
                after=near_scaled[:1],
            )
            response, turned = call(
                responding, (wide(iface, width), wide(width, iface)), (schur, full), flops=2 * flops
            )
            behind, behind_rows = (turned,), around
        if not last:
            far_outs, near_outs = [
                tuple(wide(c[3] + c[3] // LANES * behind_rows) for c in group) for group in (far, near)
            ]
            ahead, rounded, *far_parts = call(
                functools.partial(between_far, chans, far, around),
                (wide(iface), half) + far_outs,
                (schur, load, state, *scaled, *scaled_gots, *behind),
                flops=flops,
            )
            near_parts = call(
                functools.partial(between_near, near, around),
                near_outs,
                (schur, load, rounded, *behind),
                flops=flops,
                after=far_parts[:1],
            )
            parts = (*far_parts, *near_parts)
            gots = exchange(chans, parts)
    mapping, values = coarse_step(coarse, mapping, hold=near_scaled[:1], after=scaled_gots[: len(far)], sent=1, done=1)
    landed = call(
        functools.partial(landing, chans, ncl),
        wide(iface),
        (state, spread, values[0], *scaled, *scaled_gots),
        flops=WEIGHT,
    )
    out = call(functools.partial(closing, chans, ncl), half, (spread, landed, *values))
    return out[None, None]


def solution(mesh):
    return jax.shard_map(
        shards,
        mesh=mesh,
        in_specs=(
            P("grp", "sub", None, None),
            P("grp", "sub", None, None),
            P("grp", "sub", None),
            P("grp", "sub", None, None),
            P("grp", "sub", None),
            P("grp", None),
            P("grp", "sub", None, None),
            P("grp", "sub", None, None),
        ),
        out_specs=P("grp", "sub", None, None),
        check_vma=False,
    )
```

```python
import functools

import jax
import jax.numpy as jnp
from jax import lax
from jax.experimental import pallas as pl
from jax.experimental.pallas import tpu as pltpu
from jax.sharding import PartitionSpec as P

ITERS = 3
HIGHEST = lax.Precision.HIGHEST
EVEN, ODD, BOTH = range(3)
LANES = 128
PIECES = 8
WEIGHT = 4 * 10**9
MIB = 2**20
WHOLE = pl.BlockSpec(memory_space=pltpu.VMEM)
AWAY = pl.BlockSpec(memory_space=pltpu.HBM)
ANYWHERE = pl.BlockSpec(memory_space=pl.ANY)


def channels(grp, sub, face):
    found = []
    for axis, devices, base in (("grp", grp, 2 * face), ("sub", sub, 0)):
        if devices == 2:
            found.append((axis, BOTH, base, 2 * face))
        else:
            found += [(axis, ODD, base, face), (axis, EVEN, base, face)]
    return tuple(found)


def mate(kind, index, devices):
    if kind == BOTH:
        return 1 - index
    step = 1 - 2 * (index % 2)
    if kind == ODD:
        step = -step
    return (index + step + devices) % devices


def swap(array, channel):
    axis, kind = channel[:2]
    devices = lax.axis_size(axis)
    return lax.ppermute(array, axis, [(i, mate(kind, i, devices)) for i in range(devices)])


def exchange(chans, sends):
    return tuple(swap(send, channel) for channel, send in zip(chans, sends))


def first_row(channel):
    axis, kind, base, rows = channel
    if kind == BOTH:
        return base
    odd = lax.rem(lax.axis_index(axis), 2)
    return pl.multiple_of(base + (odd if kind == ODD else 1 - odd) * rows, rows)


def own_rows(channel):
    return pl.ds(first_row(channel), channel[3])


def row_blocks(channel):
    blocks = channel[3] // LANES
    for block in range(blocks):
        rows = pl.ds(pl.multiple_of(first_row(channel) + block * LANES, LANES), LANES)
        yield block, rows, (block + blocks // 2) % blocks if channel[1] == BOTH else block


def across(channel, got):
    rows = channel[3]
    if channel[1] == BOTH:
        return jnp.concatenate([got[rows // 2 : rows], got[0 : rows // 2]], axis=0)
    return got[0:rows]


def product(a, b):
    return jnp.dot(a, b, preferred_element_type=jnp.float32)


def split(values, axis):
    high = values.astype(jnp.bfloat16)
    low = (values - high.astype(jnp.float32)).astype(jnp.bfloat16)
    return jnp.concatenate([high, low, high], axis=axis)


def thrice(values):
    high = values.astype(jnp.bfloat16).astype(jnp.float32)
    return jnp.concatenate([high, high, values - high], axis=1).astype(jnp.bfloat16)


def call(body, outs, args, scratch=(), flops=0, away=0, after=(), grant=16 * MIB, out=WHOLE):
    moved = sum(a.size * a.dtype.itemsize for a in args)
    ahead = len(after)
    return pl.pallas_call(
        lambda *refs: body(*refs[ahead:]),
        out_shape=outs,
        in_specs=[ANYWHERE] * ahead + [AWAY] * away + [WHOLE] * (len(args) - away),
        out_specs=jax.tree.map(lambda _: out, outs),
        scratch_shapes=scratch,
        cost_estimate=pl.CostEstimate(flops=flops, bytes_accessed=moved, transcendentals=0),
        compiler_params=pltpu.CompilerParams(vmem_limit_bytes=grant),
    )(*after, *args)


class Values:
    def __init__(self, chans, ncl, near, far, second):
        self.chans, self.ncl = chans, ncl
        self.near, self.far, self.second = near, far, second
        self.order = near_order(chans)

    def at(self, *path):
        grp = [c for c in path if self.chans[c][0] == "grp"]
        sub = [c for c in path if self.chans[c][0] == "sub"]
        grp, sub = [[] if len(p) == 2 and p[0] == p[1] else p for p in (grp, sub)]
        if len(grp) == 2:
            return self.second[grp[0]][...]
        source = self.far[grp[0]] if grp else self.near
        place = self.order.index(tuple(sub)) * self.ncl
        return source[place : place + self.ncl]

    def around(self, *path):
        return [self.at(*path)] + [self.at(*path, c) for c in range(len(self.chans))]


def near_order(chans):
    kinds = [c for c, channel in enumerate(chans) if channel[0] == "sub"]
    return [()] + [(c,) for c in kinds] + [(c, d) for c in kinds for d in kinds if c != d]


def value_refs(chans, ncl, refs):
    far = sum(channel[0] == "grp" for channel in chans)
    second = far if far > 1 else 0
    values = Values(chans, ncl, refs[0], refs[1 : 1 + far], refs[1 + far : 1 + far + second])
    return values, refs[1 + far + second :]


def opening(chans, matrix, load, state, basis_across, *refs):
    count = len(refs) // 2 - 2
    outs, (rows, mine, now, basis, sems), sends = refs[:count], refs[count : count + 5], refs[count + 5 :]
    piece = matrix.shape[0] // PIECES
    order = [(at + PIECES // 2) % PIECES * piece for at in range(PIECES)]
    pairs = [(state, now), (load, mine), (basis_across, basis)]
    pairs += [(matrix.at[pl.ds(at, piece)], rows.at[pl.ds(at, piece)]) for at in order]
    copies = [pltpu.make_async_copy(a, b, sems.at[i]) for i, (a, b) in enumerate(pairs)]
    for copy in copies:
        copy.start()
    first = 3 + PIECES // 2
    for copy in copies[:first]:
        copy.wait()
    waiting = copies[first:]
    written = []

    def write(send):
        at = len(written)
        written.append(pltpu.make_async_copy(send, outs[at], sems.at[len(pairs) + at]))
        written[-1].start()

    for channel, send in zip(chans, sends):
        if channel[0] == "sub":
            while waiting:
                waiting.pop(0).wait()
        own = own_rows(channel)
        send[0 : channel[3]] = mine[own].astype(jnp.float32) - product(rows[own], now[...])
        if channel[0] == "sub":
            basis_on(channel, basis, send, channel[3])
        write(send)
    for channel, send in zip(chans, sends[len(chans) :]):
        basis_on(channel, basis, send, 0)
        write(send)
    for copy in written:
        copy.wait()


def basis_on(channel, basis, send, start):
    ncl = basis.shape[0]
    for block, columns, _ in row_blocks(channel):
        at = start + block * ncl
        send[at : at + ncl] = basis[:, columns].astype(jnp.float32)


def smooth(chans, weights, resid_on, weighted):
    for at, channel in enumerate(chans):
        own = own_rows(channel)
        weighted[own] = (weights[own] * resid_on(at, own)).astype(jnp.bfloat16)


def smoothing_near(chans, matrix, weights, weighted, sends):
    for channel, send in zip(chans, sends):
        own = own_rows(channel)
        send[...] = weights[own] * product(matrix[own], weighted[...])


def stash(*refs):
    count = len(refs) // 2
    for part, out in zip(refs[:count], refs[count:]):
        out[...] = part[0 : out.shape[0]]


def summing(chans, *refs):
    count = len(chans)
    parts, gots, out = refs[:count], refs[count : 2 * count], refs[2 * count]
    for channel, part, got in zip(chans, parts, gots):
        out[own_rows(channel)] = part[0 : channel[3]] + across(channel, got)


def smoothing_first(chans, far, matrix, weights, *refs):
    count = len(chans)
    parts, gots = refs[:count], refs[count : 2 * count]

    def resid_on(at, own):
        return parts[at][...] + across(chans[at], gots[at])

    smooth(chans, weights, resid_on, refs[2 * count])
    smoothing_near(far, matrix, weights, refs[2 * count], refs[2 * count + 1 :])


def correct(chans, ncl, weights, ahead, spread, summed, refs):
    reach = refs[: len(chans)]
    values, refs = value_refs(chans, ncl, refs[len(chans) :])
    state, weighted, rest = refs[0], refs[1], refs[2:]
    here = values.around()

    def resid_on(at, own):
        pair = jnp.concatenate([here[0], values.at(at)], axis=0)
        state[own] = (ahead[own] + product(spread[own], split(pair, 0))).astype(state.dtype)
        both = jnp.concatenate(here + values.around(at), axis=0)
        return summed[own] - product(reach[at][...], split(both, 0)[0 : 2 * both.shape[0]])

    smooth(chans, weights, resid_on, weighted)
    return weighted, rest


def smoothing_far(chans, far, ncl, matrix, weights, ahead, spread, summed, *refs):
    weighted, sends = correct(chans, ncl, weights, ahead, spread, summed, refs)
    smoothing_near(far, matrix, weights, weighted, sends)


def smoothing_last(chans, ncl, basis_across, weights, ahead, spread, summed, *refs):
    weighted, (coarse,) = correct(chans, ncl, weights, ahead, spread, summed, refs)
    coarse[...] = product(basis_across[...], weighted[...])


def smoothing_rows(chans, matrix, weights, weighted, *sends):
    smoothing_near(chans, matrix, weights, weighted, sends)


def smoothing_sub(near, matrix, weights, weighted, basis_across, *refs):
    inverse = refs[: -len(near) - 1]
    coarse, sends = refs[-len(near) - 1], refs[-len(near) :]
    ncl = basis_across.shape[0]
    coarse[0:ncl] = product(basis_across[...], weighted[...])
    for rows in inverse:
        padded = rows.shape[0] + -rows.shape[0] % 8
        coarse[ncl:] = jnp.zeros((coarse.shape[0] - ncl, coarse.shape[1]), jnp.float32)
        for at in range(0, rows.shape[1], LANES):
            start = ncl + at // LANES * padded
            columns = min(LANES, rows.shape[1] - at)
            coarse[start : start + rows.shape[0], 0:columns] = rows[:, at : at + columns]
    smoothing_near(near, matrix, weights, weighted, sends)


def spreading(chans, weights, basis_across, *refs):
    gots, thin, full = refs[:-2], refs[-2], refs[-1]
    ncl = basis_across.shape[0]
    width = full.shape[1] // 2
    for at, (channel, got) in enumerate(zip(chans, gots)):
        for _, own, block in row_blocks(channel):
            from_row = block * ncl + (channel[3] if channel[0] == "sub" else 0)
            weight = weights[own][:, 0:ncl]
            here = weight * basis_across[:, own].astype(jnp.float32).T
            there = (1.0 - weight) * got[from_row : from_row + ncl].T
            thin[own] = thrice(jnp.concatenate([here, there], axis=1))
            before = [jnp.zeros((LANES, at * ncl), jnp.float32)] if at else []
            behind = jnp.zeros((LANES, width - (at + 2) * ncl), jnp.float32)
            placed = jnp.concatenate([here, *before, there, behind], axis=1)
            high = placed.astype(jnp.bfloat16)
            full[own, 0:width] = high
            full[own, width:] = (placed - high.astype(jnp.float32)).astype(jnp.bfloat16)


def responding(matrix, full, out, turned):
    width = out.shape[1]
    both = product(matrix[...], full[...])
    out[...] = both[:, 0:width] + both[:, width:]
    for at in range(0, out.shape[0], LANES):
        turned[:, at : at + LANES] = out[at : at + LANES].T


def reaching(channel, count, response, got, out):
    for block, own, from_block in row_blocks(channel):
        at = channel[3] + from_block * count
        theirs = got[at : at + count].T
        both = jnp.concatenate([response[own][:, 0:count], theirs], axis=1)
        out[block * LANES : (block + 1) * LANES] = jnp.concatenate([both, both], axis=1).astype(jnp.bfloat16)


def joining(first, second, out):
    out[...] = jnp.concatenate([first[...], second[...]], axis=0)


def coarse_first(chans, order, sub, ncl, numbers, kept, got, out, values, *scratch):
    arranged, upright, relative, pieces = scratch
    index = lax.axis_index("sub")
    rows_of = order // sub
    padded = rows_of + -rows_of % 8
    stride = kept.shape[0] * 2 // sub
    upright[...] = jnp.broadcast_to(numbers[...].astype(jnp.float32), (8, numbers.shape[1])).T
    for block, origin in enumerate(origins(sub)):
        origin = jnp.bitwise_xor(index, origin)
        half = sub // 2
        source = kept if block < half else got
        at = (block % half) * stride
        pieces[block * ncl : (block + 1) * ncl] = source[at : at + ncl]
        to = pl.ds(pl.multiple_of(origin * padded, 8), padded)
        for tile in range(arranged.shape[1] // LANES):
            start = at + ncl + tile * padded
            arranged[to, tile * LANES : (tile + 1) * LANES] = source[start : start + padded]
        relative[block * ncl : (block + 1) * ncl] = upright[pl.ds(pl.multiple_of(origin * ncl, 8), ncl)]
    wanted = []
    for path in near_order(chans):
        place = index
        for c in path:
            place = mate(chans[c][1], place, sub)
        wanted.append(upright[pl.ds(pl.multiple_of(place * ncl, 8), ncl)])
    wanted = jnp.concatenate(wanted, axis=0)[:, 0:1].astype(jnp.int32)
    lane = lax.broadcasted_iota(jnp.int32, (wanted.shape[0], sub * padded), 1)
    inside = lane % padded
    held = jnp.where(inside < rows_of, (lane // padded) * rows_of + inside, -1)
    pick = jnp.where(wanted == held, 1.0, 0.0).astype(jnp.float32)
    chosen = jnp.dot(pick, arranged[...], precision=HIGHEST, preferred_element_type=jnp.float32)
    column = lax.broadcasted_iota(jnp.int32, (relative.shape[0], arranged.shape[1]), 1)
    place = jnp.where(relative[...][:, 0:1].astype(jnp.int32) == column, 1.0, 0.0).astype(jnp.float32)
    whole = lax.dot_general(
        chosen, place, (((1,), (1,)), ((), ())), precision=HIGHEST, preferred_element_type=jnp.float32
    )
    values[...] = jnp.dot(whole, pieces[...], precision=HIGHEST, preferred_element_type=jnp.float32)
    half = whole.shape[1] // 2
    out[:, 0 : 3 * half] = thrice(whole[:, 0:half])
    out[:, 3 * half :] = thrice(whole[:, half:])


def coarse_values(mapping, kept, got, out):
    half = mapping.shape[1] // 2
    out[...] = product(mapping[:, 0:half], split(kept[...], 0)) + product(mapping[:, half:], split(got[...], 0))


def between_far(chans, far, count, matrix, load, state, *refs):
    size = len(chans)
    parts, gots = refs[:size], refs[size : 2 * size]
    turned = refs[2 * size : -len(far) - 2]
    ahead, rounded, sends = refs[-len(far) - 2], refs[-len(far) - 1], refs[-len(far) :]
    for channel, part, got in zip(chans, parts, gots):
        own = own_rows(channel)
        ahead[own] = state[own].astype(jnp.float32) + part[...] + across(channel, got)
        rounded[own] = ahead[own].astype(rounded.dtype)
    between_near(far, count, matrix, load, rounded, *turned, *sends)


def between_near(chans, count, matrix, load, state, *refs):
    sends = refs[-len(chans) :]
    for channel, send in zip(chans, sends):
        rows = channel[3]
        own = own_rows(channel)
        send[0:rows] = load[own].astype(jnp.float32) - product(matrix[own], state[...])
        for turned in refs[: -len(chans)]:
            for block, columns, _ in row_blocks(channel):
                send[rows + block * count : rows + (block + 1) * count] = turned[0:count, columns]


def landing(chans, ncl, state, spread, near_values, *refs):
    count = len(chans)
    parts, gots, out = refs[:count], refs[count : 2 * count], refs[2 * count]
    values = Values(chans, ncl, near_values, (), ())
    for at, channel in enumerate(chans):
        own = own_rows(channel)
        theirs = values.at(at) if channel[0] == "sub" else jnp.zeros((ncl, state.shape[1]), jnp.float32)
        update = product(spread[own], split(jnp.concatenate([values.at(), theirs], axis=0), 0))
        update += parts[at][...] + across(channel, gots[at])
        out[own] = state[own].astype(jnp.float32) + update


def closing(chans, ncl, spread, landed, *refs):
    values, (out,) = value_refs(chans, ncl, refs)
    for at, channel in enumerate(chans):
        own = own_rows(channel)
        last = landed[own]
        if channel[0] == "grp":
            theirs = values.at(at)
            pair = jnp.concatenate([jnp.zeros_like(theirs), theirs], axis=0)
            last += product(spread[own], split(pair, 0))
        out[own] = last.astype(out.dtype)


def steps(sub):
    found, step = [], sub // 2
    while step:
        found.append(step)
        step //= 2
    return found


def origins(sub):
    found = [0]
    for step in steps(sub):
        found += [origin ^ step for origin in found]
    return found


def gathered(piece, sub, hold=(), wide=False, early=()):
    def hop(move):
        return lax.ppermute(piece, "sub", [(i, i ^ move) for i in range(sub)])

    moves = steps(sub)
    if wide:
        first, second, *moves = moves
        pieces = [piece] + [hop(move) for move in (first, second, first ^ second)]
        piece = jnp.concatenate(pieces, axis=0)
    for at, move in enumerate(moves[:-1]):
        got = hop(move)
        after = hold if at + 1 == len(moves) // 2 else early if at == 0 else ()
        if after:
            joined = jax.ShapeDtypeStruct((2 * piece.shape[0], piece.shape[1]), piece.dtype)
            piece = call(joining, joined, (piece, got), after=after, flops=0 if after is hold else WEIGHT // 2)
        else:
            piece = jnp.concatenate([piece, got], axis=0)
    return piece, hop(moves[-1])


def shards(
    schur_t, neumann_t, face_weights, coarse_basis, coarse_inverse, coarse_number, loads, iterate
):
    schur, neumann = schur_t[0, 0], neumann_t[0, 0]
    basis_across = coarse_basis[0, 0].T
    load, state = loads[0, 0], iterate[0, 0]
    iface, columns = state.shape
    ncl = basis_across.shape[0]
    face = iface // 4
    grp, sub = lax.axis_size("grp"), lax.axis_size("sub")
    chans = channels(grp, sub, face)
    far = tuple(c for c in chans if c[0] == "grp")
    near = chans[len(far) :]
    around = (len(chans) + 1) * ncl
    order = coarse_inverse.shape[2]

    def wide(rows, width=columns):
        return jax.ShapeDtypeStruct((rows, width), jnp.float32)

    def short(rows, width=columns):
        return jax.ShapeDtypeStruct((rows, width), jnp.bfloat16)

    far_plain, near_plain = [tuple(wide(c[3]) for c in group) for group in (far, near)]
    half = short(iface)
    flops = iface * iface * columns

    opened = (
        *far_plain,
        *(wide(c[3] + c[3] // LANES * ncl) for c in near),
        *(wide(c[3] // LANES * ncl) for c in far),
    )
    parts = call(
        functools.partial(opening, chans),
        opened,
        (schur, load, state, basis_across),
        scratch=(
            pltpu.VMEM(schur.shape, schur.dtype),
            pltpu.VMEM(load.shape, load.dtype),
            pltpu.VMEM(state.shape, state.dtype),
            pltpu.VMEM(basis_across.shape, basis_across.dtype),
            pltpu.SemaphoreType.DMA((3 + PIECES + len(opened),)),
            *(pltpu.VMEM(out.shape, out.dtype) for out in opened),
        ),
        flops=2 * flops,
        away=4,
        grant=56 * MIB,
        out=AWAY,
    )
    parts, far_basis = parts[: len(chans)], parts[len(chans) :]
    gots = exchange(chans, parts)
    basis_gots = (*exchange(far, far_basis), *gots[len(far) :])
    parts = call(stash, far_plain + near_plain, tuple(parts))

    weights = jnp.broadcast_to(face_weights[0, 0][:, None], (iface, columns))
    rows_of = coarse_inverse.shape[1]
    tiles = (order + -order % LANES) // LANES
    inverse_rows = (rows_of + -rows_of % 8) * tiles
    mapping = None

    def coarse_step(coarse, mapping, hold=(), after=(), early=(), sent=1 + len(near)):
        rows = len(near_order(chans)) * ncl
        kept, got = gathered(coarse, sub, hold, False, early)
        if mapping is None:
            mapping, own = call(
                functools.partial(coarse_first, chans, order, sub, ncl),
                (short(rows, 3 * sub * ncl), wide(rows)),
                (coarse_number, kept, got),
                scratch=(
                    pltpu.VMEM((inverse_rows // tiles * sub, tiles * LANES), jnp.float32),
                    pltpu.VMEM((sub * ncl, 8), jnp.float32),
                    pltpu.VMEM((sub * ncl, 8), jnp.float32),
                    pltpu.VMEM((sub * ncl, columns), jnp.float32),
                ),
                after=after,
            )
        else:
            own = call(coarse_values, wide(rows), (mapping, kept, got), after=after)
        known = own[0 : sent * ncl]
        theirs = [swap(known, channel) for channel in far]
        beyond = []
        if len(far) > 1:
            beyond = [swap(theirs[1 - at][0:ncl], channel) for at, channel in enumerate(far)]
        return mapping, (own, *theirs, *beyond)

    def sums(sent, got):
        return call(functools.partial(summing, chans), wide(iface), (*sent, *got), flops=WEIGHT)

    for step in range(ITERS):
        start, last = step == 0, step + 1 == ITERS
        if start:
            weighted, *far_scaled = call(
                functools.partial(smoothing_first, chans, far),
                (half,) + far_plain,
                (neumann, weights, *parts, *gots),
                flops=flops,
            )
        else:
            early = (response,) if step == 1 else near_scaled[:1]
            mapping, values = coarse_step(coarse, mapping, hold=far_parts[:1], early=early)
            if step == 1:
                reach = [
                    call(
                        functools.partial(reaching, channel, around),
                        short(channel[3], 4 * around),
                        (response, got),
                        after=values[:1],
                    )
                    for channel, got in zip(chans, gots)
                ]
            known = (weights, ahead, spread, sums(parts, gots), *reach, *values)
            if last:
                state, weighted, coarse = call(
                    functools.partial(smoothing_last, chans, ncl),
                    (half, half, wide(ncl)),
                    (basis_across, *known),
                )
                far_scaled = call(
                    functools.partial(smoothing_rows, far),
                    far_plain,
                    (neumann, weights, weighted),
                    flops=flops,
                )
                near_scaled = call(
                    functools.partial(smoothing_rows, near),
                    near_plain,
                    (neumann, weights, weighted),
                    flops=flops,
                    after=far_scaled[:1],
                )
            else:
                state, weighted, *far_scaled = call(
                    functools.partial(smoothing_far, chans, far, ncl),
                    (half, half) + far_plain,
                    (neumann, *known),
                    flops=flops,
                )
        if not last:
            inverse = (coarse_inverse[0],) if start else ()
            coarse, *near_scaled = call(
                functools.partial(smoothing_sub, near),
                (wide(ncl + len(inverse) * inverse_rows),) + near_plain,
                (neumann, weights, weighted, basis_across, *inverse),
                flops=flops,
            )
        scaled = (*far_scaled, *near_scaled)
        scaled_gots = exchange(chans, scaled)
        behind, behind_rows = (), 0
        if start:
            width = around + -around % LANES
            spread, full = call(
                functools.partial(spreading, chans),
                (short(iface, 6 * ncl), short(iface, 2 * width)),
                (weights, basis_across, *basis_gots),
                after=near_scaled[:1],
            )
            response, turned = call(
                responding, (wide(iface, width), wide(width, iface)), (schur, full), flops=2 * flops
            )
            behind, behind_rows = (turned,), around
        if not last:
            far_outs, near_outs = [
                tuple(wide(c[3] + c[3] // LANES * behind_rows) for c in group) for group in (far, near)
            ]
            ahead, rounded, *far_parts = call(
                functools.partial(between_far, chans, far, around),
                (wide(iface), half) + far_outs,
                (schur, load, state, *scaled, *scaled_gots, *behind),
                flops=flops,
            )
            near_parts = call(
                functools.partial(between_near, near, around),
                near_outs,
                (schur, load, rounded, *behind),
                flops=flops,
                after=far_parts[:1],
            )
            parts = (*far_parts, *near_parts)
            gots = exchange(chans, parts)
    mapping, values = coarse_step(coarse, mapping, after=scaled_gots[len(far) :], sent=1)
    landed = call(
        functools.partial(landing, chans, ncl),
        wide(iface),
        (state, spread, values[0], *scaled, *scaled_gots),
        flops=WEIGHT,
    )
    out = call(functools.partial(closing, chans, ncl), half, (spread, landed, *values))
    return out[None, None]


def solution(mesh):
    return jax.shard_map(
        shards,
        mesh=mesh,
        in_specs=(
            P("grp", "sub", None, None),
            P("grp", "sub", None, None),
            P("grp", "sub", None),
            P("grp", "sub", None, None),
            P("grp", "sub", None),
            P("grp", None),
            P("grp", "sub", None, None),
            P("grp", "sub", None, None),
        ),
        out_specs=P("grp", "sub", None, None),
        check_vma=False,
    )
```

```python
import functools

import jax
import jax.numpy as jnp
from jax import lax
from jax.experimental import pallas as pl
from jax.experimental.pallas import tpu as pltpu
from jax.sharding import PartitionSpec as P

ITERS = 3
HIGHEST = lax.Precision.HIGHEST
EVEN, ODD, BOTH = range(3)
LANES = 128
PIECES = 8
WEIGHT = 4 * 10**9
MIB = 2**20
WHOLE = pl.BlockSpec(memory_space=pltpu.VMEM)
AWAY = pl.BlockSpec(memory_space=pltpu.HBM)
ANYWHERE = pl.BlockSpec(memory_space=pl.ANY)


def channels(grp, sub, face):
    found = []
    for axis, devices, base in (("grp", grp, 2 * face), ("sub", sub, 0)):
        if devices == 2:
            found.append((axis, BOTH, base, 2 * face))
        else:
            found += [(axis, ODD, base, face), (axis, EVEN, base, face)]
    return tuple(found)


def mate(kind, index, devices):
    if kind == BOTH:
        return 1 - index
    step = 1 - 2 * (index % 2)
    if kind == ODD:
        step = -step
    return (index + step + devices) % devices


def swap(array, channel):
    axis, kind = channel[:2]
    devices = lax.axis_size(axis)
    return lax.ppermute(array, axis, [(i, mate(kind, i, devices)) for i in range(devices)])


def exchange(chans, sends):
    return tuple(swap(send, channel) for channel, send in zip(chans, sends))


def first_row(channel):
    axis, kind, base, rows = channel
    if kind == BOTH:
        return base
    odd = lax.rem(lax.axis_index(axis), 2)
    return pl.multiple_of(base + (odd if kind == ODD else 1 - odd) * rows, rows)


def own_rows(channel):
    return pl.ds(first_row(channel), channel[3])


def row_blocks(channel):
    blocks = channel[3] // LANES
    for block in range(blocks):
        rows = pl.ds(pl.multiple_of(first_row(channel) + block * LANES, LANES), LANES)
        yield block, rows, (block + blocks // 2) % blocks if channel[1] == BOTH else block


def across(channel, got):
    rows = channel[3]
    if channel[1] == BOTH:
        return jnp.concatenate([got[rows // 2 : rows], got[0 : rows // 2]], axis=0)
    return got[0:rows]


def product(a, b):
    return jnp.dot(a, b, preferred_element_type=jnp.float32)


def split(values, axis):
    high = values.astype(jnp.bfloat16)
    low = (values - high.astype(jnp.float32)).astype(jnp.bfloat16)
    return jnp.concatenate([high, low, high], axis=axis)


def thrice(values):
    high = values.astype(jnp.bfloat16).astype(jnp.float32)
    return jnp.concatenate([high, high, values - high], axis=1).astype(jnp.bfloat16)


def call(body, outs, args, scratch=(), flops=0, away=0, after=(), grant=16 * MIB, out=WHOLE):
    moved = sum(a.size * a.dtype.itemsize for a in args)
    ahead = len(after)
    return pl.pallas_call(
        lambda *refs: body(*refs[ahead:]),
        out_shape=outs,
        in_specs=[ANYWHERE] * ahead + [AWAY] * away + [WHOLE] * (len(args) - away),
        out_specs=jax.tree.map(lambda _: out, outs),
        scratch_shapes=scratch,
        cost_estimate=pl.CostEstimate(flops=flops, bytes_accessed=moved, transcendentals=0),
        compiler_params=pltpu.CompilerParams(vmem_limit_bytes=grant),
    )(*after, *args)


class Values:
    def __init__(self, chans, ncl, near, far, second):
        self.chans, self.ncl = chans, ncl
        self.near, self.far, self.second = near, far, second
        self.order = near_order(chans)

    def at(self, *path):
        grp = [c for c in path if self.chans[c][0] == "grp"]
        sub = [c for c in path if self.chans[c][0] == "sub"]
        grp, sub = [[] if len(p) == 2 and p[0] == p[1] else p for p in (grp, sub)]
        if len(grp) == 2:
            return self.second[grp[0]][...]
        source = self.far[grp[0]] if grp else self.near
        place = self.order.index(tuple(sub)) * self.ncl
        return source[place : place + self.ncl]

    def around(self, *path):
        return [self.at(*path)] + [self.at(*path, c) for c in range(len(self.chans))]


def near_order(chans):
    kinds = [c for c, channel in enumerate(chans) if channel[0] == "sub"]
    return [()] + [(c,) for c in kinds] + [(c, d) for c in kinds for d in kinds if c != d]


def value_refs(chans, ncl, refs):
    far = sum(channel[0] == "grp" for channel in chans)
    second = far if far > 1 else 0
    values = Values(chans, ncl, refs[0], refs[1 : 1 + far], refs[1 + far : 1 + far + second])
    return values, refs[1 + far + second :]


def opening(chans, matrix, load, state, basis_across, *refs):
    count = len(refs) // 2 - 2
    outs, (rows, mine, now, basis, sems), sends = refs[:count], refs[count : count + 5], refs[count + 5 :]
    piece = matrix.shape[0] // PIECES
    order = [(at + PIECES // 2) % PIECES * piece for at in range(PIECES)]
    pairs = [(state, now), (load, mine), (basis_across, basis)]
    pairs += [(matrix.at[pl.ds(at, piece)], rows.at[pl.ds(at, piece)]) for at in order]
    copies = [pltpu.make_async_copy(a, b, sems.at[i]) for i, (a, b) in enumerate(pairs)]
    for copy in copies:
        copy.start()
    first = 3 + PIECES // 2
    for copy in copies[:first]:
        copy.wait()
    waiting = copies[first:]
    written = []

    def write(send):
        at = len(written)
        written.append(pltpu.make_async_copy(send, outs[at], sems.at[len(pairs) + at]))
        written[-1].start()

    for channel, send in zip(chans, sends):
        if channel[0] == "sub":
            while waiting:
                waiting.pop(0).wait()
        own = own_rows(channel)
        send[0 : channel[3]] = mine[own].astype(jnp.float32) - product(rows[own], now[...])
        if channel[0] == "sub":
            basis_on(channel, basis, send, channel[3])
        write(send)
    for channel, send in zip(chans, sends[len(chans) :]):
        basis_on(channel, basis, send, 0)
        write(send)
    for copy in written:
        copy.wait()


def basis_on(channel, basis, send, start):
    ncl = basis.shape[0]
    for block, columns, _ in row_blocks(channel):
        at = start + block * ncl
        send[at : at + ncl] = basis[:, columns].astype(jnp.float32)


def smooth(chans, weights, resid_on, weighted):
    for at, channel in enumerate(chans):
        own = own_rows(channel)
        weighted[own] = (weights[own] * resid_on(at, own)).astype(jnp.bfloat16)


def smoothing_near(chans, matrix, weights, weighted, sends):
    for channel, send in zip(chans, sends):
        own = own_rows(channel)
        send[...] = weights[own] * product(matrix[own], weighted[...])


def stash(*refs):
    count = len(refs) // 2
    for part, out in zip(refs[:count], refs[count:]):
        out[...] = part[0 : out.shape[0]]


def summing(chans, *refs):
    count = len(chans)
    parts, gots, out = refs[:count], refs[count : 2 * count], refs[2 * count]
    for channel, part, got in zip(chans, parts, gots):
        out[own_rows(channel)] = part[0 : channel[3]] + across(channel, got)


def smoothing_first(chans, far, matrix, weights, *refs):
    count = len(chans)
    parts, gots = refs[:count], refs[count : 2 * count]

    def resid_on(at, own):
        return parts[at][...] + across(chans[at], gots[at])

    smooth(chans, weights, resid_on, refs[2 * count])
    smoothing_near(far, matrix, weights, refs[2 * count], refs[2 * count + 1 :])


def correct(chans, ncl, weights, ahead, spread, summed, refs):
    reach = refs[: len(chans)]
    values, refs = value_refs(chans, ncl, refs[len(chans) :])
    state, weighted, rest = refs[0], refs[1], refs[2:]
    here = values.around()

    def resid_on(at, own):
        pair = jnp.concatenate([here[0], values.at(at)], axis=0)
        state[own] = (ahead[own] + product(spread[own], split(pair, 0))).astype(state.dtype)
        both = jnp.concatenate(here + values.around(at), axis=0)
        return summed[own] - product(reach[at][...], split(both, 0)[0 : 2 * both.shape[0]])

    smooth(chans, weights, resid_on, weighted)
    return weighted, rest


def smoothing_far(chans, far, ncl, matrix, weights, ahead, spread, summed, *refs):
    weighted, sends = correct(chans, ncl, weights, ahead, spread, summed, refs)
    smoothing_near(far, matrix, weights, weighted, sends)


def smoothing_last(chans, ncl, basis_across, weights, ahead, spread, summed, *refs):
    weighted, (coarse,) = correct(chans, ncl, weights, ahead, spread, summed, refs)
    coarse[...] = product(basis_across[...], weighted[...])


def smoothing_rows(chans, matrix, weights, weighted, *sends):
    smoothing_near(chans, matrix, weights, weighted, sends)


def smoothing_sub(near, matrix, weights, weighted, basis_across, *refs):
    inverse = refs[: -len(near) - 1]
    coarse, sends = refs[-len(near) - 1], refs[-len(near) :]
    ncl = basis_across.shape[0]
    coarse[0:ncl] = product(basis_across[...], weighted[...])
    for rows in inverse:
        padded = rows.shape[0] + -rows.shape[0] % 8
        coarse[ncl:] = jnp.zeros((coarse.shape[0] - ncl, coarse.shape[1]), jnp.float32)
        for at in range(0, rows.shape[1], LANES):
            start = ncl + at // LANES * padded
            columns = min(LANES, rows.shape[1] - at)
            coarse[start : start + rows.shape[0], 0:columns] = rows[:, at : at + columns]
    smoothing_near(near, matrix, weights, weighted, sends)


def spreading(chans, weights, basis_across, *refs):
    gots, thin, full = refs[:-2], refs[-2], refs[-1]
    ncl = basis_across.shape[0]
    width = full.shape[1] // 2
    for at, (channel, got) in enumerate(zip(chans, gots)):
        for _, own, block in row_blocks(channel):
            from_row = block * ncl + (channel[3] if channel[0] == "sub" else 0)
            weight = weights[own][:, 0:ncl]
            here = weight * basis_across[:, own].astype(jnp.float32).T
            there = (1.0 - weight) * got[from_row : from_row + ncl].T
            thin[own] = thrice(jnp.concatenate([here, there], axis=1))
            before = [jnp.zeros((LANES, at * ncl), jnp.float32)] if at else []
            behind = jnp.zeros((LANES, width - (at + 2) * ncl), jnp.float32)
            placed = jnp.concatenate([here, *before, there, behind], axis=1)
            high = placed.astype(jnp.bfloat16)
            full[own, 0:width] = high
            full[own, width:] = (placed - high.astype(jnp.float32)).astype(jnp.bfloat16)


def responding(matrix, full, out, turned):
    width = out.shape[1]
    both = product(matrix[...], full[...])
    out[...] = both[:, 0:width] + both[:, width:]
    for at in range(0, out.shape[0], LANES):
        turned[:, at : at + LANES] = out[at : at + LANES].T


def reaching(channel, count, response, got, out):
    for block, own, from_block in row_blocks(channel):
        at = channel[3] + from_block * count
        theirs = got[at : at + count].T
        both = jnp.concatenate([response[own][:, 0:count], theirs], axis=1)
        out[block * LANES : (block + 1) * LANES] = jnp.concatenate([both, both], axis=1).astype(jnp.bfloat16)


def joining(first, second, out):
    out[...] = jnp.concatenate([first[...], second[...]], axis=0)


def coarse_first(chans, order, sub, ncl, numbers, kept, got, out, values, *scratch):
    arranged, upright, relative, pieces = scratch
    index = lax.axis_index("sub")
    rows_of = order // sub
    padded = rows_of + -rows_of % 8
    stride = kept.shape[0] * 2 // sub
    upright[...] = jnp.broadcast_to(numbers[...].astype(jnp.float32), (8, numbers.shape[1])).T
    for block, origin in enumerate(origins(sub)):
        origin = jnp.bitwise_xor(index, origin)
        half = sub // 2
        source = kept if block < half else got
        at = (block % half) * stride
        pieces[block * ncl : (block + 1) * ncl] = source[at : at + ncl]
        to = pl.ds(pl.multiple_of(origin * padded, 8), padded)
        for tile in range(arranged.shape[1] // LANES):
            start = at + ncl + tile * padded
            arranged[to, tile * LANES : (tile + 1) * LANES] = source[start : start + padded]
        relative[block * ncl : (block + 1) * ncl] = upright[pl.ds(pl.multiple_of(origin * ncl, 8), ncl)]
    wanted = []
    for path in near_order(chans):
        place = index
        for c in path:
            place = mate(chans[c][1], place, sub)
        wanted.append(upright[pl.ds(pl.multiple_of(place * ncl, 8), ncl)])
    wanted = jnp.concatenate(wanted, axis=0)[:, 0:1].astype(jnp.int32)
    lane = lax.broadcasted_iota(jnp.int32, (wanted.shape[0], sub * padded), 1)
    inside = lane % padded
    held = jnp.where(inside < rows_of, (lane // padded) * rows_of + inside, -1)
    pick = jnp.where(wanted == held, 1.0, 0.0).astype(jnp.float32)
    chosen = jnp.dot(pick, arranged[...], precision=HIGHEST, preferred_element_type=jnp.float32)
    column = lax.broadcasted_iota(jnp.int32, (relative.shape[0], arranged.shape[1]), 1)
    place = jnp.where(relative[...][:, 0:1].astype(jnp.int32) == column, 1.0, 0.0).astype(jnp.float32)
    whole = lax.dot_general(
        chosen, place, (((1,), (1,)), ((), ())), precision=HIGHEST, preferred_element_type=jnp.float32
    )
    values[...] = jnp.dot(whole, pieces[...], precision=HIGHEST, preferred_element_type=jnp.float32)
    half = whole.shape[1] // 2
    out[:, 0 : 3 * half] = thrice(whole[:, 0:half])
    out[:, 3 * half :] = thrice(whole[:, half:])


def coarse_values(mapping, kept, got, out):
    half = mapping.shape[1] // 2
    out[...] = product(mapping[:, 0:half], split(kept[...], 0)) + product(mapping[:, half:], split(got[...], 0))


def between_far(chans, far, count, matrix, load, state, *refs):
    size = len(chans)
    parts, gots = refs[:size], refs[size : 2 * size]
    turned = refs[2 * size : -len(far) - 2]
    ahead, rounded, sends = refs[-len(far) - 2], refs[-len(far) - 1], refs[-len(far) :]
    for channel, part, got in zip(chans, parts, gots):
        own = own_rows(channel)
        ahead[own] = state[own].astype(jnp.float32) + part[...] + across(channel, got)
        rounded[own] = ahead[own].astype(rounded.dtype)
    between_near(far, count, matrix, load, rounded, *turned, *sends)


def between_near(chans, count, matrix, load, state, *refs):
    sends = refs[-len(chans) :]
    for channel, send in zip(chans, sends):
        rows = channel[3]
        own = own_rows(channel)
        send[0:rows] = load[own].astype(jnp.float32) - product(matrix[own], state[...])
        for turned in refs[: -len(chans)]:
            for block, columns, _ in row_blocks(channel):
                send[rows + block * count : rows + (block + 1) * count] = turned[0:count, columns]


def landing(chans, ncl, state, spread, near_values, *refs):
    count = len(chans)
    parts, gots, out = refs[:count], refs[count : 2 * count], refs[2 * count]
    values = Values(chans, ncl, near_values, (), ())
    for at, channel in enumerate(chans):
        own = own_rows(channel)
        theirs = values.at(at) if channel[0] == "sub" else jnp.zeros((ncl, state.shape[1]), jnp.float32)
        update = product(spread[own], split(jnp.concatenate([values.at(), theirs], axis=0), 0))
        update += parts[at][...] + across(channel, gots[at])
        out[own] = state[own].astype(jnp.float32) + update


def closing(chans, ncl, spread, landed, *refs):
    values, (out, rounded, sems) = value_refs(chans, ncl, refs)
    half = rounded.shape[0] // 2
    copies = [
        pltpu.make_async_copy(rounded.at[pl.ds(at, half)], out.at[pl.ds(at, half)], sems.at[i])
        for i, at in enumerate((0, half))
    ]
    rounded[0:half] = landed[0:half].astype(rounded.dtype)
    copies[0].start()
    for at, channel in enumerate(chans):
        if channel[0] == "grp":
            own = own_rows(channel)
            theirs = values.at(at)
            pair = jnp.concatenate([jnp.zeros_like(theirs), theirs], axis=0)
            rounded[own] = (landed[own] + product(spread[own], split(pair, 0))).astype(rounded.dtype)
    copies[1].start()
    for copy in copies:
        copy.wait()


def steps(sub):
    found, step = [], sub // 2
    while step:
        found.append(step)
        step //= 2
    return found


def origins(sub):
    found = [0]
    for step in steps(sub):
        found += [origin ^ step for origin in found]
    return found


def gathered(piece, sub, hold=(), wide=False, early=()):
    def hop(move):
        return lax.ppermute(piece, "sub", [(i, i ^ move) for i in range(sub)])

    moves = steps(sub)
    if wide:
        first, second, *moves = moves
        pieces = [piece] + [hop(move) for move in (first, second, first ^ second)]
        piece = jnp.concatenate(pieces, axis=0)
    for at, move in enumerate(moves[:-1]):
        got = hop(move)
        after = hold if at + 1 == len(moves) // 2 else early if at == 0 else ()
        if after:
            joined = jax.ShapeDtypeStruct((2 * piece.shape[0], piece.shape[1]), piece.dtype)
            piece = call(joining, joined, (piece, got), after=after, flops=0 if after is hold else WEIGHT // 2)
        else:
            piece = jnp.concatenate([piece, got], axis=0)
    return piece, hop(moves[-1])


def shards(
    schur_t, neumann_t, face_weights, coarse_basis, coarse_inverse, coarse_number, loads, iterate
):
    schur, neumann = schur_t[0, 0], neumann_t[0, 0]
    basis_across = coarse_basis[0, 0].T
    load, state = loads[0, 0], iterate[0, 0]
    iface, columns = state.shape
    ncl = basis_across.shape[0]
    face = iface // 4
    grp, sub = lax.axis_size("grp"), lax.axis_size("sub")
    chans = channels(grp, sub, face)
    far = tuple(c for c in chans if c[0] == "grp")
    near = chans[len(far) :]
    around = (len(chans) + 1) * ncl
    order = coarse_inverse.shape[2]

    def wide(rows, width=columns):
        return jax.ShapeDtypeStruct((rows, width), jnp.float32)

    def short(rows, width=columns):
        return jax.ShapeDtypeStruct((rows, width), jnp.bfloat16)

    far_plain, near_plain = [tuple(wide(c[3]) for c in group) for group in (far, near)]
    half = short(iface)
    flops = iface * iface * columns

    opened = (
        *far_plain,
        *(wide(c[3] + c[3] // LANES * ncl) for c in near),
        *(wide(c[3] // LANES * ncl) for c in far),
    )
    parts = call(
        functools.partial(opening, chans),
        opened,
        (schur, load, state, basis_across),
        scratch=(
            pltpu.VMEM(schur.shape, schur.dtype),
            pltpu.VMEM(load.shape, load.dtype),
            pltpu.VMEM(state.shape, state.dtype),
            pltpu.VMEM(basis_across.shape, basis_across.dtype),
            pltpu.SemaphoreType.DMA((3 + PIECES + len(opened),)),
            *(pltpu.VMEM(out.shape, out.dtype) for out in opened),
        ),
        flops=2 * flops,
        away=4,
        grant=56 * MIB,
        out=AWAY,
    )
    parts, far_basis = parts[: len(chans)], parts[len(chans) :]
    gots = exchange(chans, parts)
    basis_gots = (*exchange(far, far_basis), *gots[len(far) :])
    parts = call(stash, far_plain + near_plain, tuple(parts))

    weights = jnp.broadcast_to(face_weights[0, 0][:, None], (iface, columns))
    rows_of = coarse_inverse.shape[1]
    tiles = (order + -order % LANES) // LANES
    inverse_rows = (rows_of + -rows_of % 8) * tiles
    mapping = None

    def coarse_step(coarse, mapping, hold=(), after=(), early=(), sent=1 + len(near)):
        rows = len(near_order(chans)) * ncl
        kept, got = gathered(coarse, sub, hold, False, early)
        if mapping is None:
            mapping, own = call(
                functools.partial(coarse_first, chans, order, sub, ncl),
                (short(rows, 3 * sub * ncl), wide(rows)),
                (coarse_number, kept, got),
                scratch=(
                    pltpu.VMEM((inverse_rows // tiles * sub, tiles * LANES), jnp.float32),
                    pltpu.VMEM((sub * ncl, 8), jnp.float32),
                    pltpu.VMEM((sub * ncl, 8), jnp.float32),
                    pltpu.VMEM((sub * ncl, columns), jnp.float32),
                ),
                after=after,
            )
        else:
            own = call(coarse_values, wide(rows), (mapping, kept, got), after=after)
        known = own[0 : sent * ncl]
        theirs = [swap(known, channel) for channel in far]
        beyond = []
        if len(far) > 1:
            beyond = [swap(theirs[1 - at][0:ncl], channel) for at, channel in enumerate(far)]
        return mapping, (own, *theirs, *beyond)

    def sums(sent, got):
        return call(functools.partial(summing, chans), wide(iface), (*sent, *got), flops=WEIGHT)

    for step in range(ITERS):
        start, last = step == 0, step + 1 == ITERS
        if start:
            weighted, *far_scaled = call(
                functools.partial(smoothing_first, chans, far),
                (half,) + far_plain,
                (neumann, weights, *parts, *gots),
                flops=flops,
            )
        else:
            early = (response,) if step == 1 else near_scaled[:1]
            mapping, values = coarse_step(coarse, mapping, hold=far_parts[:1], early=early)
            if step == 1:
                reach = [
                    call(
                        functools.partial(reaching, channel, around),
                        short(channel[3], 4 * around),
                        (response, got),
                        after=values[:1],
                    )
                    for channel, got in zip(chans, gots)
                ]
            known = (weights, ahead, spread, sums(parts, gots), *reach, *values)
            if last:
                state, weighted, coarse = call(
                    functools.partial(smoothing_last, chans, ncl),
                    (half, half, wide(ncl)),
                    (basis_across, *known),
                )
                far_scaled = call(
                    functools.partial(smoothing_rows, far),
                    far_plain,
                    (neumann, weights, weighted),
                    flops=flops,
                )
                near_scaled = call(
                    functools.partial(smoothing_rows, near),
                    near_plain,
                    (neumann, weights, weighted),
                    flops=flops,
                    after=far_scaled[:1],
                )
            else:
                state, weighted, *far_scaled = call(
                    functools.partial(smoothing_far, chans, far, ncl),
                    (half, half) + far_plain,
                    (neumann, *known),
                    flops=flops,
                )
        if not last:
            inverse = (coarse_inverse[0],) if start else ()
            coarse, *near_scaled = call(
                functools.partial(smoothing_sub, near),
                (wide(ncl + len(inverse) * inverse_rows),) + near_plain,
                (neumann, weights, weighted, basis_across, *inverse),
                flops=flops,
            )
        scaled = (*far_scaled, *near_scaled)
        scaled_gots = exchange(chans, scaled)
        behind, behind_rows = (), 0
        if start:
            width = around + -around % LANES
            spread, full = call(
                functools.partial(spreading, chans),
                (short(iface, 6 * ncl), short(iface, 2 * width)),
                (weights, basis_across, *basis_gots),
                after=near_scaled[:1],
            )
            response, turned = call(
                responding, (wide(iface, width), wide(width, iface)), (schur, full), flops=2 * flops
            )
            behind, behind_rows = (turned,), around
        if not last:
            far_outs, near_outs = [
                tuple(wide(c[3] + c[3] // LANES * behind_rows) for c in group) for group in (far, near)
            ]
            ahead, rounded, *far_parts = call(
                functools.partial(between_far, chans, far, around),
                (wide(iface), half) + far_outs,
                (schur, load, state, *scaled, *scaled_gots, *behind),
                flops=flops,
            )
            near_parts = call(
                functools.partial(between_near, near, around),
                near_outs,
                (schur, load, rounded, *behind),
                flops=flops,
                after=far_parts[:1],
            )
            parts = (*far_parts, *near_parts)
            gots = exchange(chans, parts)
    mapping, values = coarse_step(coarse, mapping, after=scaled_gots[len(far) :], sent=1)
    landed = call(
        functools.partial(landing, chans, ncl),
        wide(iface),
        (state, spread, values[0], *scaled, *scaled_gots),
        flops=WEIGHT,
    )
    out = call(
        functools.partial(closing, chans, ncl),
        half,
        (spread, landed, *values),
        scratch=(pltpu.VMEM(half.shape, half.dtype), pltpu.SemaphoreType.DMA((2,))),
        out=AWAY,
    )
    return out[None, None]


def solution(mesh):
    return jax.shard_map(
        shards,
        mesh=mesh,
        in_specs=(
            P("grp", "sub", None, None),
            P("grp", "sub", None, None),
            P("grp", "sub", None),
            P("grp", "sub", None, None),
            P("grp", "sub", None),
            P("grp", None),
            P("grp", "sub", None, None),
            P("grp", "sub", None, None),
        ),
        out_specs=P("grp", "sub", None, None),
        check_vma=False,
    )
```

```python
import functools

import jax
import jax.numpy as jnp
from jax import lax
from jax.experimental import pallas as pl
from jax.experimental.pallas import tpu as pltpu
from jax.sharding import PartitionSpec as P

ITERS = 3
HIGHEST = lax.Precision.HIGHEST
EVEN, ODD, BOTH = range(3)
LANES = 128
PIECES = 8
WEIGHT = 4 * 10**9
MIB = 2**20
WHOLE = pl.BlockSpec(memory_space=pltpu.VMEM)
AWAY = pl.BlockSpec(memory_space=pltpu.HBM)
ANYWHERE = pl.BlockSpec(memory_space=pl.ANY)


def channels(grp, sub, face):
    found = []
    for axis, devices, base in (("grp", grp, 2 * face), ("sub", sub, 0)):
        if devices == 2:
            found.append((axis, BOTH, base, 2 * face))
        else:
            found += [(axis, ODD, base, face), (axis, EVEN, base, face)]
    return tuple(found)


def mate(kind, index, devices):
    if kind == BOTH:
        return 1 - index
    step = 1 - 2 * (index % 2)
    if kind == ODD:
        step = -step
    return (index + step + devices) % devices


def swap(array, channel):
    axis, kind = channel[:2]
    devices = lax.axis_size(axis)
    return lax.ppermute(array, axis, [(i, mate(kind, i, devices)) for i in range(devices)])


def exchange(chans, sends):
    return tuple(swap(send, channel) for channel, send in zip(chans, sends))


def first_row(channel):
    axis, kind, base, rows = channel
    if kind == BOTH:
        return base
    odd = lax.rem(lax.axis_index(axis), 2)
    return pl.multiple_of(base + (odd if kind == ODD else 1 - odd) * rows, rows)


def own_rows(channel):
    return pl.ds(first_row(channel), channel[3])


def row_blocks(channel):
    blocks = channel[3] // LANES
    for block in range(blocks):
        rows = pl.ds(pl.multiple_of(first_row(channel) + block * LANES, LANES), LANES)
        yield block, rows, (block + blocks // 2) % blocks if channel[1] == BOTH else block


def across(channel, got):
    rows = channel[3]
    if channel[1] == BOTH:
        return jnp.concatenate([got[rows // 2 : rows], got[0 : rows // 2]], axis=0)
    return got[0:rows]


def product(a, b):
    return jnp.dot(a, b, preferred_element_type=jnp.float32)


def split(values, axis):
    high = values.astype(jnp.bfloat16)
    low = (values - high.astype(jnp.float32)).astype(jnp.bfloat16)
    return jnp.concatenate([high, low, high], axis=axis)


def thrice(values):
    high = values.astype(jnp.bfloat16).astype(jnp.float32)
    return jnp.concatenate([high, high, values - high], axis=1).astype(jnp.bfloat16)


def call(body, outs, args, scratch=(), flops=0, away=0, after=(), grant=16 * MIB, out=WHOLE):
    moved = sum(a.size * a.dtype.itemsize for a in args)
    ahead = len(after)
    return pl.pallas_call(
        lambda *refs: body(*refs[ahead:]),
        out_shape=outs,
        in_specs=[ANYWHERE] * ahead + [AWAY] * away + [WHOLE] * (len(args) - away),
        out_specs=jax.tree.map(lambda _: out, outs),
        scratch_shapes=scratch,
        cost_estimate=pl.CostEstimate(flops=flops, bytes_accessed=moved, transcendentals=0),
        compiler_params=pltpu.CompilerParams(vmem_limit_bytes=grant),
    )(*after, *args)


class Values:
    def __init__(self, chans, ncl, near, far, second):
        self.chans, self.ncl = chans, ncl
        self.near, self.far, self.second = near, far, second
        self.order = near_order(chans)

    def at(self, *path):
        grp = [c for c in path if self.chans[c][0] == "grp"]
        sub = [c for c in path if self.chans[c][0] == "sub"]
        grp, sub = [[] if len(p) == 2 and p[0] == p[1] else p for p in (grp, sub)]
        if len(grp) == 2:
            return self.second[grp[0]][...]
        source = self.far[grp[0]] if grp else self.near
        place = self.order.index(tuple(sub)) * self.ncl
        return source[place : place + self.ncl]

    def around(self, *path):
        return [self.at(*path)] + [self.at(*path, c) for c in range(len(self.chans))]


def near_order(chans):
    kinds = [c for c, channel in enumerate(chans) if channel[0] == "sub"]
    return [()] + [(c,) for c in kinds] + [(c, d) for c in kinds for d in kinds if c != d]


def value_refs(chans, ncl, refs):
    far = sum(channel[0] == "grp" for channel in chans)
    second = far if far > 1 else 0
    values = Values(chans, ncl, refs[0], refs[1 : 1 + far], refs[1 + far : 1 + far + second])
    return values, refs[1 + far + second :]


def opening(chans, matrix, load, state, basis_across, *refs):
    count = len(refs) // 2 - 2
    outs, (rows, mine, now, basis, sems), sends = refs[:count], refs[count : count + 5], refs[count + 5 :]
    piece = matrix.shape[0] // PIECES
    order = [(at + PIECES // 2) % PIECES * piece for at in range(PIECES)]
    pairs = [(state, now), (load, mine), (basis_across, basis)]
    pairs += [(matrix.at[pl.ds(at, piece)], rows.at[pl.ds(at, piece)]) for at in order]
    copies = [pltpu.make_async_copy(a, b, sems.at[i]) for i, (a, b) in enumerate(pairs)]
    for copy in copies:
        copy.start()
    first = 3 + PIECES // 2
    for copy in copies[:first]:
        copy.wait()
    waiting = copies[first:]
    written = []

    def write(send):
        at = len(written)
        written.append(pltpu.make_async_copy(send, outs[at], sems.at[len(pairs) + at]))
        written[-1].start()

    for channel, send in zip(chans, sends):
        if channel[0] == "sub":
            while waiting:
                waiting.pop(0).wait()
        own = own_rows(channel)
        send[0 : channel[3]] = mine[own].astype(jnp.float32) - product(rows[own], now[...])
        if channel[0] == "sub":
            basis_on(channel, basis, send, channel[3])
        write(send)
    for channel, send in zip(chans, sends[len(chans) :]):
        basis_on(channel, basis, send, 0)
        write(send)
    for copy in written:
        copy.wait()


def basis_on(channel, basis, send, start):
    ncl = basis.shape[0]
    for block, columns, _ in row_blocks(channel):
        at = start + block * ncl
        send[at : at + ncl] = basis[:, columns].astype(jnp.float32)


def smooth(chans, weights, resid_on, weighted):
    for at, channel in enumerate(chans):
        own = own_rows(channel)
        weighted[own] = (weights[own] * resid_on(at, own)).astype(jnp.bfloat16)


def smoothing_near(chans, matrix, weights, weighted, sends):
    for channel, send in zip(chans, sends):
        own = own_rows(channel)
        send[...] = weights[own] * product(matrix[own], weighted[...])


def stash(*refs):
    count = len(refs) // 2
    for part, out in zip(refs[:count], refs[count:]):
        out[...] = part[0 : out.shape[0]]


def summing(chans, *refs):
    count = len(chans)
    parts, gots, out = refs[:count], refs[count : 2 * count], refs[2 * count]
    for channel, part, got in zip(chans, parts, gots):
        out[own_rows(channel)] = part[0 : channel[3]] + across(channel, got)


def smoothing_first(chans, far, matrix, weights, *refs):
    count = len(chans)
    parts, gots = refs[:count], refs[count : 2 * count]

    def resid_on(at, own):
        return parts[at][...] + across(chans[at], gots[at])

    smooth(chans, weights, resid_on, refs[2 * count])
    smoothing_near(far, matrix, weights, refs[2 * count], refs[2 * count + 1 :])


def correct(chans, ncl, weights, ahead, spread, summed, refs):
    reach = refs[: len(chans)]
    values, refs = value_refs(chans, ncl, refs[len(chans) :])
    state, weighted, rest = refs[0], refs[1], refs[2:]
    here = values.around()

    def resid_on(at, own):
        pair = jnp.concatenate([here[0], values.at(at)], axis=0)
        state[own] = (ahead[own] + product(spread[own], split(pair, 0))).astype(state.dtype)
        both = jnp.concatenate(here + values.around(at), axis=0)
        return summed[own] - product(reach[at][...], split(both, 0)[0 : 2 * both.shape[0]])

    smooth(chans, weights, resid_on, weighted)
    return weighted, rest


def smoothing_far(chans, far, ncl, matrix, weights, ahead, spread, summed, *refs):
    weighted, sends = correct(chans, ncl, weights, ahead, spread, summed, refs)
    smoothing_near(far, matrix, weights, weighted, sends)


def smoothing_last(chans, ncl, basis_across, weights, ahead, spread, summed, *refs):
    weighted, (coarse,) = correct(chans, ncl, weights, ahead, spread, summed, refs)
    coarse[...] = product(basis_across[...], weighted[...])


def smoothing_rows(chans, matrix, weights, weighted, *sends):
    smoothing_near(chans, matrix, weights, weighted, sends)


def smoothing_sub(near, matrix, weights, weighted, basis_across, *refs):
    inverse = refs[: -len(near) - 1]
    coarse, sends = refs[-len(near) - 1], refs[-len(near) :]
    ncl = basis_across.shape[0]
    coarse[0:ncl] = product(basis_across[...], weighted[...])
    for rows in inverse:
        padded = rows.shape[0] + -rows.shape[0] % 8
        coarse[ncl:] = jnp.zeros((coarse.shape[0] - ncl, coarse.shape[1]), jnp.float32)
        for at in range(0, rows.shape[1], LANES):
            start = ncl + at // LANES * padded
            columns = min(LANES, rows.shape[1] - at)
            coarse[start : start + rows.shape[0], 0:columns] = rows[:, at : at + columns]
    smoothing_near(near, matrix, weights, weighted, sends)


def spreading(chans, weights, basis_across, *refs):
    gots, thin, full = refs[:-2], refs[-2], refs[-1]
    ncl = basis_across.shape[0]
    width = full.shape[1] // 2
    for at, (channel, got) in enumerate(zip(chans, gots)):
        for _, own, block in row_blocks(channel):
            from_row = block * ncl + (channel[3] if channel[0] == "sub" else 0)
            weight = weights[own][:, 0:ncl]
            here = weight * basis_across[:, own].astype(jnp.float32).T
            there = (1.0 - weight) * got[from_row : from_row + ncl].T
            thin[own] = thrice(jnp.concatenate([here, there], axis=1))
            before = [jnp.zeros((LANES, at * ncl), jnp.float32)] if at else []
            behind = jnp.zeros((LANES, width - (at + 2) * ncl), jnp.float32)
            placed = jnp.concatenate([here, *before, there, behind], axis=1)
            high = placed.astype(jnp.bfloat16)
            full[own, 0:width] = high
            full[own, width:] = (placed - high.astype(jnp.float32)).astype(jnp.bfloat16)


def responding(matrix, full, out, turned):
    width = out.shape[1]
    both = product(matrix[...], full[...])
    out[...] = both[:, 0:width] + both[:, width:]
    for at in range(0, out.shape[0], LANES):
        turned[:, at : at + LANES] = out[at : at + LANES].T


def reaching(channel, count, response, got, out):
    for block, own, from_block in row_blocks(channel):
        at = channel[3] + from_block * count
        theirs = got[at : at + count].T
        both = jnp.concatenate([response[own][:, 0:count], theirs], axis=1)
        out[block * LANES : (block + 1) * LANES] = jnp.concatenate([both, both], axis=1).astype(jnp.bfloat16)


def joining(first, second, out):
    out[...] = jnp.concatenate([first[...], second[...]], axis=0)


def coarse_first(chans, order, sub, ncl, numbers, kept, got, out, values, *scratch):
    arranged, upright, relative, pieces = scratch
    index = lax.axis_index("sub")
    rows_of = order // sub
    padded = rows_of + -rows_of % 8
    stride = kept.shape[0] * 2 // sub
    upright[...] = jnp.broadcast_to(numbers[...].astype(jnp.float32), (8, numbers.shape[1])).T
    for block, origin in enumerate(origins(sub)):
        origin = jnp.bitwise_xor(index, origin)
        half = sub // 2
        source = kept if block < half else got
        at = (block % half) * stride
        pieces[block * ncl : (block + 1) * ncl] = source[at : at + ncl]
        to = pl.ds(pl.multiple_of(origin * padded, 8), padded)
        for tile in range(arranged.shape[1] // LANES):
            start = at + ncl + tile * padded
            arranged[to, tile * LANES : (tile + 1) * LANES] = source[start : start + padded]
        relative[block * ncl : (block + 1) * ncl] = upright[pl.ds(pl.multiple_of(origin * ncl, 8), ncl)]
    wanted = []
    for path in near_order(chans):
        place = index
        for c in path:
            place = mate(chans[c][1], place, sub)
        wanted.append(upright[pl.ds(pl.multiple_of(place * ncl, 8), ncl)])
    wanted = jnp.concatenate(wanted, axis=0)[:, 0:1].astype(jnp.int32)
    lane = lax.broadcasted_iota(jnp.int32, (wanted.shape[0], sub * padded), 1)
    inside = lane % padded
    held = jnp.where(inside < rows_of, (lane // padded) * rows_of + inside, -1)
    pick = jnp.where(wanted == held, 1.0, 0.0).astype(jnp.float32)
    chosen = jnp.dot(pick, arranged[...], precision=HIGHEST, preferred_element_type=jnp.float32)
    column = lax.broadcasted_iota(jnp.int32, (relative.shape[0], arranged.shape[1]), 1)
    place = jnp.where(relative[...][:, 0:1].astype(jnp.int32) == column, 1.0, 0.0).astype(jnp.float32)
    whole = lax.dot_general(
        chosen, place, (((1,), (1,)), ((), ())), precision=HIGHEST, preferred_element_type=jnp.float32
    )
    values[...] = jnp.dot(whole, pieces[...], precision=HIGHEST, preferred_element_type=jnp.float32)
    half = whole.shape[1] // 2
    out[:, 0 : 3 * half] = thrice(whole[:, 0:half])
    out[:, 3 * half :] = thrice(whole[:, half:])


def coarse_values(mapping, kept, got, out):
    half = mapping.shape[1] // 2
    out[...] = product(mapping[:, 0:half], split(kept[...], 0)) + product(mapping[:, half:], split(got[...], 0))


def between_far(chans, far, count, matrix, load, state, *refs):
    size = len(chans)
    parts, gots = refs[:size], refs[size : 2 * size]
    turned = refs[2 * size : -len(far) - 2]
    ahead, rounded, sends = refs[-len(far) - 2], refs[-len(far) - 1], refs[-len(far) :]
    for channel, part, got in zip(chans, parts, gots):
        own = own_rows(channel)
        ahead[own] = state[own].astype(jnp.float32) + part[...] + across(channel, got)
        rounded[own] = ahead[own].astype(rounded.dtype)
    between_near(far, count, matrix, load, rounded, *turned, *sends)


def between_near(chans, count, matrix, load, state, *refs):
    sends = refs[-len(chans) :]
    for channel, send in zip(chans, sends):
        rows = channel[3]
        own = own_rows(channel)
        send[0:rows] = load[own].astype(jnp.float32) - product(matrix[own], state[...])
        for turned in refs[: -len(chans)]:
            for block, columns, _ in row_blocks(channel):
                send[rows + block * count : rows + (block + 1) * count] = turned[0:count, columns]


def landing(chans, ncl, state, spread, near_values, *refs):
    count = len(chans)
    parts, gots, out = refs[:count], refs[count : 2 * count], refs[2 * count]
    values = Values(chans, ncl, near_values, (), ())
    for at, channel in enumerate(chans):
        own = own_rows(channel)
        theirs = values.at(at) if channel[0] == "sub" else jnp.zeros((ncl, state.shape[1]), jnp.float32)
        update = product(spread[own], split(jnp.concatenate([values.at(), theirs], axis=0), 0))
        update += parts[at][...] + across(channel, gots[at])
        out[own] = state[own].astype(jnp.float32) + update


def closing(chans, ncl, spread, landed, *refs):
    values, (out, rounded, sems) = value_refs(chans, ncl, refs)
    half = rounded.shape[0] // 2
    copies = [
        pltpu.make_async_copy(rounded.at[pl.ds(at, half)], out.at[pl.ds(at, half)], sems.at[i])
        for i, at in enumerate((0, half))
    ]
    rounded[0:half] = landed[0:half].astype(rounded.dtype)
    copies[0].start()
    for at, channel in enumerate(chans):
        if channel[0] == "grp":
            own = own_rows(channel)
            theirs = values.at(at)
            pair = jnp.concatenate([jnp.zeros_like(theirs), theirs], axis=0)
            rounded[own] = (landed[own] + product(spread[own], split(pair, 0))).astype(rounded.dtype)
    copies[1].start()
    for copy in copies:
        copy.wait()


def steps(sub):
    found, step = [], sub // 2
    while step:
        found.append(step)
        step //= 2
    return found


def origins(sub):
    found = [0]
    for step in steps(sub):
        found += [origin ^ step for origin in found]
    return found


def gathered(piece, sub, hold=(), wide=False, early=(), done=0):
    def hop(move):
        return lax.ppermute(piece, "sub", [(i, i ^ move) for i in range(sub)])

    moves = steps(sub)
    if wide:
        first, second, *moves = moves
        pieces = [piece] + [hop(move) for move in (first, second, first ^ second)]
        piece = jnp.concatenate(pieces, axis=0)
    for at, move in enumerate(moves[:-1]):
        if at < done:
            continue
        got = hop(move)
        after = hold if at + 1 == len(moves) // 2 else early if at == 0 else ()
        if after:
            joined = jax.ShapeDtypeStruct((2 * piece.shape[0], piece.shape[1]), piece.dtype)
            piece = call(joining, joined, (piece, got), after=after, flops=0 if after is hold else WEIGHT // 2)
        else:
            piece = jnp.concatenate([piece, got], axis=0)
    return piece, hop(moves[-1])


def shards(
    schur_t, neumann_t, face_weights, coarse_basis, coarse_inverse, coarse_number, loads, iterate
):
    schur, neumann = schur_t[0, 0], neumann_t[0, 0]
    basis_across = coarse_basis[0, 0].T
    load, state = loads[0, 0], iterate[0, 0]
    iface, columns = state.shape
    ncl = basis_across.shape[0]
    face = iface // 4
    grp, sub = lax.axis_size("grp"), lax.axis_size("sub")
    chans = channels(grp, sub, face)
    far = tuple(c for c in chans if c[0] == "grp")
    near = chans[len(far) :]
    around = (len(chans) + 1) * ncl
    order = coarse_inverse.shape[2]

    def wide(rows, width=columns):
        return jax.ShapeDtypeStruct((rows, width), jnp.float32)

    def short(rows, width=columns):
        return jax.ShapeDtypeStruct((rows, width), jnp.bfloat16)

    far_plain, near_plain = [tuple(wide(c[3]) for c in group) for group in (far, near)]
    half = short(iface)
    flops = iface * iface * columns

    opened = (
        *far_plain,
        *(wide(c[3] + c[3] // LANES * ncl) for c in near),
        *(wide(c[3] // LANES * ncl) for c in far),
    )
    parts = call(
        functools.partial(opening, chans),
        opened,
        (schur, load, state, basis_across),
        scratch=(
            pltpu.VMEM(schur.shape, schur.dtype),
            pltpu.VMEM(load.shape, load.dtype),
            pltpu.VMEM(state.shape, state.dtype),
            pltpu.VMEM(basis_across.shape, basis_across.dtype),
            pltpu.SemaphoreType.DMA((3 + PIECES + len(opened),)),
            *(pltpu.VMEM(out.shape, out.dtype) for out in opened),
        ),
        flops=2 * flops,
        away=4,
        grant=56 * MIB,
        out=AWAY,
    )
    parts, far_basis = parts[: len(chans)], parts[len(chans) :]
    gots = exchange(chans, parts)
    basis_gots = (*exchange(far, far_basis), *gots[len(far) :])
    parts = call(stash, far_plain + near_plain, tuple(parts))

    weights = jnp.broadcast_to(face_weights[0, 0][:, None], (iface, columns))
    rows_of = coarse_inverse.shape[1]
    tiles = (order + -order % LANES) // LANES
    inverse_rows = (rows_of + -rows_of % 8) * tiles
    mapping = None

    def coarse_step(coarse, mapping, hold=(), after=(), early=(), sent=1 + len(near), done=0):
        rows = len(near_order(chans)) * ncl
        kept, got = gathered(coarse, sub, hold, False, early, done)
        if mapping is None:
            mapping, own = call(
                functools.partial(coarse_first, chans, order, sub, ncl),
                (short(rows, 3 * sub * ncl), wide(rows)),
                (coarse_number, kept, got),
                scratch=(
                    pltpu.VMEM((inverse_rows // tiles * sub, tiles * LANES), jnp.float32),
                    pltpu.VMEM((sub * ncl, 8), jnp.float32),
                    pltpu.VMEM((sub * ncl, 8), jnp.float32),
                    pltpu.VMEM((sub * ncl, columns), jnp.float32),
                ),
                after=after,
            )
        else:
            own = call(coarse_values, wide(rows), (mapping, kept, got), after=after)
        known = own[0 : sent * ncl]
        theirs = [swap(known, channel) for channel in far]
        beyond = []
        if len(far) > 1:
            beyond = [swap(theirs[1 - at][0:ncl], channel) for at, channel in enumerate(far)]
        return mapping, (own, *theirs, *beyond)

    def sums(sent, got):
        return call(functools.partial(summing, chans), wide(iface), (*sent, *got), flops=WEIGHT)

    for step in range(ITERS):
        start, last = step == 0, step + 1 == ITERS
        if start:
            weighted, *far_scaled = call(
                functools.partial(smoothing_first, chans, far),
                (half,) + far_plain,
                (neumann, weights, *parts, *gots),
                flops=flops,
            )
        else:
            early = (response,) if step == 1 else near_scaled[:1]
            mapping, values = coarse_step(coarse, mapping, hold=far_parts[:1], early=early)
            if step == 1:
                reach = [
                    call(
                        functools.partial(reaching, channel, around),
                        short(channel[3], 4 * around),
                        (response, got),
                        after=values[:1],
                    )
                    for channel, got in zip(chans, gots)
                ]
            known = (weights, ahead, spread, sums(parts, gots), *reach, *values)
            if last:
                state, weighted, coarse = call(
                    functools.partial(smoothing_last, chans, ncl),
                    (half, half, wide(ncl)),
                    (basis_across, *known),
                )
                far_scaled = call(
                    functools.partial(smoothing_rows, far),
                    far_plain,
                    (neumann, weights, weighted),
                    flops=flops,
                )
                hop = lax.ppermute(coarse, "sub", [(i, i ^ steps(sub)[0]) for i in range(sub)])
                coarse = call(joining, wide(2 * ncl), (coarse, hop), after=far_scaled[:1])
                near_scaled = call(
                    functools.partial(smoothing_rows, near),
                    near_plain,
                    (neumann, weights, weighted),
                    flops=flops,
                    after=(coarse,),
                )
            else:
                state, weighted, *far_scaled = call(
                    functools.partial(smoothing_far, chans, far, ncl),
                    (half, half) + far_plain,
                    (neumann, *known),
                    flops=flops,
                )
        if not last:
            inverse = (coarse_inverse[0],) if start else ()
            coarse, *near_scaled = call(
                functools.partial(smoothing_sub, near),
                (wide(ncl + len(inverse) * inverse_rows),) + near_plain,
                (neumann, weights, weighted, basis_across, *inverse),
                flops=flops,
            )
        scaled = (*far_scaled, *near_scaled)
        scaled_gots = exchange(chans, scaled)
        behind, behind_rows = (), 0
        if start:
            width = around + -around % LANES
            spread, full = call(
                functools.partial(spreading, chans),
                (short(iface, 6 * ncl), short(iface, 2 * width)),
                (weights, basis_across, *basis_gots),
                after=near_scaled[:1],
            )
            response, turned = call(
                responding, (wide(iface, width), wide(width, iface)), (schur, full), flops=2 * flops
            )
            behind, behind_rows = (turned,), around
        if not last:
            far_outs, near_outs = [
                tuple(wide(c[3] + c[3] // LANES * behind_rows) for c in group) for group in (far, near)
            ]
            ahead, rounded, *far_parts = call(
                functools.partial(between_far, chans, far, around),
                (wide(iface), half) + far_outs,
                (schur, load, state, *scaled, *scaled_gots, *behind),
                flops=flops,
            )
            near_parts = call(
                functools.partial(between_near, near, around),
                near_outs,
                (schur, load, rounded, *behind),
                flops=flops,
                after=far_parts[:1],
            )
            parts = (*far_parts, *near_parts)
            gots = exchange(chans, parts)
    mapping, values = coarse_step(coarse, mapping, hold=near_scaled[:1], after=scaled_gots[: len(far)], sent=1, done=1)
    landed = call(
        functools.partial(landing, chans, ncl),
        wide(iface),
        (state, spread, values[0], *scaled, *scaled_gots),
        flops=WEIGHT,
    )
    out = call(
        functools.partial(closing, chans, ncl),
        half,
        (spread, landed, *values),
        scratch=(pltpu.VMEM(half.shape, half.dtype), pltpu.SemaphoreType.DMA((2,))),
        out=AWAY,
    )
    return out[None, None]


def solution(mesh):
    return jax.shard_map(
        shards,
        mesh=mesh,
        in_specs=(
            P("grp", "sub", None, None),
            P("grp", "sub", None, None),
            P("grp", "sub", None),
            P("grp", "sub", None, None),
            P("grp", "sub", None),
            P("grp", None),
            P("grp", "sub", None, None),
            P("grp", "sub", None, None),
        ),
        out_specs=P("grp", "sub", None, None),
        check_vma=False,
    )
```
